32 devices in a mesh: front: 4 (over x, core), row: 2 (over y), col: 4 (over z).
Axes of the slice: x: 2, y: 2, z: 4, core: 2. Of those that a mesh axis runs over, the one named last changes fastest.
Arguments:
- contrib: float32 [32768, 4096], P(('front', 'row'), 'col'), parts along dimension 0, as said below
- front_diag: float32 [32768], P(('front', 'row')), parts along dimension 0, may hold values from 1 to 4
- child_map: int32 [8, 32], P('front'), parts along dimension 0, may hold values from 0 to 63, as said below
- pivots: int32 [16], P('front'), parts along dimension 0, may hold values from 0 to 63, as said below
Outputs:
- lfactor: float32 [32768, 512], P(('front', 'row'), 'col'), parts along dimension 0
- schur_block: float32 [32768, 8192], P(('front', 'row'), 'col'), parts along dimension 0
The draws below stay inside these ranges and needn't reach their ends.
There are 4 independent parts, one for each index of `front`. The reference program is written for one: setup_inputs(seed, part) draws one part's arguments, and reference() takes and returns one part's arrays. A program takes and returns all parts, laid end to end along the dimension named above; each array names one. Nothing has to cross between parts.
Inputs may be any that keep to these rules, and one draw needn't show every extreme that they name: child_map[c, b] is b or b + 32, chosen for each child and block. `pivots`: 4 distinct front blocks. `contrib`: each child's contribution block is symmetric positive definite.
All inputs are finite; a program needn't handle non-finite values.
Results may differ from the reference program's by a relative error of at most 0.0001.
Values sent between devices are 32-bit elements; how exact they have to be, the bound alone decides.
No kernel may reach another device: no remote copies, remote signals or barrier semaphores. Data moves between devices by JAX's collectives and lax.ppermute only.
A program may use at most 192 MiB of HBM per device.

```python
import math
import jax
import jax.numpy as jnp
from jax import lax

NF = 8192
NB = 64
NPAN = 2
BLK = 128
CB = 4096
CBB = 32
NPB = 4
N_ROW = 2
N_COL = 4


def stored_rows(values, device_count):
    length = values.shape[0]
    reshaped = values.reshape((length // (device_count * BLK), device_count, BLK) + values.shape[1:])
    return jnp.swapaxes(reshaped, 0, 1).reshape(values.shape)


def child_matrix(child_key):
    subkeys = jax.random.split(child_key, 4)
    places = jax.random.permutation(subkeys[0], CB).astype(jnp.float32)
    reach = 2.0
    scales = jnp.exp(jax.random.uniform(subkeys[1], (CB,), jnp.float32, math.log(0.5), math.log(2.0)))
    dominant = 2.0 * jax.random.uniform(subkeys[3], (CB,), jnp.float32, 1.02, 1.5)
    kernel = scales[:, None] * scales[None, :] * jnp.exp(-jnp.abs(places[:, None] - places[None, :]) / reach)
    rough = jax.random.uniform(subkeys[2], (CB, CB), jnp.float32, -1.0, 1.0) * (2.0 / CB)
    rough = 0.5 * (rough + rough.T) * (1.0 - jnp.eye(CB, dtype=jnp.float32))
    return kernel + rough + jnp.diag(dominant)


def draw_contrib(key, part):
    halves = []
    for child_index in range(2):
        matrix = child_matrix(jax.random.fold_in(key, 101 + child_index))
        matrix = stored_rows(matrix, N_ROW // 2)
        matrix = stored_rows(matrix.T, N_COL).T
        halves.append(matrix)
    return jnp.concatenate(halves, axis=0)


def draw_child_map(key, part):
    upper = jax.random.randint(jax.random.fold_in(key, 7), (2, CBB), 0, 2)
    upper = upper.at[0, 0].set(0).at[0, CBB - 1].set(1)
    return (jnp.arange(CBB, dtype=jnp.int32)[None, :] + CBB * upper).astype(jnp.int32)


def draw_pivots(key, part):
    shuffled = jax.random.permutation(jax.random.fold_in(key, 13), NB)
    return shuffled[:NPB].astype(jnp.int32)


def block_levels(key, extent, pieces, smallest, largest):
    loudness, own = 1.0, jax.random.fold_in(key, 6)
    for axis_at, parts in pieces:
        draws = jnp.exp(jax.random.uniform(jax.random.fold_in(own, axis_at), (parts,), jnp.float32, smallest / len(pieces), largest / len(pieces)))
        loudness = loudness * jnp.repeat(draws, extent[axis_at] // parts).reshape([-1 if axis == axis_at else 1 for axis in range(len(extent))])
    return loudness


def setup_inputs(seed: int = 0, part: int = 0) -> dict:
    streams_of = jax.random.split(jax.random.key(seed), 5)
    part_splits = jax.random.split(jax.random.fold_in(streams_of[4], part), 5)
    contrib = draw_contrib(jax.random.fold_in(jax.random.fold_in(streams_of[4], part), 71), part)
    front_diag = jnp.clip(1.0 + 3.0 * jax.random.uniform(part_splits[1], (NF,), jnp.float32) ** block_levels(part_splits[1], (NF,), ((0, 2),), -0.2, 0.2), 1.0, 4.0)
    child_map = draw_child_map(jax.random.fold_in(jax.random.fold_in(streams_of[4], part), 71), part)
    pivots = draw_pivots(jax.random.fold_in(jax.random.fold_in(streams_of[4], part), 71), part)
    return {"contrib": contrib, "front_diag": front_diag, "child_map": child_map, "pivots": pivots}


def rows_to_logical(values, device_count):
    length = values.shape[0]
    reshaped = values.reshape((device_count, length // (device_count * BLK), BLK) + values.shape[1:])
    return jnp.swapaxes(reshaped, 0, 1).reshape(values.shape)

def rows_to_stored(values, device_count):
    length = values.shape[0]
    reshaped = values.reshape((length // (device_count * BLK), device_count, BLK) + values.shape[1:])
    return jnp.swapaxes(reshaped, 0, 1).reshape(values.shape)

def reference(contrib, front_diag, child_map, pivots):
    half_rows = N_ROW // 2
    blocks = jnp.zeros((NB, NB, BLK, BLK), jnp.float32)
    for child_index in range(2):
        child_part = contrib[child_index * CB:(child_index + 1) * CB]
        child_part = rows_to_logical(child_part, half_rows)
        child_part = rows_to_logical(child_part.T, N_COL).T
        child_tiles = child_part.reshape(CBB, BLK, CBB, BLK).transpose(0, 2, 1, 3)
        target_ids = child_map[child_index]
        blocks = blocks.at[target_ids[:, None], target_ids[None, :]].add(child_tiles)
    front_matrix = blocks.transpose(0, 2, 1, 3).reshape(NF, NF)
    front_matrix = front_matrix + jnp.diag(rows_to_logical(front_diag, N_ROW))
    offsets = jnp.arange(BLK, dtype=jnp.int32)
    factor_list = []
    for panel_index in range(NPAN):
        pivot_ids = jnp.concatenate([pivots[2 * panel_index] * BLK + offsets, pivots[2 * panel_index + 1] * BLK + offsets]).astype(jnp.int32)
        panel_cols = jnp.take(front_matrix, pivot_ids, axis=1)
        pivot_block = jnp.take(panel_cols, pivot_ids, axis=0)
        lower_factor = jnp.linalg.cholesky(pivot_block)
        factor = lax.linalg.triangular_solve(lower_factor, panel_cols, left_side=False, lower=True, transpose_a=True)
        front_matrix = front_matrix - jnp.dot(factor.astype(jnp.float32), factor.T.astype(jnp.float32), precision=lax.Precision.HIGHEST, preferred_element_type=jnp.float32)
        keep_mask = jnp.ones((NF,), jnp.float32).at[pivot_ids].set(0.0)
        front_matrix = front_matrix * keep_mask[:, None] * keep_mask[None, :]
        factor_list.append(factor)
    lfactor = rows_to_stored(jnp.concatenate(factor_list, axis=1), N_ROW)
    schur_block = rows_to_stored(rows_to_stored(front_matrix, N_ROW).T, N_COL).T
    return (lfactor, schur_block)
```

```python
import functools

import jax
import jax.numpy as jnp
import numpy as np
from jax import lax
from jax.experimental import pallas as pl
from jax.experimental.pallas import tpu as pltpu
from jax.sharding import PartitionSpec as P

NF = 8192
BLK = 128
CHUNKS = 4
ROWS_AT_ONCE = 2

highest = lax.Precision.HIGHEST


def swapped(shard, axis, bit):
    return lax.ppermute(shard, axis, [(i, i ^ 1 << bit) for i in range(lax.axis_size(axis))])


def tied(values, after):
    return lax.optimization_barrier((values, after))[0]


def spread_plan(rows, cols):
    sources = cols // rows
    where = -np.ones((sources, rows, cols), np.int32)
    for r in range(rows):
        for s in range(sources):
            where[s, r, r + s * rows] = 0
    steps = []
    while (where < 0).any():
        for buffer in range(len(steps) + 1):
            moves = []
            for r in range(rows):
                sign = 1 if r <= cols - 1 - (r + (sources - 1) * rows) else -1
                taken = set()
                for h in range(cols)[::sign]:
                    for s in range(sources):
                        if where[s, r, h] != buffer:
                            continue
                        open_to = [
                            d for d in range(cols)
                            if where[s, r, d] < 0 and d not in taken and abs(d - h) <= rows
                        ]
                        if open_to:
                            d = max(open_to, key=lambda d: sign * (d - h))
                            taken.add(d)
                            moves.append((s, r, h, d))
            if moves:
                break
        steps.append((buffer, [(r * cols + h, r * cols + d) for _, r, h, d in moves]))
        for s, r, _, d in moves:
            where[s, r, d] = len(steps)
    return steps, where


def fold_plan(where):
    sources, rows, cols = where.shape
    steps = where.max()
    order = -np.ones((steps + 1, rows, cols), np.int32)
    folded = np.zeros_like(where)
    for r in range(rows):
        for d in range(cols):
            got = sorted((where[s, r, d], s) for s in range(sources) if where[s, r, d] > 0)
            for n, (step, s) in enumerate(got):
                order[step, r, d] = n
                folded[s, r, d] = n + 1
    return order, folded


class Meta:
    def __init__(self, child_blocks, pivot_count, sources):
        self.child_blocks, self.pivot_count, self.sources = child_blocks, pivot_count, sources

    def pack(self, child_map, pivots, row_index, col_index, where):
        place = jnp.stack([row_index, col_index]).astype(jnp.int32)
        held = jnp.asarray(where)[:, row_index, col_index]
        return jnp.concatenate([child_map.reshape(-1), pivots, place, held])

    def has(self, meta, child, block, front_block):
        return meta[child * self.child_blocks + block] == front_block

    def pivot(self, meta, p):
        return meta[2 * self.child_blocks + p]

    def row(self, meta):
        return meta[2 * self.child_blocks + self.pivot_count]

    def col(self, meta):
        return meta[2 * self.child_blocks + self.pivot_count + 1]

    def held(self, meta, s):
        return meta[2 * self.child_blocks + self.pivot_count + 2 + s]

    def is_pivot(self, meta, front_block):
        hit = front_block == self.pivot(meta, 0)
        for p in range(1, self.pivot_count):
            hit = jnp.logical_or(hit, front_block == self.pivot(meta, p))
        return hit


def as_float(flag):
    return jnp.where(flag, 1.0, 0.0).astype(jnp.float32)


def eye_mask():
    return lax.broadcasted_iota(jnp.int32, (BLK, BLK), 0) == lax.broadcasted_iota(jnp.int32, (BLK, BLK), 1)


def split(value):
    high = value.astype(jnp.bfloat16)
    return high, (value - high.astype(jnp.float32)).astype(jnp.bfloat16)


def dot_t(a, b):
    return lax.dot_general(
        a, b, (((1,), (1,)), ((), ())), precision=highest, preferred_element_type=jnp.float32
    )


def dot(a, b):
    return jnp.dot(a, b, precision=highest, preferred_element_type=jnp.float32)


def pick_kernel(info, rows, cols, meta, child, diag, panel, pivot_part):
    half = rows // 2
    r, q = info.row(meta), info.col(meta)
    mine, within = r // half, r % half
    p = pl.program_id(0)
    front_block = info.pivot(meta, p)
    block = front_block % info.child_blocks
    present = jnp.logical_and(info.has(meta, mine, block, front_block), block % half == within)
    panel[0] = child[0] * as_float(present)
    first = p * (p + 1) // 2
    for t in range(info.pivot_count):
        other = info.pivot(meta, t)
        other_block = other % info.child_blocks
        here = jnp.logical_and(info.has(meta, mine, other_block, other), other_block % cols == q)

        @pl.when(t <= p)
        def _():
            at = pl.multiple_of(other_block // cols * BLK, BLK)
            pivot_part[first + t] = panel[0, :, pl.ds(at, BLK)] * as_float(here)

    on_diagonal = jnp.logical_and(front_block % rows == r, front_block % cols == q)

    @pl.when(on_diagonal)
    def _():
        pivot_part[first + p] += jnp.where(eye_mask(), diag[0], 0.0)


def cholesky_kernel(count, blocks, lower, inverse, work, rest):
    at = lambda i, j: i * (i + 1) // 2 + j
    span = lambda i: slice(i * BLK, (i + 1) * BLK)
    lower[...] = jnp.zeros_like(lower)
    inverse[...] = jnp.zeros_like(inverse)
    rest[...] = blocks[...]
    row_ids = lax.broadcasted_iota(jnp.int32, (BLK, BLK), 0)
    col_ids = lax.broadcasted_iota(jnp.int32, (BLK, BLK), 1)
    wide_ids = lax.broadcasted_iota(jnp.int32, (1, 2 * BLK), 1)
    column_ids = lax.broadcasted_iota(jnp.int32, (BLK, 1), 0)
    for p in range(count):
        work[:, :BLK] = rest[at(p, p)]
        work[:, BLK:] = jnp.where(row_ids == col_ids, 1.0, 0.0)

        def eliminate(j, carry):
            row = work[pl.ds(j, 1), :]
            lead = jnp.sum(jnp.where(wide_ids == j, row, 0.0), axis=1, keepdims=True)
            left = work[:, :BLK]
            column = jnp.sum(jnp.where(col_ids == j, left, 0.0), axis=1, keepdims=True)
            column = jnp.where(column_ids > j, column, 0.0)
            scaled = row / lead
            work[...] = work[...] - column * scaled
            return carry

        lax.fori_loop(0, BLK, eliminate, 0)
        left = work[:, :BLK]
        lead = jnp.sum(jnp.where(row_ids == col_ids, left, 0.0), axis=1, keepdims=True)
        scale = 1.0 / jnp.sqrt(lead)
        lower[span(p), span(p)] = jnp.where(row_ids <= col_ids, left * scale, 0.0).T
        inverse[span(p), span(p)] = work[:, BLK:] * scale
        own_inverse = inverse[span(p), span(p)]
        for i in range(p + 1, count):
            lower[span(i), span(p)] = dot_t(rest[at(i, p)], own_inverse)
        for i in range(p + 1, count):
            for k in range(p + 1, i + 1):
                rest[at(i, k)] -= dot_t(lower[span(i), span(p)], lower[span(k), span(p)])
    for i in range(1, count):
        for j in range(i):
            known = slice(j * BLK, i * BLK)
            partial = dot(lower[span(i), known], inverse[known, span(j)])
            inverse[span(i), span(j)] = -dot(inverse[span(i), span(i)], partial)


def columns_kernel(info, rows, cols, child_slots, width, meta, own, other, inverse, high, low):
    r, q = info.row(meta), info.col(meta)
    mine = r // (rows // 2)
    v, step = pl.program_id(0), pl.program_id(1)
    parts = []
    for i in range(width):
        block = (step * width + i) * cols + q
        front_block = block + v * info.child_blocks
        keep = jnp.logical_not(info.is_pivot(meta, front_block))
        lanes = slice(i * BLK, (i + 1) * BLK)
        take = as_float(jnp.logical_and(keep, info.has(meta, mine, block, front_block)))
        take_other = as_float(jnp.logical_and(keep, info.has(meta, 1 - mine, block, front_block)))
        parts.append(own[:, lanes] * take + other[:, lanes] * take_other)
    high[...], low[...] = split(dot(inverse[...], jnp.concatenate(parts, axis=1)))


def rows_kernel(info, rows, cols, width, share, held_count, meta, *refs):
    own, other = refs[:held_count], refs[held_count : 2 * held_count]
    lower, inverse, factor, high, low, work = refs[2 * held_count :]
    r, q = info.row(meta), info.col(meta)
    mine = r // (rows // 2)
    s, step = pl.program_id(0), pl.program_id(1)
    holder = info.held(meta, s)

    def chosen(pieces):
        value = pieces[0][...]
        for n in range(1, held_count):
            value = jnp.where(holder == n, pieces[n][...], value)
        return value

    mine_value, other_value = chosen(own), chosen(other)
    parts = []
    for v in range(2):
        for i in range(width):
            block = (step * width + i) * cols + r + s * rows
            front_block = block + v * info.child_blocks
            lanes = slice(i * BLK, (i + 1) * BLK)
            take = as_float(info.has(meta, mine, block, front_block))
            take_other = as_float(info.has(meta, 1 - mine, block, front_block))
            parts.append(mine_value[:, lanes] * take + other_value[:, lanes] * take_other)
    work[...] = dot_t(jnp.concatenate(parts, axis=1).T, inverse[...])
    at = pl.multiple_of(q * share // BLK * BLK, BLK)
    for v in range(2):
        for i in range(width):
            n = v * width + i
            high[v, i, 0], low[v, i, 0] = split(work[n * BLK : (n + 1) * BLK, :])
            factor[v, i, 0] = work[n * BLK : (n + 1) * BLK, pl.ds(at, BLK)]
            block = (step * width + i) * cols + r + s * rows
            for p in range(info.pivot_count):

                @pl.when(block + v * info.child_blocks == info.pivot(meta, p))
                def _():
                    factor[v, i, 0] = lower[p * BLK : (p + 1) * BLK, pl.ds(at, BLK)]
                    high[v, i, 0] = jnp.zeros_like(high[v, i, 0])
                    low[v, i, 0] = jnp.zeros_like(low[v, i, 0])


def update_kernel(info, rows, cols, child_slots, width, first, row_half, meta, *refs):
    own, other, high, low, col_high, col_low, diag = refs[:7]
    tile = refs[-1]
    r, q = info.row(meta), info.col(meta)
    mine = r // (rows // 2)
    step = pl.program_id(0)
    depth = high.shape[-1]
    count = 2 * ROWS_AT_ONCE * BLK
    a_high, a_low = high[...].reshape(count, depth), low[...].reshape(count, depth)
    left = jnp.concatenate([a_high, a_low, a_high], axis=1)

    def row_block(u, j):
        return (first + step * ROWS_AT_ONCE + j) * rows + r + u * info.child_blocks

    takes = {}
    for u in range(2):
        for j in range(ROWS_AT_ONCE):
            front_block = row_block(u, j)
            block = front_block - u * info.child_blocks
            keep = jnp.logical_not(info.is_pivot(meta, front_block))
            takes[u, j] = [
                as_float(jnp.logical_and(keep, info.has(meta, c, block, front_block))) for c in (mine, 1 - mine)
            ]
    for v in range(2):
        for start in range(0, child_slots, width):
            lanes = slice((v * child_slots + start) * BLK, (v * child_slots + start + width) * BLK)
            b_high, b_low = col_high[:, lanes], col_low[:, lanes]
            right = jnp.concatenate([b_high, b_high, b_low], axis=0)
            change = jnp.dot(left, right, preferred_element_type=jnp.float32)
            for i in range(width):
                block = (start + i) * cols + q
                front_block = block + v * info.child_blocks
                keep = jnp.logical_not(info.is_pivot(meta, front_block))
                col_takes = [
                    as_float(jnp.logical_and(keep, info.has(meta, c, block, front_block))) for c in (mine, 1 - mine)
                ]
                from_lanes = slice((start + i) * BLK, (start + i + 1) * BLK)
                to_lanes = slice((v * child_slots + start + i) * BLK, (v * child_slots + start + i + 1) * BLK)
                for u in range(2):
                    for j in range(ROWS_AT_ONCE):
                        n = u * ROWS_AT_ONCE + j
                        tile[u, j, :, to_lanes] = (
                            own[j, 0, :, from_lanes] * (takes[u, j][0] * col_takes[0])
                            + other[j, :, from_lanes] * (takes[u, j][1] * col_takes[1])
                            - change[n * BLK : (n + 1) * BLK, i * BLK : (i + 1) * BLK]
                        )
    for u in range(2):
        for j in range(ROWS_AT_ONCE):
            front_block = row_block(u, j)
            keep = jnp.logical_not(info.is_pivot(meta, front_block))

            @pl.when(jnp.logical_and(keep, front_block % cols == q))
            def _():
                at = pl.multiple_of(front_block // cols * BLK, BLK)
                tile[u, j, :, pl.ds(at, BLK)] += jnp.where(eye_mask(), diag[u, j], 0.0)


def params(grid_size, mib=56):
    return pltpu.CompilerParams(
        dimension_semantics=("arbitrary",) * grid_size, vmem_limit_bytes=mib * 1024 * 1024
    )


def per_device(contrib, front_diag, child_map, pivots):
    rows, cols = lax.axis_size("row"), lax.axis_size("col")
    r, q = lax.axis_index("row"), lax.axis_index("col")
    half = rows // 2
    half_bit = half.bit_length() - 1
    sources = cols // rows
    local_rows, child_width = front_diag.shape[0], contrib.shape[1]
    row_slots = local_rows // BLK
    tile_cols = NF // cols
    child_slots = child_width // BLK
    child_rows = contrib.shape[0] // BLK
    row_half = child_rows // 2
    child_blocks, pivot_count = child_map.shape[1], pivots.shape[0]
    depth = pivot_count * BLK
    width = min(2, child_slots)
    steps, where = spread_plan(rows, cols)
    order = None
    if len(steps) > 2 * sources:
        order, where = fold_plan(where)
    held_count = int(where.max()) + 1
    info = Meta(child_blocks, pivot_count, sources)
    meta = info.pack(child_map, pivots, r, q, where)
    f32, bf16 = jnp.float32, jnp.bfloat16
    shape = jax.ShapeDtypeStruct

    lower_count = pivot_count * (pivot_count + 1) // 2
    panel, pivot_part = pl.pallas_call(
        functools.partial(pick_kernel, info, rows, cols),
        grid_spec=pltpu.PrefetchScalarGridSpec(
            num_scalar_prefetch=1,
            grid=(pivot_count,),
            in_specs=[
                pl.BlockSpec(
                    (1, BLK, child_width), lambda p, m: (info.pivot(m, p) % child_blocks // half, 0, 0)
                ),
                pl.BlockSpec((1, 1, BLK), lambda p, m: (info.pivot(m, p) // rows, 0, 0)),
            ],
            out_specs=[
                pl.BlockSpec((1, BLK, child_width), lambda p, m: (p, 0, 0)),
                pl.BlockSpec((lower_count, BLK, BLK), lambda p, m: (0, 0, 0)),
            ],
        ),
        out_shape=[
            shape((pivot_count, BLK, child_width), f32),
            shape((lower_count, BLK, BLK), f32),
        ],
        compiler_params=params(1),
        name="pick",
    )(meta, contrib.reshape(child_rows, BLK, child_width), front_diag.reshape(row_slots, 1, BLK))
    pivot_blocks = lax.psum(pivot_part, ("row", "col"))
    own = panel.reshape(depth, child_width)
    for bit in range(half_bit):
        own = own + swapped(own, "row", bit)
    other = swapped(own, "row", half_bit)

    def spread(piece):
        held = [piece]
        for buffer, pairs in steps:
            held.append(lax.ppermute(held[buffer], ("row", "col"), pairs))
        if order is None:
            return held
        mine_order = jnp.asarray(order)[:, r, q]
        folded = [piece]
        for n in range(held_count - 1):
            folded.append(sum(jnp.where(mine_order[k] == n, held[k], 0.0) for k in range(1, len(held))))
        return folded

    own_held = spread(own)
    other_held = spread(other)

    own_view = contrib.reshape(row_half, 2, BLK, child_width)
    mine = r // half
    chunk = max(row_half // CHUNKS, ROWS_AT_ONCE)
    received = []
    for first in range(0, row_half, chunk):
        part = lax.dynamic_slice(
            own_view, (first, 1 - mine, 0, 0), (chunk, 1, BLK, child_width)
        ).reshape(chunk, BLK, child_width)
        part = tied(part, received[-2] if len(received) > 1 else other)
        received.append(swapped(part, "row", half_bit))

    lower, inverse = pl.pallas_call(
        functools.partial(cholesky_kernel, pivot_count),
        out_shape=[shape((depth, depth), f32), shape((depth, depth), f32)],
        scratch_shapes=[pltpu.VMEM((BLK, 2 * BLK), f32), pltpu.VMEM((lower_count, BLK, BLK), f32)],
        compiler_params=params(0, 32),
        name="factor_pivots",
    )(pivot_blocks)

    lanes = width * BLK
    groups = child_slots // width
    whole = lambda *_: (0, 0)
    col_high, col_low = pl.pallas_call(
        functools.partial(columns_kernel, info, rows, cols, child_slots, width),
        grid_spec=pltpu.PrefetchScalarGridSpec(
            num_scalar_prefetch=1,
            grid=(2, groups),
            in_specs=[
                pl.BlockSpec((depth, lanes), lambda v, g, m: (0, g)),
                pl.BlockSpec((depth, lanes), lambda v, g, m: (0, g)),
                pl.BlockSpec((depth, depth), whole),
            ],
            out_specs=[pl.BlockSpec((depth, lanes), lambda v, g, m: (0, v * groups + g))] * 2,
        ),
        out_shape=[shape((depth, tile_cols), bf16)] * 2,
        compiler_params=params(2),
        name="factor_at_columns",
    )(meta, own, other, inverse)

    share = depth // cols

    def held_spec(n):
        return pl.BlockSpec(
            (depth, lanes), lambda s, g, m: (0, jnp.where(info.held(m, s) == n, g, 0))
        )

    by_group = lambda s, g, m: (0, g, s, 0, 0)
    factor, row_high, row_low = pl.pallas_call(
        functools.partial(rows_kernel, info, rows, cols, width, share, held_count),
        grid_spec=pltpu.PrefetchScalarGridSpec(
            num_scalar_prefetch=1,
            grid=(sources, groups),
            in_specs=[held_spec(n) for n in range(held_count)] * 2 + [pl.BlockSpec((depth, depth), whole)] * 2,
            out_specs=[
                pl.BlockSpec((2, width, 1, BLK, BLK), by_group),
                pl.BlockSpec((2, width, 1, BLK, depth), by_group),
                pl.BlockSpec((2, width, 1, BLK, depth), by_group),
            ],
            scratch_shapes=[pltpu.VMEM((2 * lanes, depth), f32)],
        ),
        out_shape=[
            shape((2, child_slots, sources, BLK, BLK), f32),
            shape((2, child_slots, sources, BLK, depth), bf16),
            shape((2, child_slots, sources, BLK, depth), bf16),
        ],
        compiler_params=params(2),
        name="factor_at_rows",
    )(meta, *own_held, *other_held, lower, inverse)
    row_high = row_high.reshape(2, row_half, BLK, depth)
    row_low = row_low.reshape(2, row_half, BLK, depth)
    factor = factor.reshape(local_rows, BLK)
    if share < BLK:
        factor = lax.dynamic_slice_in_dim(factor, q * share % BLK, share, 1)

    tile = None
    diag_view = front_diag.reshape(2, row_half, 1, BLK)
    for n, part in enumerate(received):
        first = n * chunk
        at = first // ROWS_AT_ONCE
        mine_of = lambda m: info.row(m) // half
        in_specs = [
            pl.BlockSpec((ROWS_AT_ONCE, 1, BLK, child_width), lambda t, m, at=at: (at + t, mine_of(m), 0, 0)),
            pl.BlockSpec((ROWS_AT_ONCE, BLK, child_width), lambda t, m: (t, 0, 0)),
            pl.BlockSpec((2, ROWS_AT_ONCE, BLK, depth), lambda t, m, at=at: (0, at + t, 0, 0)),
            pl.BlockSpec((2, ROWS_AT_ONCE, BLK, depth), lambda t, m, at=at: (0, at + t, 0, 0)),
            pl.BlockSpec((depth, tile_cols), whole),
            pl.BlockSpec((depth, tile_cols), whole),
            pl.BlockSpec((2, ROWS_AT_ONCE, 1, BLK), lambda t, m, at=at: (0, at + t, 0, 0)),
        ]
        operands = [own_view, part, row_high, row_low, col_high, col_low, diag_view]
        aliases = {}
        if tile is not None:
            in_specs.append(pl.BlockSpec(memory_space=pl.ANY))
            operands.append(tile)
            aliases = {len(operands): 0}
        tile = pl.pallas_call(
            functools.partial(update_kernel, info, rows, cols, child_slots, width, first, row_half),
            grid_spec=pltpu.PrefetchScalarGridSpec(
                num_scalar_prefetch=1,
                grid=(chunk // ROWS_AT_ONCE,),
                in_specs=in_specs,
                out_specs=pl.BlockSpec(
                    (2, ROWS_AT_ONCE, BLK, tile_cols), lambda t, m, at=at: (0, at + t, 0, 0)
                ),
            ),
            out_shape=shape((2, row_half, BLK, tile_cols), f32),
            input_output_aliases=aliases,
            compiler_params=params(1),
            name="update_tile",
        )(meta, *operands)
    return factor, tile.reshape(local_rows, tile_cols)


def solution(mesh):
    placed = (P(("front", "row"), "col"), P(("front", "row")), P("front", None), P("front"))
    return jax.shard_map(
        per_device,
        mesh=mesh,
        in_specs=placed,
        out_specs=(P(("front", "row"), "col"), P(("front", "row"), "col")),
        check_vma=False,
    )
```

```python
import functools

import jax
import jax.numpy as jnp
import numpy as np
from jax import lax
from jax.experimental import pallas as pl
from jax.experimental.pallas import tpu as pltpu
from jax.sharding import PartitionSpec as P

NF = 8192
BLK = 128
CHUNKS = (10, 4, 2)
ROWS_AT_ONCE = 2

highest = lax.Precision.HIGHEST


def swapped(shard, axis, bit):
    return lax.ppermute(shard, axis, [(i, i ^ 1 << bit) for i in range(lax.axis_size(axis))])


def tied(values, after):
    return lax.optimization_barrier((values, after))[0]


def spread_plan(rows, cols):
    sources = cols // rows
    where = -np.ones((sources, rows, cols), np.int32)
    for r in range(rows):
        for s in range(sources):
            where[s, r, r + s * rows] = 0
    steps = []
    while (where < 0).any():
        for buffer in range(len(steps) + 1):
            moves = []
            for r in range(rows):
                sign = 1 if r <= cols - 1 - (r + (sources - 1) * rows) else -1
                taken = set()
                for h in range(cols)[::sign]:
                    for s in range(sources):
                        if where[s, r, h] != buffer:
                            continue
                        open_to = [
                            d for d in range(cols)
                            if where[s, r, d] < 0 and d not in taken and abs(d - h) <= rows
                        ]
                        if open_to:
                            d = max(open_to, key=lambda d: sign * (d - h))
                            taken.add(d)
                            moves.append((s, r, h, d))
            if moves:
                break
        steps.append((buffer, [(r * cols + h, r * cols + d) for _, r, h, d in moves]))
        for s, r, _, d in moves:
            where[s, r, d] = len(steps)
    return steps, where


def fold_plan(where):
    sources, rows, cols = where.shape
    steps = where.max()
    order = -np.ones((steps + 1, rows, cols), np.int32)
    folded = np.zeros_like(where)
    for r in range(rows):
        for d in range(cols):
            got = sorted((where[s, r, d], s) for s in range(sources) if where[s, r, d] > 0)
            for n, (step, s) in enumerate(got):
                order[step, r, d] = n
                folded[s, r, d] = n + 1
    return order, folded


class Meta:
    def __init__(self, child_blocks, pivot_count, sources):
        self.child_blocks, self.pivot_count, self.sources = child_blocks, pivot_count, sources

    def pack(self, child_map, pivots, row_index, col_index, where):
        place = jnp.stack([row_index, col_index]).astype(jnp.int32)
        held = jnp.asarray(where)[:, row_index, col_index]
        return jnp.concatenate([child_map.reshape(-1), pivots, place, held])

    def has(self, meta, child, block, front_block):
        return meta[child * self.child_blocks + block] == front_block

    def pivot(self, meta, p):
        return meta[2 * self.child_blocks + p]

    def row(self, meta):
        return meta[2 * self.child_blocks + self.pivot_count]

    def col(self, meta):
        return meta[2 * self.child_blocks + self.pivot_count + 1]

    def held(self, meta, s):
        return meta[2 * self.child_blocks + self.pivot_count + 2 + s]

    def is_pivot(self, meta, front_block):
        hit = front_block == self.pivot(meta, 0)
        for p in range(1, self.pivot_count):
            hit = jnp.logical_or(hit, front_block == self.pivot(meta, p))
        return hit


def as_float(flag):
    return jnp.where(flag, 1.0, 0.0).astype(jnp.float32)


def eye_mask():
    return lax.broadcasted_iota(jnp.int32, (BLK, BLK), 0) == lax.broadcasted_iota(jnp.int32, (BLK, BLK), 1)


def split(value):
    high = value.astype(jnp.bfloat16)
    return high, (value - high.astype(jnp.float32)).astype(jnp.bfloat16)


def dot_t(a, b):
    return lax.dot_general(
        a, b, (((1,), (1,)), ((), ())), precision=highest, preferred_element_type=jnp.float32
    )


def dot(a, b):
    return jnp.dot(a, b, precision=highest, preferred_element_type=jnp.float32)


def pick_kernel(info, rows, cols, meta, child, diag, panel, pivot_part):
    half = rows // 2
    r, q = info.row(meta), info.col(meta)
    mine, within = r // half, r % half
    p = pl.program_id(0)
    front_block = info.pivot(meta, p)
    block = front_block % info.child_blocks
    present = jnp.logical_and(info.has(meta, mine, block, front_block), block % half == within)
    panel[0] = child[0] * as_float(present)
    first = p * (p + 1) // 2
    for t in range(info.pivot_count):
        other = info.pivot(meta, t)
        other_block = other % info.child_blocks
        here = jnp.logical_and(info.has(meta, mine, other_block, other), other_block % cols == q)

        @pl.when(t <= p)
        def _():
            at = pl.multiple_of(other_block // cols * BLK, BLK)
            pivot_part[first + t] = panel[0, :, pl.ds(at, BLK)] * as_float(here)

    on_diagonal = jnp.logical_and(front_block % rows == r, front_block % cols == q)

    @pl.when(on_diagonal)
    def _():
        pivot_part[first + p] += jnp.where(eye_mask(), diag[0], 0.0)


def cholesky_kernel(count, blocks, lower, inverse, work, rest):
    at = lambda i, j: i * (i + 1) // 2 + j
    span = lambda i: slice(i * BLK, (i + 1) * BLK)
    lower[...] = jnp.zeros_like(lower)
    inverse[...] = jnp.zeros_like(inverse)
    rest[...] = blocks[...]
    row_ids = lax.broadcasted_iota(jnp.int32, (BLK, BLK), 0)
    col_ids = lax.broadcasted_iota(jnp.int32, (BLK, BLK), 1)
    wide_ids = lax.broadcasted_iota(jnp.int32, (1, 2 * BLK), 1)
    column_ids = lax.broadcasted_iota(jnp.int32, (BLK, 1), 0)
    for p in range(count):
        work[:, :BLK] = rest[at(p, p)]
        work[:, BLK:] = jnp.where(row_ids == col_ids, 1.0, 0.0)

        def eliminate(j, carry):
            row = work[pl.ds(j, 1), :]
            lead = jnp.sum(jnp.where(wide_ids == j, row, 0.0), axis=1, keepdims=True)
            left = work[:, :BLK]
            column = jnp.sum(jnp.where(col_ids == j, left, 0.0), axis=1, keepdims=True)
            column = jnp.where(column_ids > j, column, 0.0)
            scaled = row / lead
            work[...] = work[...] - column * scaled
            return carry

        lax.fori_loop(0, BLK, eliminate, 0)
        left = work[:, :BLK]
        lead = jnp.sum(jnp.where(row_ids == col_ids, left, 0.0), axis=1, keepdims=True)
        scale = 1.0 / jnp.sqrt(lead)
        lower[span(p), span(p)] = jnp.where(row_ids <= col_ids, left * scale, 0.0).T
        inverse[span(p), span(p)] = work[:, BLK:] * scale
        own_inverse = inverse[span(p), span(p)]
        for i in range(p + 1, count):
            lower[span(i), span(p)] = dot_t(rest[at(i, p)], own_inverse)
        for i in range(p + 1, count):
            for k in range(p + 1, i + 1):
                rest[at(i, k)] -= dot_t(lower[span(i), span(p)], lower[span(k), span(p)])
    for i in range(1, count):
        for j in range(i):
            known = slice(j * BLK, i * BLK)
            partial = dot(lower[span(i), known], inverse[known, span(j)])
            inverse[span(i), span(j)] = -dot(inverse[span(i), span(i)], partial)


def columns_kernel(info, rows, cols, child_slots, width, meta, own, other, inverse, high, low):
    r, q = info.row(meta), info.col(meta)
    mine = r // (rows // 2)
    v, step = pl.program_id(0), pl.program_id(1)
    parts = []
    for i in range(width):
        block = (step * width + i) * cols + q
        front_block = block + v * info.child_blocks
        keep = jnp.logical_not(info.is_pivot(meta, front_block))
        lanes = slice(i * BLK, (i + 1) * BLK)
        take = as_float(jnp.logical_and(keep, info.has(meta, mine, block, front_block)))
        take_other = as_float(jnp.logical_and(keep, info.has(meta, 1 - mine, block, front_block)))
        parts.append(own[:, lanes] * take + other[:, lanes] * take_other)
    high[...], low[...] = split(dot(inverse[...], jnp.concatenate(parts, axis=1)))


def chosen(holder, pieces):
    value = pieces[0][...]
    for n in range(1, len(pieces)):
        value = jnp.where(holder == n, pieces[n][...], value)
    return value


def rows_first_kernel(info, meta, *refs):
    pieces, inverse, product = refs[:-2], refs[-2], refs[-1]
    product[0] = dot_t(chosen(info.held(meta, pl.program_id(0)), pieces).T, inverse[...])


def rows_kernel(info, rows, cols, width, share, meta, *refs):
    pieces = refs[:-7]
    own, lower, inverse, factor, high, low, work = refs[-7:]
    r, q = info.row(meta), info.col(meta)
    mine = r // (rows // 2)
    s, step = pl.program_id(0), pl.program_id(1)
    other = dot_t(chosen(info.held(meta, s), pieces).T, inverse[...])
    at = pl.multiple_of(q * share // BLK * BLK, BLK)
    for i in range(width):
        block = (step * width + i) * cols + r + s * rows
        span = slice(i * BLK, (i + 1) * BLK)
        for v in range(2):
            front_block = block + v * info.child_blocks
            take = as_float(info.has(meta, mine, block, front_block))
            take_other = as_float(info.has(meta, 1 - mine, block, front_block))
            value = own[0, span, :] * take + other[span, :] * take_other
            high[v, i, 0], low[v, i, 0] = split(value)
            work[...] = value
            factor[v, i, 0] = work[:, pl.ds(at, BLK)]
            for p in range(info.pivot_count):

                @pl.when(front_block == info.pivot(meta, p))
                def _():
                    factor[v, i, 0] = lower[p * BLK : (p + 1) * BLK, pl.ds(at, BLK)]
                    high[v, i, 0] = jnp.zeros_like(high[v, i, 0])
                    low[v, i, 0] = jnp.zeros_like(low[v, i, 0])


def update_kernel(info, rows, cols, child_slots, width, first, meta, *refs):
    own, other, high, low, col_high, col_low, diag = refs[:7]
    tile = refs[-1]
    r, q = info.row(meta), info.col(meta)
    mine = r // (rows // 2)
    step, v = pl.program_id(0), pl.program_id(1)
    depth = high.shape[-1]
    count = 2 * ROWS_AT_ONCE * BLK
    a_high, a_low = high[...].reshape(count, depth), low[...].reshape(count, depth)
    left = jnp.concatenate([a_high, a_low, a_high], axis=1)

    def takes(block, front_block):
        keep = jnp.logical_not(info.is_pivot(meta, front_block))
        return [as_float(jnp.logical_and(keep, info.has(meta, c, block, front_block))) for c in (mine, 1 - mine)]

    def row_block(j):
        return (first + step * ROWS_AT_ONCE + j) * rows + r

    row_takes = {
        (u, j): takes(row_block(j), row_block(j) + u * info.child_blocks)
        for u in range(2)
        for j in range(ROWS_AT_ONCE)
    }
    for start in range(0, child_slots, width):
        at = pl.multiple_of((v * child_slots + start) * BLK, BLK)
        b_high, b_low = col_high[:, pl.ds(at, width * BLK)], col_low[:, pl.ds(at, width * BLK)]
        right = jnp.concatenate([b_high, b_high, b_low], axis=0)
        change = jnp.dot(left, right, preferred_element_type=jnp.float32)
        for i in range(width):
            block = (start + i) * cols + q
            col_takes = takes(block, block + v * info.child_blocks)
            lanes = slice((start + i) * BLK, (start + i + 1) * BLK)
            for (u, j), row_take in row_takes.items():
                n = u * ROWS_AT_ONCE + j
                tile[u, j, :, lanes] = (
                    own[j, 0, :, lanes] * (row_take[0] * col_takes[0])
                    + other[j, :, lanes] * (row_take[1] * col_takes[1])
                    - change[n * BLK : (n + 1) * BLK, i * BLK : (i + 1) * BLK]
                )
    for u in range(2):
        for j in range(ROWS_AT_ONCE):
            front_block = row_block(j) + u * info.child_blocks
            slot = front_block // cols
            here = jnp.logical_and(front_block % cols == q, slot // child_slots == v)

            @pl.when(jnp.logical_and(here, jnp.logical_not(info.is_pivot(meta, front_block))))
            def _():
                at = pl.multiple_of(slot % child_slots * BLK, BLK)
                tile[u, j, :, pl.ds(at, BLK)] += jnp.where(eye_mask(), diag[u, j], 0.0)


def params(grid_size, mib=56):
    return pltpu.CompilerParams(
        dimension_semantics=("arbitrary",) * grid_size, vmem_limit_bytes=mib * 1024 * 1024
    )


def per_device(contrib, front_diag, child_map, pivots):
    rows, cols = lax.axis_size("row"), lax.axis_size("col")
    r, q = lax.axis_index("row"), lax.axis_index("col")
    half = rows // 2
    half_bit = half.bit_length() - 1
    sources = cols // rows
    local_rows, child_width = front_diag.shape[0], contrib.shape[1]
    row_slots = local_rows // BLK
    tile_cols = NF // cols
    child_slots = child_width // BLK
    child_rows = contrib.shape[0] // BLK
    row_half = child_rows // 2
    child_blocks, pivot_count = child_map.shape[1], pivots.shape[0]
    depth = pivot_count * BLK
    width = min(4, child_slots)
    steps, where = spread_plan(rows, cols)
    order = None
    if len(steps) > 2 * sources:
        order, where = fold_plan(where)
    held_count = int(where.max()) + 1
    info = Meta(child_blocks, pivot_count, sources)
    meta = info.pack(child_map, pivots, r, q, where)
    f32, bf16 = jnp.float32, jnp.bfloat16
    shape = jax.ShapeDtypeStruct

    lower_count = pivot_count * (pivot_count + 1) // 2
    panel, pivot_part = pl.pallas_call(
        functools.partial(pick_kernel, info, rows, cols),
        grid_spec=pltpu.PrefetchScalarGridSpec(
            num_scalar_prefetch=1,
            grid=(pivot_count,),
            in_specs=[
                pl.BlockSpec(
                    (1, BLK, child_width), lambda p, m: (info.pivot(m, p) % child_blocks // half, 0, 0)
                ),
                pl.BlockSpec((1, 1, BLK), lambda p, m: (info.pivot(m, p) // rows, 0, 0)),
            ],
            out_specs=[
                pl.BlockSpec((1, BLK, child_width), lambda p, m: (p, 0, 0)),
                pl.BlockSpec((lower_count, BLK, BLK), lambda p, m: (0, 0, 0)),
            ],
        ),
        out_shape=[
            shape((pivot_count, BLK, child_width), f32),
            shape((lower_count, BLK, BLK), f32),
        ],
        compiler_params=params(1),
        name="pick",
    )(meta, contrib.reshape(child_rows, BLK, child_width), front_diag.reshape(row_slots, 1, BLK))
    pivot_blocks = pivot_part
    first_blocks = None
    for bit in range(cols.bit_length() - 1):
        received_blocks = swapped(pivot_blocks, "col", bit)
        first_blocks = received_blocks if first_blocks is None else first_blocks
        pivot_blocks = pivot_blocks + received_blocks
    for bit in range(half_bit, -1, -1):
        received_blocks = swapped(pivot_blocks, "row", bit)
        pivot_blocks = pivot_blocks + received_blocks
    own = panel.reshape(depth, child_width)
    for bit in range(half_bit):
        own = own + swapped(own, "row", bit)
    other = swapped(own, "row", half_bit)

    def spread(piece, late=(), wait=None):
        held = [piece]
        for n, (buffer, pairs) in enumerate(steps):
            sent = tied(held[buffer], wait) if n in late else held[buffer]
            held.append(lax.ppermute(sent, ("row", "col"), pairs))
        if order is None:
            return held
        mine_order = jnp.asarray(order)[:, r, q]
        folded = [piece]
        for n in range(held_count - 1):
            folded.append(sum(jnp.where(mine_order[k] == n, held[k], 0.0) for k in range(1, len(held))))
        return folded

    own_held = spread(tied(own, first_blocks))

    lower, inverse = pl.pallas_call(
        functools.partial(cholesky_kernel, pivot_count),
        out_shape=[shape((depth, depth), f32), shape((depth, depth), f32)],
        scratch_shapes=[pltpu.VMEM((BLK, 2 * BLK), f32), pltpu.VMEM((lower_count, BLK, BLK), f32)],
        compiler_params=params(0, 32),
        name="factor_pivots",
    )(tied(pivot_blocks, [own_held[n] for n in (1, 3) if n < held_count]))

    other_held = spread(other, [n for n, (_, pairs) in enumerate(steps) if n not in (0, 2)], inverse)

    own_view = contrib.reshape(row_half, 2, BLK, child_width)
    mine = r // half
    chunks = CHUNKS if sum(CHUNKS) == row_half else (ROWS_AT_ONCE,) * (row_half // ROWS_AT_ONCE)
    received = []
    first = 0
    for chunk in chunks:
        part = lax.dynamic_slice(
            own_view, (first, 1 - mine, 0, 0), (chunk, 1, BLK, child_width)
        ).reshape(chunk, BLK, child_width)
        part = tied(part, (received[-2] if len(received) > 1 else own, inverse) if received else (other, received_blocks))
        received.append(swapped(part, "row", half_bit))
        first += chunk

    lanes = width * BLK
    groups = child_slots // width
    whole = lambda *_: (0, 0)
    col_high, col_low = pl.pallas_call(
        functools.partial(columns_kernel, info, rows, cols, child_slots, width),
        grid_spec=pltpu.PrefetchScalarGridSpec(
            num_scalar_prefetch=1,
            grid=(2, groups),
            in_specs=[
                pl.BlockSpec((depth, lanes), lambda v, g, m: (0, g)),
                pl.BlockSpec((depth, lanes), lambda v, g, m: (0, g)),
                pl.BlockSpec((depth, depth), whole),
            ],
            out_specs=[pl.BlockSpec((depth, lanes), lambda v, g, m: (0, v * groups + g))] * 2,
        ),
        out_shape=[shape((depth, tile_cols), bf16)] * 2,
        compiler_params=params(2),
        name="factor_at_columns",
    )(meta, own, other, inverse)

    share = depth // cols

    def held_spec(n):
        return pl.BlockSpec(
            (depth, lanes), lambda s, g, m: (0, jnp.where(info.held(m, s) == n, g, 0))
        )

    by_group = lambda s, g, m: (0, g, s, 0, 0)
    own_rows = pl.pallas_call(
        functools.partial(rows_first_kernel, info),
        grid_spec=pltpu.PrefetchScalarGridSpec(
            num_scalar_prefetch=1,
            grid=(sources, groups),
            in_specs=[held_spec(n) for n in range(held_count)] + [pl.BlockSpec((depth, depth), whole)],
            out_specs=pl.BlockSpec((1, lanes, depth), lambda s, g, m: (s, g, 0)),
        ),
        out_shape=shape((sources, child_width, depth), f32),
        compiler_params=params(2),
        name="factor_at_rows_first",
    )(meta, *own_held, inverse)
    factor, row_high, row_low = pl.pallas_call(
        functools.partial(rows_kernel, info, rows, cols, width, share),
        grid_spec=pltpu.PrefetchScalarGridSpec(
            num_scalar_prefetch=1,
            grid=(sources, groups),
            in_specs=[held_spec(n) for n in range(held_count)]
            + [pl.BlockSpec((1, lanes, depth), lambda s, g, m: (s, g, 0))]
            + [pl.BlockSpec((depth, depth), whole)] * 2,
            out_specs=[
                pl.BlockSpec((2, width, 1, BLK, BLK), by_group),
                pl.BlockSpec((2, width, 1, BLK, depth), by_group),
                pl.BlockSpec((2, width, 1, BLK, depth), by_group),
            ],
            scratch_shapes=[pltpu.VMEM((BLK, depth), f32)],
        ),
        out_shape=[
            shape((2, child_slots, sources, BLK, BLK), f32),
            shape((2, child_slots, sources, BLK, depth), bf16),
            shape((2, child_slots, sources, BLK, depth), bf16),
        ],
        compiler_params=params(2),
        name="factor_at_rows",
    )(meta, *other_held, own_rows, lower, inverse)
    row_high = row_high.reshape(2, row_half, BLK, depth)
    row_low = row_low.reshape(2, row_half, BLK, depth)
    factor = factor.reshape(local_rows, BLK)
    if share < BLK:
        factor = lax.dynamic_slice_in_dim(factor, q * share % BLK, share, 1)

    tile = None
    diag_view = front_diag.reshape(2, row_half, 1, BLK)
    mine_of = lambda m: info.row(m) // half
    first = 0
    for part in received:
        at = first // ROWS_AT_ONCE
        in_specs = [
            pl.BlockSpec((ROWS_AT_ONCE, 1, BLK, child_width), lambda t, v, m, at=at: (at + t, mine_of(m), 0, 0)),
            pl.BlockSpec((ROWS_AT_ONCE, BLK, child_width), lambda t, v, m: (t, 0, 0)),
            pl.BlockSpec((2, ROWS_AT_ONCE, BLK, depth), lambda t, v, m, at=at: (0, at + t, 0, 0)),
            pl.BlockSpec((2, ROWS_AT_ONCE, BLK, depth), lambda t, v, m, at=at: (0, at + t, 0, 0)),
            pl.BlockSpec((depth, tile_cols), whole),
            pl.BlockSpec((depth, tile_cols), whole),
            pl.BlockSpec((2, ROWS_AT_ONCE, 1, BLK), lambda t, v, m, at=at: (0, at + t, 0, 0)),
        ]
        operands = [own_view, part, row_high, row_low, col_high, col_low, diag_view]
        aliases = {}
        if tile is not None:
            in_specs.append(pl.BlockSpec(memory_space=pl.ANY))
            operands.append(tile)
            aliases = {len(operands): 0}
        tile = pl.pallas_call(
            functools.partial(update_kernel, info, rows, cols, child_slots, width, first),
            grid_spec=pltpu.PrefetchScalarGridSpec(
                num_scalar_prefetch=1,
                grid=(part.shape[0] // ROWS_AT_ONCE, 2),
                in_specs=in_specs,
                out_specs=pl.BlockSpec(
                    (2, ROWS_AT_ONCE, BLK, child_width), lambda t, v, m, at=at: (0, at + t, 0, v)
                ),
            ),
            out_shape=shape((2, row_half, BLK, tile_cols), f32),
            input_output_aliases=aliases,
            compiler_params=params(2),
            name="update_tile",
        )(meta, *operands)
        first += part.shape[0]
    return factor, tile.reshape(local_rows, tile_cols)


def solution(mesh):
    placed = (P(("front", "row"), "col"), P(("front", "row")), P("front", None), P("front"))
    return jax.shard_map(
        per_device,
        mesh=mesh,
        in_specs=placed,
        out_specs=(P(("front", "row"), "col"), P(("front", "row"), "col")),
        check_vma=False,
    )
```

```python
import functools

import jax
import jax.numpy as jnp
import numpy as np
from jax import lax
from jax.experimental import pallas as pl
from jax.experimental.pallas import tpu as pltpu
from jax.sharding import PartitionSpec as P

NF = 8192
BLK = 128
HALVES = 2
CHUNKS = (4, 4)
ROWS_AT_ONCE = 2
PACE = 1.0
LATE = 1.0

highest = lax.Precision.HIGHEST


def swapped(shard, axis, bit):
    return lax.ppermute(shard, axis, [(i, i ^ 1 << bit) for i in range(lax.axis_size(axis))])


def one_after(*arrays):
    first = [array[(0,) * array.ndim] for array in arrays]
    there = functools.reduce(jnp.logical_and, [value == value for value in first])
    return jnp.where(there, 1, 0)


def gated(value, *arrays):
    return value * one_after(*arrays).astype(value.dtype)


def spread_plan(rows, cols):
    sources = cols // rows
    where = -np.ones((sources, rows, cols), np.int32)
    for r in range(rows):
        for s in range(sources):
            where[s, r, r + s * rows] = 0
    steps = []
    while (where < 0).any():
        for buffer in range(len(steps) + 1):
            moves = []
            for r in range(rows):
                sign = 1 if r <= cols - 1 - (r + (sources - 1) * rows) else -1
                taken = set()
                for h in range(cols)[::-sign]:
                    for s in range(sources):
                        if where[s, r, h] != buffer:
                            continue
                        open_to = [
                            d for d in range(cols)
                            if where[s, r, d] < 0 and d not in taken and abs(d - h) <= rows
                        ]
                        if open_to:
                            d = max(open_to, key=lambda d: sign * (d - h))
                            taken.add(d)
                            moves.append((s, r, h, d))
            if moves:
                break
        steps.append((buffer, [(r * cols + h, r * cols + d) for _, r, h, d in moves]))
        for s, r, _, d in moves:
            where[s, r, d] = len(steps)
    return steps, where


def fold_plan(where):
    sources, rows, cols = where.shape
    steps = where.max()
    order = -np.ones((steps + 1, rows, cols), np.int32)
    folded = np.zeros_like(where)
    for r in range(rows):
        for d in range(cols):
            got = sorted((where[s, r, d], s) for s in range(sources) if where[s, r, d] > 0)
            for n, (step, s) in enumerate(got):
                order[step, r, d] = n
                folded[s, r, d] = n + 1
    return order, folded


class Meta:
    def __init__(self, child_blocks, pivot_count, sources):
        self.child_blocks, self.pivot_count, self.sources = child_blocks, pivot_count, sources

    def pack(self, child_map, pivots, row_index, col_index, where, turns):
        place = jnp.stack([row_index, col_index]).astype(jnp.int32)
        held = jnp.asarray(np.concatenate([where, turns]))[:, row_index, col_index]
        return jnp.concatenate([child_map.reshape(-1), pivots, place, held])

    def has(self, meta, child, block, front_block):
        return meta[child * self.child_blocks + block] == front_block

    def pivot(self, meta, p):
        return meta[2 * self.child_blocks + p]

    def row(self, meta):
        return meta[2 * self.child_blocks + self.pivot_count]

    def col(self, meta):
        return meta[2 * self.child_blocks + self.pivot_count + 1]

    def held(self, meta, s):
        return meta[2 * self.child_blocks + self.pivot_count + 2 + s]

    def source(self, meta, turn):
        return self.held(meta, self.sources + turn)

    def is_pivot(self, meta, front_block):
        hit = front_block == self.pivot(meta, 0)
        for p in range(1, self.pivot_count):
            hit = jnp.logical_or(hit, front_block == self.pivot(meta, p))
        return hit


def as_float(flag):
    return jnp.where(flag, 1.0, 0.0).astype(jnp.float32)


def eye_mask():
    return lax.broadcasted_iota(jnp.int32, (BLK, BLK), 0) == lax.broadcasted_iota(jnp.int32, (BLK, BLK), 1)


def split(value):
    high = value.astype(jnp.bfloat16)
    return high, (value - high.astype(jnp.float32)).astype(jnp.bfloat16)


def dot_t(a, b):
    return lax.dot_general(
        a, b, (((1,), (1,)), ((), ())), precision=highest, preferred_element_type=jnp.float32
    )


def dot(a, b):
    return jnp.dot(a, b, precision=highest, preferred_element_type=jnp.float32)


def pick_kernel(info, rows, cols, meta, child, diag, panel, pivot_part):
    half = rows // 2
    r, q = info.row(meta), info.col(meta)
    mine, within = r // half, r % half
    p = pl.program_id(0)
    front_block = info.pivot(meta, p)
    block = front_block % info.child_blocks
    present = jnp.logical_and(info.has(meta, mine, block, front_block), block % half == within)
    panel[0] = child[0] * as_float(present)
    first = p * (p + 1) // 2
    for t in range(info.pivot_count):
        other = info.pivot(meta, t)
        other_block = other % info.child_blocks
        here = jnp.logical_and(info.has(meta, mine, other_block, other), other_block % cols == q)

        @pl.when(t <= p)
        def _():
            at = pl.multiple_of(other_block // cols * BLK, BLK)
            pivot_part[first + t] = panel[0, :, pl.ds(at, BLK)] * as_float(here)

    on_diagonal = jnp.logical_and(front_block % rows == r, front_block % cols == q)

    @pl.when(on_diagonal)
    def _():
        pivot_part[first + p] += jnp.where(eye_mask(), diag[0], 0.0)


def cholesky_kernel(count, blocks, lower, inverse, inverse_t, work, rest):
    at = lambda i, j: i * (i + 1) // 2 + j
    span = lambda i: slice(i * BLK, (i + 1) * BLK)
    lower[...] = jnp.zeros_like(lower)
    inverse[...] = jnp.zeros_like(inverse)
    rest[...] = blocks[...]
    row_ids = lax.broadcasted_iota(jnp.int32, (BLK, BLK), 0)
    col_ids = lax.broadcasted_iota(jnp.int32, (BLK, BLK), 1)
    wide_ids = lax.broadcasted_iota(jnp.int32, (1, 2 * BLK), 1)
    column_ids = lax.broadcasted_iota(jnp.int32, (BLK, 1), 0)
    for p in range(count):
        work[:, :BLK] = rest[at(p, p)]
        work[:, BLK:] = jnp.where(row_ids == col_ids, 1.0, 0.0)

        def eliminate(j, carry):
            row = work[pl.ds(j, 1), :]
            lead = jnp.sum(jnp.where(wide_ids == j, row, 0.0), axis=1, keepdims=True)
            left = work[:, :BLK]
            column = jnp.sum(jnp.where(col_ids == j, left, 0.0), axis=1, keepdims=True)
            column = jnp.where(column_ids > j, column, 0.0)
            scaled = row / lead
            work[...] = work[...] - column * scaled
            return carry

        lax.fori_loop(0, BLK, eliminate, 0)
        left = work[:, :BLK]
        lead = jnp.sum(jnp.where(row_ids == col_ids, left, 0.0), axis=1, keepdims=True)
        scale = 1.0 / jnp.sqrt(lead)
        lower[span(p), span(p)] = jnp.where(row_ids <= col_ids, left * scale, 0.0).T
        inverse[span(p), span(p)] = work[:, BLK:] * scale
        own_inverse = inverse[span(p), span(p)]
        for i in range(p + 1, count):
            lower[span(i), span(p)] = dot_t(rest[at(i, p)], own_inverse)
        for i in range(p + 1, count):
            for k in range(p + 1, i + 1):
                rest[at(i, k)] -= dot_t(lower[span(i), span(p)], lower[span(k), span(p)])
    for i in range(1, count):
        for j in range(i):
            known = slice(j * BLK, i * BLK)
            partial = dot(lower[span(i), known], inverse[known, span(j)])
            inverse[span(i), span(j)] = -dot(inverse[span(i), span(i)], partial)
    inverse_t[...] = inverse[...].T


def columns_kernel(info, rows, cols, child_slots, width, meta, own, other, inverse, *refs):
    stacked = refs[-1]
    r, q = info.row(meta), info.col(meta)
    mine = r // (rows // 2)
    v, step = pl.program_id(0), pl.program_id(1)
    parts = []
    for i in range(width):
        block = (step * width + i) * cols + q
        front_block = block + v * info.child_blocks
        keep = jnp.logical_not(info.is_pivot(meta, front_block))
        lanes = slice(i * BLK, (i + 1) * BLK)
        take = as_float(jnp.logical_and(keep, info.has(meta, mine, block, front_block)))
        take_other = as_float(jnp.logical_and(keep, info.has(meta, 1 - mine, block, front_block)))
        parts.append(own[:, lanes] * take + other[:, lanes] * take_other)
    high, low = split(dot(inverse[...], jnp.concatenate(parts, axis=1)))
    depth = high.shape[0]
    stacked[:depth], stacked[depth : 2 * depth], stacked[2 * depth :] = high, high, low


def chosen(holder, used, pieces):
    value = pieces[0][...]
    for n, piece in zip(used[1:], pieces[1:]):
        value = jnp.where(holder == n, piece[...], value)
    return value


def rows_kernel(info, rows, cols, width, share, turn, first, used, meta, *refs):
    r, q = info.row(meta), info.col(meta)
    mine = r // (rows // 2)
    s, step = info.source(meta, turn), pl.program_id(0) + first
    lower, inverse_t = refs[len(used) :][:2]
    factor, parts, work = refs[-3:]
    piece = chosen(info.held(meta, s), used, refs[: len(used)])
    half_depth = piece.shape[0] // 2
    own_value = dot(piece[:half_depth].T, inverse_t[...])
    other_value = dot(piece[half_depth:].T, inverse_t[...])
    at = pl.multiple_of(q * share // BLK * BLK, BLK)
    depth = lower.shape[0]
    for i in range(width):
        block = (step * width + i) * cols + r + s * rows
        span = slice(i * BLK, (i + 1) * BLK)
        for v in range(2):
            front_block = block + v * info.child_blocks
            take = as_float(info.has(meta, mine, block, front_block))
            take_other = as_float(info.has(meta, 1 - mine, block, front_block))
            value = own_value[span, :] * take + other_value[span, :] * take_other
            high, low = split(value)
            parts[v, i, :, :depth], parts[v, i, :, depth : 2 * depth], parts[v, i, :, 2 * depth :] = high, low, high
            work[...] = value
            factor[v, i, 0] = work[:, pl.ds(at, BLK)]
            for p in range(info.pivot_count):

                @pl.when(front_block == info.pivot(meta, p))
                def _():
                    factor[v, i, 0] = lower[p * BLK : (p + 1) * BLK, pl.ds(at, BLK)]
                    parts[v, i] = jnp.zeros_like(parts[v, i])


def update_kernel(info, rows, cols, child_slots, width, turn, first, meta, *refs):
    own, other, left, right, diag = refs[:5]
    tile, token = refs[-2:]
    token[...] = jnp.zeros_like(token)
    r, q = info.row(meta), info.col(meta)
    mine = r // (rows // 2)
    step, v = pl.program_id(0), pl.program_id(1)
    left_rows = left[...].reshape(2 * ROWS_AT_ONCE * BLK, left.shape[-1])

    def takes(block, front_block):
        keep = jnp.logical_not(info.is_pivot(meta, front_block))
        return [as_float(jnp.logical_and(keep, info.has(meta, c, block, front_block))) for c in (mine, 1 - mine)]

    def row_block(j):
        return (first + step * ROWS_AT_ONCE + j) * cols + info.source(meta, turn) * rows + r

    row_takes = {
        (u, j): takes(row_block(j), row_block(j) + u * info.child_blocks)
        for u in range(2)
        for j in range(ROWS_AT_ONCE)
    }
    for start in range(0, child_slots, width):
        at = pl.multiple_of((v * child_slots + start) * BLK, BLK)
        change = jnp.dot(left_rows, right[:, pl.ds(at, width * BLK)], preferred_element_type=jnp.float32)
        for i in range(width):
            block = (start + i) * cols + q
            col_takes = takes(block, block + v * info.child_blocks)
            lanes = slice((start + i) * BLK, (start + i + 1) * BLK)
            for (u, j), row_take in row_takes.items():
                n = u * ROWS_AT_ONCE + j
                tile[u, j, 0, :, lanes] = (
                    own[j, 0, 0, :, lanes] * (row_take[0] * col_takes[0])
                    + other[j, :, lanes] * (row_take[1] * col_takes[1])
                    - change[n * BLK : (n + 1) * BLK, i * BLK : (i + 1) * BLK]
                )
    for u in range(2):
        for j in range(ROWS_AT_ONCE):
            front_block = row_block(j) + u * info.child_blocks
            slot = front_block // cols
            here = jnp.logical_and(front_block % cols == q, slot // child_slots == v)

            @pl.when(jnp.logical_and(here, jnp.logical_not(info.is_pivot(meta, front_block))))
            def _():
                at = pl.multiple_of(slot % child_slots * BLK, BLK)
                tile[u, j, 0, :, pl.ds(at, BLK)] += jnp.where(eye_mask(), diag[u, j, 0], 0.0)


def params(grid_size, mib=32):
    return pltpu.CompilerParams(
        dimension_semantics=("arbitrary",) * grid_size, vmem_limit_bytes=mib * 1024 * 1024
    )


def about(micros):
    micros *= PACE
    return pl.CostEstimate(flops=int(micros * 1.15e9), bytes_accessed=int(micros * 3.69e6), transcendentals=0)


def per_device(contrib, front_diag, child_map, pivots):
    rows, cols = lax.axis_size("row"), lax.axis_size("col")
    r, q = lax.axis_index("row"), lax.axis_index("col")
    half = rows // 2
    half_bit = half.bit_length() - 1
    sources = cols // rows
    local_rows, child_width = front_diag.shape[0], contrib.shape[1]
    row_slots = local_rows // BLK
    tile_cols = NF // cols
    child_slots = child_width // BLK
    child_rows = contrib.shape[0] // BLK
    row_half = child_rows // 2
    child_blocks, pivot_count = child_map.shape[1], pivots.shape[0]
    depth = pivot_count * BLK
    width = min(4, child_slots)
    steps, where = spread_plan(rows, cols)
    turns = np.argsort(where, axis=0, kind="stable").astype(np.int32)
    early = set(np.take_along_axis(where, turns[:1], 0).ravel()) - {0}
    order = None
    if len(steps) > 2 * sources:
        order, where = fold_plan(where)
    held_count = int(where.max()) + 1
    info = Meta(child_blocks, pivot_count, sources)
    meta = info.pack(child_map, pivots, r, q, where, turns)
    f32, bf16 = jnp.float32, jnp.bfloat16
    shape = jax.ShapeDtypeStruct

    lower_count = pivot_count * (pivot_count + 1) // 2
    panel, pivot_part = pl.pallas_call(
        functools.partial(pick_kernel, info, rows, cols),
        grid_spec=pltpu.PrefetchScalarGridSpec(
            num_scalar_prefetch=1,
            grid=(pivot_count,),
            in_specs=[
                pl.BlockSpec(
                    (1, BLK, child_width), lambda p, m: (info.pivot(m, p) % child_blocks // half, 0, 0)
                ),
                pl.BlockSpec((1, 1, BLK), lambda p, m: (info.pivot(m, p) // rows, 0, 0)),
            ],
            out_specs=[
                pl.BlockSpec((1, BLK, child_width), lambda p, m: (p, 0, 0)),
                pl.BlockSpec((lower_count, BLK, BLK), lambda p, m: (0, 0, 0)),
            ],
        ),
        out_shape=[
            shape((pivot_count, BLK, child_width), f32),
            shape((lower_count, BLK, BLK), f32),
        ],
        compiler_params=params(1),
        name="pick",
        cost_estimate=about(5),
    )(meta, contrib.reshape(child_rows, BLK, child_width), front_diag.reshape(row_slots, 1, BLK))
    own = panel.reshape(depth, child_width)
    for bit in range(half_bit):
        own = own + swapped(own, "row", bit)
    other = swapped(own, "row", half_bit)

    def folded(held):
        if order is None:
            return held
        mine_order = jnp.asarray(order)[:, r, q]
        merged = [held[0]]
        for n in range(held_count - 1):
            merged.append(sum(jnp.where(mine_order[k] == n, held[k], 0.0) for k in range(1, len(held))))
        return merged

    pivot_blocks = pivot_part
    for bit in range(cols.bit_length() - 1):
        across = swapped(pivot_blocks, "col", bit)
        pivot_blocks = pivot_blocks + across
    pivot_blocks = gated(pivot_blocks, other)
    for bit in range(half_bit, -1, -1):
        pivot_blocks = pivot_blocks + swapped(pivot_blocks, "row", bit)

    both = jnp.concatenate([own, other]) * one_after(across).astype(f32)
    halves = HALVES if child_slots // ROWS_AT_ONCE % HALVES == 0 and order is None else 1
    held = [[both]]
    for n, (buffer, pairs) in enumerate(steps):
        sent = held[buffer][0]
        if n + 1 not in early:
            sent = jnp.split(sent, halves, axis=1)
        else:
            sent = [sent]
        held.append([lax.ppermute(part, ("row", "col"), pairs) for part in sent])
    meanwhile = [part for n in early for part in held[n]]
    if order is not None:
        held = [[part] for part in folded([parts[0] for parts in held])]

    lower, inverse, inverse_t = pl.pallas_call(
        functools.partial(cholesky_kernel, pivot_count),
        out_shape=[shape((depth, depth), f32)] * 3,
        scratch_shapes=[pltpu.VMEM((BLK, 2 * BLK), f32), pltpu.VMEM((lower_count, BLK, BLK), f32)],
        compiler_params=params(0),
        name="factor_pivots",
        cost_estimate=about(59),
    )(pivot_blocks)

    own_view = contrib.reshape(child_slots, sources, 2, BLK, child_width)
    mine = r // half
    partner_turns = jnp.asarray(turns)[:, r ^ half, q]
    received = []
    for turn in range(sources):
        chunks = (child_slots,)
        if turn > 0 and sum(CHUNKS) == child_slots:
            chunks = CHUNKS
        first = 0
        for chunk in chunks:
            if not received:
                start = one_after(pivot_blocks)
            elif len(received) == 1:
                start = one_after(inverse)
            else:
                start = one_after(*[part for _, _, part in received[:-1]])
            part = lax.dynamic_slice(
                own_view,
                (first, partner_turns[turn] * start, 1 - mine, 0, 0),
                (chunk, 1, 1, BLK, child_width),
            ).reshape(chunk, BLK, child_width)
            received.append((turn, first, swapped(part, "row", half_bit)))
            first += chunk
    meanwhile.append(received[0][2])

    lanes = width * BLK
    groups = child_slots // width
    whole = lambda *_: (0, 0)
    untouched = pl.BlockSpec(memory_space=pl.ANY)
    col_parts = pl.pallas_call(
        functools.partial(columns_kernel, info, rows, cols, child_slots, width),
        grid_spec=pltpu.PrefetchScalarGridSpec(
            num_scalar_prefetch=1,
            grid=(2, groups),
            in_specs=[
                pl.BlockSpec((depth, lanes), lambda v, g, m: (0, g)),
                pl.BlockSpec((depth, lanes), lambda v, g, m: (0, g)),
                pl.BlockSpec((depth, depth), whole),
            ]
            + [untouched] * len(meanwhile),
            out_specs=pl.BlockSpec((3 * depth, lanes), lambda v, g, m: (0, v * groups + g)),
        ),
        out_shape=shape((3 * depth, tile_cols), bf16),
        compiler_params=params(2),
        name="factor_at_columns",
        cost_estimate=about(10),
    )(meta, own, other, inverse, *meanwhile)

    share = depth // cols
    factor = None
    tile = token = None
    diag_view = front_diag.reshape(2, child_slots, sources, 1, BLK)
    mine_of = lambda m: info.row(m) // half
    square = pl.BlockSpec((depth, depth), whole)
    few = min(2, width)
    counts = [1] + [halves] * (sources - 1)
    row_parts = [[] for _ in counts]

    order_of_work = [("rows", 0, 0), ("rows", 1, 0), ("tile", 0)]
    order_of_work += [("rows", turn, n) for turn in range(1, sources) for n in range(counts[turn]) if (turn, n) != (1, 0)]
    order_of_work += [("tile", turn) for turn in range(1, sources)]
    for work, turn, *rest in order_of_work:
        parts_count = counts[turn]
        if work == "rows":
            (at_half,) = rest
            used = sorted({int(n) for n in np.take_along_axis(where, turns[turn : turn + 1], 0).ravel()})
            steps_here = child_slots // few // parts_count
            first = at_half * steps_here

            def piece(n, turn=turn, first=first, at_half=at_half):
                base = first if len(held[n]) == 1 else 0
                return held[n][-1 if base else min(at_half, len(held[n]) - 1)], pl.BlockSpec(
                    (2 * depth, few * BLK),
                    lambda g, m: (0, jnp.where(info.held(m, info.source(m, turn)) == n, base + g, 0)),
                )

            operands = [piece(n)[0] for n in used] + [lower, inverse_t]
            in_specs = [piece(n)[1] for n in used] + [square, square]
            if factor is None:
                factor, aliases = jnp.zeros((2, 1, sources, BLK, BLK), f32), {}
            else:
                aliases = {len(operands) + 1: 0}
            operands += [factor, meta if token is None else token]
            in_specs += [untouched] * 2
            factor, row_part = pl.pallas_call(
                functools.partial(rows_kernel, info, rows, cols, few, share, turn, first, used),
                grid_spec=pltpu.PrefetchScalarGridSpec(
                    num_scalar_prefetch=1,
                    grid=(steps_here,),
                    in_specs=in_specs,
                    out_specs=[
                        pl.BlockSpec(
                            (2, few, 1, BLK, BLK),
                            lambda g, m, turn=turn, first=first: (0, first + g, info.source(m, turn), 0, 0),
                        ),
                        pl.BlockSpec((2, few, BLK, 3 * depth), lambda g, m: (0, g, 0, 0)),
                    ],
                    scratch_shapes=[pltpu.VMEM((BLK, depth), f32)],
                ),
                out_shape=[
                    shape((2, child_slots, sources, BLK, BLK), f32),
                    shape((2, child_slots // parts_count, BLK, 3 * depth), bf16),
                ],
                input_output_aliases=aliases,
                compiler_params=params(1, 40),
                name="factor_rows",
                cost_estimate=about(3.0 * steps_here * (LATE if turn else 1.0)),
            )(meta, *operands)
            row_parts[turn].append(row_part)
            continue

        for first, part in [(first, part) for at_turn, first, part in received if at_turn == turn]:
            at = first // ROWS_AT_ONCE
            row_part = row_parts[turn][first * parts_count // child_slots]
            left_at = at % (child_slots // parts_count // ROWS_AT_ONCE)
            source_of = functools.partial(info.source, turn=turn)
            in_specs = [
                pl.BlockSpec(
                    (ROWS_AT_ONCE, 1, 1, BLK, child_width),
                    lambda t, v, m, at=at, source_of=source_of: (at + t, source_of(m), mine_of(m), 0, 0),
                ),
                pl.BlockSpec((ROWS_AT_ONCE, BLK, child_width), lambda t, v, m: (t, 0, 0)),
                pl.BlockSpec((2, ROWS_AT_ONCE, BLK, 3 * depth), lambda t, v, m, at=left_at: (0, at + t, 0, 0)),
                pl.BlockSpec((3 * depth, tile_cols), whole),
                pl.BlockSpec(
                    (2, ROWS_AT_ONCE, 1, 1, BLK),
                    lambda t, v, m, at=at, source_of=source_of: (0, at + t, source_of(m), 0, 0),
                ),
            ]
            operands = [own_view, part, row_part, col_parts, diag_view]
            aliases = {}
            if tile is None:
                in_specs.append(untouched)
                operands.append(row_parts[1][0])
            else:
                in_specs.append(untouched)
                operands.append(tile)
                aliases = {len(operands): 0}
            tile, token = pl.pallas_call(
                functools.partial(update_kernel, info, rows, cols, child_slots, width, turn, first),
                grid_spec=pltpu.PrefetchScalarGridSpec(
                    num_scalar_prefetch=1,
                    grid=(part.shape[0] // ROWS_AT_ONCE, 2),
                    in_specs=in_specs,
                    out_specs=[
                        pl.BlockSpec(
                            (2, ROWS_AT_ONCE, 1, BLK, child_width),
                            lambda t, v, m, at=at, source_of=source_of: (0, at + t, source_of(m), 0, v),
                        ),
                        pl.BlockSpec((8, BLK), lambda t, v, m: (0, 0)),
                    ],
                ),
                out_shape=[shape((2, child_slots, sources, BLK, tile_cols), f32), shape((8, BLK), f32)],
                input_output_aliases=aliases,
                compiler_params=params(2, 36),
                name="update_tile",
                cost_estimate=about(3.0 * part.shape[0] * (LATE if turn else 1.0)),
            )(meta, *operands)
    factor = factor.reshape(local_rows, BLK)
    if share < BLK:
        factor = lax.dynamic_slice_in_dim(factor, q * share % BLK, share, 1)

    return factor, tile.reshape(local_rows, tile_cols)


def solution(mesh):
    placed = (P(("front", "row"), "col"), P(("front", "row")), P("front", None), P("front"))
    return jax.shard_map(
        per_device,
        mesh=mesh,
        in_specs=placed,
        out_specs=(P(("front", "row"), "col"), P(("front", "row"), "col")),
        check_vma=False,
    )
```

```python
import functools

import jax
import jax.numpy as jnp
import numpy as np
from jax import lax
from jax.experimental import pallas as pl
from jax.experimental.pallas import tpu as pltpu
from jax.sharding import PartitionSpec as P

NF = 8192
BLK = 128
HALVES = 2
ORDER = 1
B0 = 1
GATE3 = 0
MAGNET = 50
BOTH = 0
CHUNKS = (4, 4)
ROWS_AT_ONCE = 2
PACE = 1.0
LATE = 1.0

highest = lax.Precision.HIGHEST


def swapped(shard, axis, bit):
    return lax.ppermute(shard, axis, [(i, i ^ 1 << bit) for i in range(lax.axis_size(axis))])


def one_after(*arrays):
    first = [array[(0,) * array.ndim] for array in arrays]
    there = functools.reduce(jnp.logical_and, [value == value for value in first])
    return jnp.where(there, 1, 0)


def gated(value, *arrays):
    return value * one_after(*arrays).astype(value.dtype)


def spread_plan(rows, cols):
    sources = cols // rows
    where = -np.ones((sources, rows, cols), np.int32)
    for r in range(rows):
        for s in range(sources):
            where[s, r, r + s * rows] = 0
    steps = []
    while (where < 0).any():
        for buffer in range(len(steps) + 1):
            moves = []
            for r in range(rows):
                sign = 1 if r <= cols - 1 - (r + (sources - 1) * rows) else -1
                taken = set()
                for h in range(cols)[::-sign]:
                    for s in range(sources):
                        if where[s, r, h] != buffer:
                            continue
                        open_to = [
                            d for d in range(cols)
                            if where[s, r, d] < 0 and d not in taken and abs(d - h) <= rows
                        ]
                        if open_to:
                            d = max(open_to, key=lambda d: sign * (d - h))
                            taken.add(d)
                            moves.append((s, r, h, d))
            if moves:
                break
        steps.append((buffer, [(r * cols + h, r * cols + d) for _, r, h, d in moves]))
        for s, r, _, d in moves:
            where[s, r, d] = len(steps)
    return steps, where


def fold_plan(where):
    sources, rows, cols = where.shape
    steps = where.max()
    order = -np.ones((steps + 1, rows, cols), np.int32)
    folded = np.zeros_like(where)
    for r in range(rows):
        for d in range(cols):
            got = sorted((where[s, r, d], s) for s in range(sources) if where[s, r, d] > 0)
            for n, (step, s) in enumerate(got):
                order[step, r, d] = n
                folded[s, r, d] = n + 1
    return order, folded


class Meta:
    def __init__(self, child_blocks, pivot_count, sources):
        self.child_blocks, self.pivot_count, self.sources = child_blocks, pivot_count, sources

    def pack(self, child_map, pivots, row_index, col_index, where, turns):
        place = jnp.stack([row_index, col_index]).astype(jnp.int32)
        held = jnp.asarray(np.concatenate([where, turns]))[:, row_index, col_index]
        return jnp.concatenate([child_map.reshape(-1), pivots, place, held])

    def has(self, meta, child, block, front_block):
        return meta[child * self.child_blocks + block] == front_block

    def pivot(self, meta, p):
        return meta[2 * self.child_blocks + p]

    def row(self, meta):
        return meta[2 * self.child_blocks + self.pivot_count]

    def col(self, meta):
        return meta[2 * self.child_blocks + self.pivot_count + 1]

    def held(self, meta, s):
        return meta[2 * self.child_blocks + self.pivot_count + 2 + s]

    def source(self, meta, turn):
        return self.held(meta, self.sources + turn)

    def is_pivot(self, meta, front_block):
        hit = front_block == self.pivot(meta, 0)
        for p in range(1, self.pivot_count):
            hit = jnp.logical_or(hit, front_block == self.pivot(meta, p))
        return hit


def as_float(flag):
    return jnp.where(flag, 1.0, 0.0).astype(jnp.float32)


def eye_mask():
    return lax.broadcasted_iota(jnp.int32, (BLK, BLK), 0) == lax.broadcasted_iota(jnp.int32, (BLK, BLK), 1)


def split(value):
    high = value.astype(jnp.bfloat16)
    return high, (value - high.astype(jnp.float32)).astype(jnp.bfloat16)


def dot_t(a, b):
    return lax.dot_general(
        a, b, (((1,), (1,)), ((), ())), precision=highest, preferred_element_type=jnp.float32
    )


def dot(a, b):
    return jnp.dot(a, b, precision=highest, preferred_element_type=jnp.float32)


def pick_kernel(info, rows, cols, meta, child, diag, panel, pivot_part):
    half = rows // 2
    r, q = info.row(meta), info.col(meta)
    mine, within = r // half, r % half
    p = pl.program_id(0)
    front_block = info.pivot(meta, p)
    block = front_block % info.child_blocks
    present = jnp.logical_and(info.has(meta, mine, block, front_block), block % half == within)
    panel[0] = child[0] * as_float(present)
    first = p * (p + 1) // 2
    for t in range(info.pivot_count):
        other = info.pivot(meta, t)
        other_block = other % info.child_blocks
        here = jnp.logical_and(info.has(meta, mine, other_block, other), other_block % cols == q)

        @pl.when(t <= p)
        def _():
            at = pl.multiple_of(other_block // cols * BLK, BLK)
            pivot_part[first + t] = panel[0, :, pl.ds(at, BLK)] * as_float(here)

    on_diagonal = jnp.logical_and(front_block % rows == r, front_block % cols == q)

    @pl.when(on_diagonal)
    def _():
        pivot_part[first + p] += jnp.where(eye_mask(), diag[0], 0.0)


def cholesky_kernel(count, blocks, lower, inverse, inverse_t, work, rest):
    at = lambda i, j: i * (i + 1) // 2 + j
    span = lambda i: slice(i * BLK, (i + 1) * BLK)
    lower[...] = jnp.zeros_like(lower)
    inverse[...] = jnp.zeros_like(inverse)
    rest[...] = blocks[...]
    row_ids = lax.broadcasted_iota(jnp.int32, (BLK, BLK), 0)
    col_ids = lax.broadcasted_iota(jnp.int32, (BLK, BLK), 1)
    wide_ids = lax.broadcasted_iota(jnp.int32, (1, 2 * BLK), 1)
    column_ids = lax.broadcasted_iota(jnp.int32, (BLK, 1), 0)
    for p in range(count):
        work[:, :BLK] = rest[at(p, p)]
        work[:, BLK:] = jnp.where(row_ids == col_ids, 1.0, 0.0)

        def eliminate(j, carry):
            row = work[pl.ds(j, 1), :]
            lead = jnp.sum(jnp.where(wide_ids == j, row, 0.0), axis=1, keepdims=True)
            left = work[:, :BLK]
            column = jnp.sum(jnp.where(col_ids == j, left, 0.0), axis=1, keepdims=True)
            column = jnp.where(column_ids > j, column, 0.0)
            scaled = row / lead
            work[...] = work[...] - column * scaled
            return carry

        lax.fori_loop(0, BLK, eliminate, 0)
        left = work[:, :BLK]
        lead = jnp.sum(jnp.where(row_ids == col_ids, left, 0.0), axis=1, keepdims=True)
        scale = 1.0 / jnp.sqrt(lead)
        lower[span(p), span(p)] = jnp.where(row_ids <= col_ids, left * scale, 0.0).T
        inverse[span(p), span(p)] = work[:, BLK:] * scale
        own_inverse = inverse[span(p), span(p)]
        for i in range(p + 1, count):
            lower[span(i), span(p)] = dot_t(rest[at(i, p)], own_inverse)
        for i in range(p + 1, count):
            for k in range(p + 1, i + 1):
                rest[at(i, k)] -= dot_t(lower[span(i), span(p)], lower[span(k), span(p)])
    for i in range(1, count):
        for j in range(i):
            known = slice(j * BLK, i * BLK)
            partial = dot(lower[span(i), known], inverse[known, span(j)])
            inverse[span(i), span(j)] = -dot(inverse[span(i), span(i)], partial)
    inverse_t[...] = inverse[...].T


def columns_kernel(info, rows, cols, child_slots, width, meta, own, other, inverse, *refs):
    stacked = refs[-1]
    r, q = info.row(meta), info.col(meta)
    mine = r // (rows // 2)
    v, step = pl.program_id(0), pl.program_id(1)
    parts = []
    for i in range(width):
        block = (step * width + i) * cols + q
        front_block = block + v * info.child_blocks
        keep = jnp.logical_not(info.is_pivot(meta, front_block))
        lanes = slice(i * BLK, (i + 1) * BLK)
        take = as_float(jnp.logical_and(keep, info.has(meta, mine, block, front_block)))
        take_other = as_float(jnp.logical_and(keep, info.has(meta, 1 - mine, block, front_block)))
        parts.append(own[:, lanes] * take + other[:, lanes] * take_other)
    high, low = split(dot(inverse[...], jnp.concatenate(parts, axis=1)))
    depth = high.shape[0]
    stacked[:depth], stacked[depth : 2 * depth], stacked[2 * depth :] = high, high, low


def chosen(holder, used, pieces):
    value = pieces[0][...]
    for n, piece in zip(used[1:], pieces[1:]):
        value = jnp.where(holder == n, piece[...], value)
    return value


def rows_kernel(info, rows, cols, width, share, turn, first, used, meta, *refs):
    r, q = info.row(meta), info.col(meta)
    mine = r // (rows // 2)
    s, step = info.source(meta, turn), pl.program_id(0) + first
    lower, inverse_t = refs[len(used) :][:2]
    factor, parts, work = refs[-3:]
    piece = chosen(info.held(meta, s), used, refs[: len(used)])
    half_depth = piece.shape[0] // 2
    own_value = dot(piece[:half_depth].T, inverse_t[...])
    other_value = dot(piece[half_depth:].T, inverse_t[...])
    at = pl.multiple_of(q * share // BLK * BLK, BLK)
    depth = lower.shape[0]
    for i in range(width):
        block = (step * width + i) * cols + r + s * rows
        span = slice(i * BLK, (i + 1) * BLK)
        for v in range(2):
            front_block = block + v * info.child_blocks
            take = as_float(info.has(meta, mine, block, front_block))
            take_other = as_float(info.has(meta, 1 - mine, block, front_block))
            value = own_value[span, :] * take + other_value[span, :] * take_other
            high, low = split(value)
            parts[v, i, :, :depth], parts[v, i, :, depth : 2 * depth], parts[v, i, :, 2 * depth :] = high, low, high
            work[...] = value
            factor[v, i, 0] = work[:, pl.ds(at, BLK)]
            for p in range(info.pivot_count):

                @pl.when(front_block == info.pivot(meta, p))
                def _():
                    factor[v, i, 0] = lower[p * BLK : (p + 1) * BLK, pl.ds(at, BLK)]
                    parts[v, i] = jnp.zeros_like(parts[v, i])


def update_kernel(info, rows, cols, child_slots, width, turn, first, meta, *refs):
    own, other, left, right, diag = refs[:5]
    tile, token = refs[-2:]
    token[...] = jnp.zeros_like(token)
    r, q = info.row(meta), info.col(meta)
    mine = r // (rows // 2)
    step, v = pl.program_id(0), pl.program_id(1)
    left_rows = left[...].reshape(2 * ROWS_AT_ONCE * BLK, left.shape[-1])

    def takes(block, front_block):
        keep = jnp.logical_not(info.is_pivot(meta, front_block))
        return [as_float(jnp.logical_and(keep, info.has(meta, c, block, front_block))) for c in (mine, 1 - mine)]

    def row_block(j):
        return (first + step * ROWS_AT_ONCE + j) * cols + info.source(meta, turn) * rows + r

    row_takes = {
        (u, j): takes(row_block(j), row_block(j) + u * info.child_blocks)
        for u in range(2)
        for j in range(ROWS_AT_ONCE)
    }
    for start in range(0, child_slots, width):
        at = pl.multiple_of((v * child_slots + start) * BLK, BLK)
        change = jnp.dot(left_rows, right[:, pl.ds(at, width * BLK)], preferred_element_type=jnp.float32)
        for i in range(width):
            block = (start + i) * cols + q
            col_takes = takes(block, block + v * info.child_blocks)
            lanes = slice((start + i) * BLK, (start + i + 1) * BLK)
            for (u, j), row_take in row_takes.items():
                n = u * ROWS_AT_ONCE + j
                tile[u, j, 0, :, lanes] = (
                    own[j, 0, 0, :, lanes] * (row_take[0] * col_takes[0])
                    + other[j, :, lanes] * (row_take[1] * col_takes[1])
                    - change[n * BLK : (n + 1) * BLK, i * BLK : (i + 1) * BLK]
                )
    for u in range(2):
        for j in range(ROWS_AT_ONCE):
            front_block = row_block(j) + u * info.child_blocks
            slot = front_block // cols
            here = jnp.logical_and(front_block % cols == q, slot // child_slots == v)

            @pl.when(jnp.logical_and(here, jnp.logical_not(info.is_pivot(meta, front_block))))
            def _():
                at = pl.multiple_of(slot % child_slots * BLK, BLK)
                tile[u, j, 0, :, pl.ds(at, BLK)] += jnp.where(eye_mask(), diag[u, j, 0], 0.0)


def params(grid_size, mib=32):
    return pltpu.CompilerParams(
        dimension_semantics=("arbitrary",) * grid_size, vmem_limit_bytes=mib * 1024 * 1024
    )


def about(micros):
    micros *= PACE
    return pl.CostEstimate(flops=int(micros * 1.15e9), bytes_accessed=int(micros * 3.69e6), transcendentals=0)


def pause_kernel(*refs):
    refs[-1][...] = jnp.ones_like(refs[-1])


def pause(micros, *after):
    ones = pl.pallas_call(
        pause_kernel,
        in_specs=[pl.BlockSpec(memory_space=pl.ANY)] * len(after),
        out_shape=jax.ShapeDtypeStruct((8, BLK), jnp.float32),
        cost_estimate=about(micros),
        name="pause",
    )(*after)
    return ones[0, 0]


def per_device(contrib, front_diag, child_map, pivots):
    rows, cols = lax.axis_size("row"), lax.axis_size("col")
    r, q = lax.axis_index("row"), lax.axis_index("col")
    half = rows // 2
    half_bit = half.bit_length() - 1
    sources = cols // rows
    local_rows, child_width = front_diag.shape[0], contrib.shape[1]
    row_slots = local_rows // BLK
    tile_cols = NF // cols
    child_slots = child_width // BLK
    child_rows = contrib.shape[0] // BLK
    row_half = child_rows // 2
    child_blocks, pivot_count = child_map.shape[1], pivots.shape[0]
    depth = pivot_count * BLK
    width = min(4, child_slots)
    steps, where = spread_plan(rows, cols)
    turns = np.argsort(where, axis=0, kind="stable").astype(np.int32)
    early = set(np.take_along_axis(where, turns[:1], 0).ravel()) - {0}
    order = None
    if len(steps) > 2 * sources:
        order, where = fold_plan(where)
    held_count = int(where.max()) + 1
    info = Meta(child_blocks, pivot_count, sources)
    meta = info.pack(child_map, pivots, r, q, where, turns)
    f32, bf16 = jnp.float32, jnp.bfloat16
    shape = jax.ShapeDtypeStruct

    lower_count = pivot_count * (pivot_count + 1) // 2
    panel, pivot_part = pl.pallas_call(
        functools.partial(pick_kernel, info, rows, cols),
        grid_spec=pltpu.PrefetchScalarGridSpec(
            num_scalar_prefetch=1,
            grid=(pivot_count,),
            in_specs=[
                pl.BlockSpec(
                    (1, BLK, child_width), lambda p, m: (info.pivot(m, p) % child_blocks // half, 0, 0)
                ),
                pl.BlockSpec((1, 1, BLK), lambda p, m: (info.pivot(m, p) // rows, 0, 0)),
            ],
            out_specs=[
                pl.BlockSpec((1, BLK, child_width), lambda p, m: (p, 0, 0)),
                pl.BlockSpec((lower_count, BLK, BLK), lambda p, m: (0, 0, 0)),
            ],
        ),
        out_shape=[
            shape((pivot_count, BLK, child_width), f32),
            shape((lower_count, BLK, BLK), f32),
        ],
        compiler_params=params(1),
        name="pick",
        cost_estimate=about(5),
    )(meta, contrib.reshape(child_rows, BLK, child_width), front_diag.reshape(row_slots, 1, BLK))
    own = panel.reshape(depth, child_width)
    for bit in range(half_bit):
        own = own + swapped(own, "row", bit)
    other = swapped(own, "row", half_bit)

    def folded(held):
        if order is None:
            return held
        mine_order = jnp.asarray(order)[:, r, q]
        merged = [held[0]]
        for n in range(held_count - 1):
            merged.append(sum(jnp.where(mine_order[k] == n, held[k], 0.0) for k in range(1, len(held))))
        return merged

    pivot_blocks = pivot_part
    for bit in range(cols.bit_length() - 1):
        across = swapped(pivot_blocks, "col", bit)
        pivot_blocks = pivot_blocks + across
    pivot_blocks = gated(pivot_blocks, other)
    behind = pause(50, across, other).astype(jnp.int32) if B0 == 3 else None
    for bit in range(half_bit, -1, -1):
        pivot_blocks = pivot_blocks + swapped(pivot_blocks, "row", bit)

    both = jnp.concatenate([own, other]) * one_after([across, other, pivot_blocks][BOTH]).astype(f32)
    halves = HALVES if child_slots // ROWS_AT_ONCE % HALVES == 0 and order is None else 1
    held = [[both]]
    for n, (buffer, pairs) in enumerate(steps):
        sent = held[buffer][0]
        if n + 1 not in early:
            sent = jnp.split(sent, halves, axis=1)
        else:
            sent = [sent]
        held.append([lax.ppermute(part, ("row", "col"), pairs) for part in sent])
    meanwhile = [part for n in early for part in held[n]]
    if order is not None:
        held = [[part] for part in folded([parts[0] for parts in held])]

    lower, inverse, inverse_t = pl.pallas_call(
        functools.partial(cholesky_kernel, pivot_count),
        out_shape=[shape((depth, depth), f32)] * 3,
        scratch_shapes=[pltpu.VMEM((BLK, 2 * BLK), f32), pltpu.VMEM((lower_count, BLK, BLK), f32)],
        compiler_params=params(0),
        name="factor_pivots",
        cost_estimate=about(59),
    )(pivot_blocks)

    own_view = contrib.reshape(child_slots, sources, 2, BLK, child_width)
    mine = r // half
    partner_turns = jnp.asarray(turns)[:, r ^ half, q]
    received = []
    for turn in range(sources):
        chunks = (child_slots,)
        if turn > 0 and sum(CHUNKS) == child_slots:
            chunks = CHUNKS
        first = 0
        for chunk in chunks:
            if not received:
                start = behind if B0 == 3 else one_after([pivot_blocks, other, across][B0])
            elif len(received) == 1:
                start = one_after(inverse)
            else:
                start = one_after(inverse) if len(received) == 1 else pause(MAGNET, inverse, part).astype(jnp.int32)
            part = lax.dynamic_slice(
                own_view,
                (first, partner_turns[turn] * start, 1 - mine, 0, 0),
                (chunk, 1, 1, BLK, child_width),
            ).reshape(chunk, BLK, child_width)
            received.append((turn, first, swapped(part, "row", half_bit)))
            first += chunk
    meanwhile.append(received[0][2])

    lanes = width * BLK
    groups = child_slots // width
    whole = lambda *_: (0, 0)
    untouched = pl.BlockSpec(memory_space=pl.ANY)
    col_parts = pl.pallas_call(
        functools.partial(columns_kernel, info, rows, cols, child_slots, width),
        grid_spec=pltpu.PrefetchScalarGridSpec(
            num_scalar_prefetch=1,
            grid=(2, groups),
            in_specs=[
                pl.BlockSpec((depth, lanes), lambda v, g, m: (0, g)),
                pl.BlockSpec((depth, lanes), lambda v, g, m: (0, g)),
                pl.BlockSpec((depth, depth), whole),
            ]
            + [untouched] * len(meanwhile),
            out_specs=pl.BlockSpec((3 * depth, lanes), lambda v, g, m: (0, v * groups + g)),
        ),
        out_shape=shape((3 * depth, tile_cols), bf16),
        compiler_params=params(2),
        name="factor_at_columns",
        cost_estimate=about(10),
    )(meta, own, other, inverse, *meanwhile)

    share = depth // cols
    factor = None
    tile = token = None
    diag_view = front_diag.reshape(2, child_slots, sources, 1, BLK)
    mine_of = lambda m: info.row(m) // half
    square = pl.BlockSpec((depth, depth), whole)
    few = min(2, width)
    counts = [1] + [halves] * (sources - 1)
    row_parts = [[] for _ in counts]

    order_of_work = [("rows", 0, 0), ("rows", 1, 0), ("tile", 0)]
    chunks_of = [[(first, part) for at_turn, first, part in received if at_turn == turn] for turn in range(sources)]
    order_of_work = [("rows", 0, 0), ("rows", 1, 0), ("tile", 0, 0)]
    for turn in range(1, sources):
        ahead = len(chunks_of[turn]) // 2 if counts[turn] == 2 and ORDER else 0
        order_of_work += [("tile", turn, n) for n in range(ahead)]
        order_of_work += [("rows", turn, n) for n in range(counts[turn]) if (turn, n) != (1, 0)]
        order_of_work += [("tile", turn, n) for n in range(ahead, len(chunks_of[turn]))]
    for work, turn, *rest in order_of_work:
        parts_count = counts[turn]
        if work == "rows":
            (at_half,) = rest
            used = sorted({int(n) for n in np.take_along_axis(where, turns[turn : turn + 1], 0).ravel()})
            steps_here = child_slots // few // parts_count
            first = at_half * steps_here

            def piece(n, turn=turn, first=first, at_half=at_half):
                base = first if len(held[n]) == 1 else 0
                return held[n][-1 if base else min(at_half, len(held[n]) - 1)], pl.BlockSpec(
                    (2 * depth, few * BLK),
                    lambda g, m: (0, jnp.where(info.held(m, info.source(m, turn)) == n, base + g, 0)),
                )

            operands = [piece(n)[0] for n in used] + [lower, inverse_t]
            in_specs = [piece(n)[1] for n in used] + [square, square]
            if factor is None:
                factor, aliases = jnp.zeros((2, 1, sources, BLK, BLK), f32), {}
            else:
                aliases = {len(operands) + 1: 0}
            operands += [factor, [meta, received[0][2]][GATE3] if token is None else token]
            in_specs += [untouched] * 2
            factor, row_part = pl.pallas_call(
                functools.partial(rows_kernel, info, rows, cols, few, share, turn, first, used),
                grid_spec=pltpu.PrefetchScalarGridSpec(
                    num_scalar_prefetch=1,
                    grid=(steps_here,),
                    in_specs=in_specs,
                    out_specs=[
                        pl.BlockSpec(
                            (2, few, 1, BLK, BLK),
                            lambda g, m, turn=turn, first=first: (0, first + g, info.source(m, turn), 0, 0),
                        ),
                        pl.BlockSpec((2, few, BLK, 3 * depth), lambda g, m: (0, g, 0, 0)),
                    ],
                    scratch_shapes=[pltpu.VMEM((BLK, depth), f32)],
                ),
                out_shape=[
                    shape((2, child_slots, sources, BLK, BLK), f32),
                    shape((2, child_slots // parts_count, BLK, 3 * depth), bf16),
                ],
                input_output_aliases=aliases,
                compiler_params=params(1, 40),
                name="factor_rows",
                cost_estimate=about(3.0 * steps_here * (LATE if turn else 1.0)),
            )(meta, *operands)
            row_parts[turn].append(row_part)
            continue

        for first, part in [chunks_of[turn][rest[0]]]:
            at = first // ROWS_AT_ONCE
            row_part = row_parts[turn][first * parts_count // child_slots]
            left_at = at % (child_slots // parts_count // ROWS_AT_ONCE)
            source_of = functools.partial(info.source, turn=turn)
            in_specs = [
                pl.BlockSpec(
                    (ROWS_AT_ONCE, 1, 1, BLK, child_width),
                    lambda t, v, m, at=at, source_of=source_of: (at + t, source_of(m), mine_of(m), 0, 0),
                ),
                pl.BlockSpec((ROWS_AT_ONCE, BLK, child_width), lambda t, v, m: (t, 0, 0)),
                pl.BlockSpec((2, ROWS_AT_ONCE, BLK, 3 * depth), lambda t, v, m, at=left_at: (0, at + t, 0, 0)),
                pl.BlockSpec((3 * depth, tile_cols), whole),
                pl.BlockSpec(
                    (2, ROWS_AT_ONCE, 1, 1, BLK),
                    lambda t, v, m, at=at, source_of=source_of: (0, at + t, source_of(m), 0, 0),
                ),
            ]
            operands = [own_view, part, row_part, col_parts, diag_view]
            aliases = {}
            if tile is None:
                in_specs.append(untouched)
                operands.append(row_parts[1][0])
            else:
                in_specs.append(untouched)
                operands.append(tile)
                aliases = {len(operands): 0}
            tile, token = pl.pallas_call(
                functools.partial(update_kernel, info, rows, cols, child_slots, width, turn, first),
                grid_spec=pltpu.PrefetchScalarGridSpec(
                    num_scalar_prefetch=1,
                    grid=(part.shape[0] // ROWS_AT_ONCE, 2),
                    in_specs=in_specs,
                    out_specs=[
                        pl.BlockSpec(
                            (2, ROWS_AT_ONCE, 1, BLK, child_width),
                            lambda t, v, m, at=at, source_of=source_of: (0, at + t, source_of(m), 0, v),
                        ),
                        pl.BlockSpec((8, BLK), lambda t, v, m: (0, 0)),
                    ],
                ),
                out_shape=[shape((2, child_slots, sources, BLK, tile_cols), f32), shape((8, BLK), f32)],
                input_output_aliases=aliases,
                compiler_params=params(2, 36),
                name="update_tile",
                cost_estimate=about(3.0 * part.shape[0] * (LATE if turn else 1.0)),
            )(meta, *operands)
    factor = factor.reshape(local_rows, BLK)
    if share < BLK:
        factor = lax.dynamic_slice_in_dim(factor, q * share % BLK, share, 1)

    return factor, tile.reshape(local_rows, tile_cols)


def solution(mesh):
    placed = (P(("front", "row"), "col"), P(("front", "row")), P("front", None), P("front"))
    return jax.shard_map(
        per_device,
        mesh=mesh,
        in_specs=placed,
        out_specs=(P(("front", "row"), "col"), P(("front", "row"), "col")),
        check_vma=False,
    )
```

```python
import functools

import jax
import jax.numpy as jnp
import numpy as np
from jax import lax
from jax.experimental import pallas as pl
from jax.experimental.pallas import tpu as pltpu
from jax.sharding import PartitionSpec as P

NF = 8192
BLK = 128
HALVES = 2
ORDER = 1
B0 = 3
GATE3 = 0
MAGNET = 50
G5 = 0
G6 = 0
BOTH = 0
CHUNKS = (4, 4)
ROWS_AT_ONCE = 2
PACE = 1.0
LATE = 1.0

highest = lax.Precision.HIGHEST


def swapped(shard, axis, bit):
    return lax.ppermute(shard, axis, [(i, i ^ 1 << bit) for i in range(lax.axis_size(axis))])


def one_after(*arrays):
    first = [array[(0,) * array.ndim] for array in arrays]
    there = functools.reduce(jnp.logical_and, [value == value for value in first])
    return jnp.where(there, 1, 0)


def gated(value, *arrays):
    return value * one_after(*arrays).astype(value.dtype)


def spread_plan(rows, cols):
    sources = cols // rows
    where = -np.ones((sources, rows, cols), np.int32)
    for r in range(rows):
        for s in range(sources):
            where[s, r, r + s * rows] = 0
    steps = []
    while (where < 0).any():
        for buffer in range(len(steps) + 1):
            moves = []
            for r in range(rows):
                sign = 1 if r <= cols - 1 - (r + (sources - 1) * rows) else -1
                taken = set()
                for h in range(cols)[::-sign]:
                    for s in range(sources):
                        if where[s, r, h] != buffer:
                            continue
                        open_to = [
                            d for d in range(cols)
                            if where[s, r, d] < 0 and d not in taken and abs(d - h) <= rows
                        ]
                        if open_to:
                            d = max(open_to, key=lambda d: sign * (d - h))
                            taken.add(d)
                            moves.append((s, r, h, d))
            if moves:
                break
        steps.append((buffer, [(r * cols + h, r * cols + d) for _, r, h, d in moves]))
        for s, r, _, d in moves:
            where[s, r, d] = len(steps)
    return steps, where


def fold_plan(where):
    sources, rows, cols = where.shape
    steps = where.max()
    order = -np.ones((steps + 1, rows, cols), np.int32)
    folded = np.zeros_like(where)
    for r in range(rows):
        for d in range(cols):
            got = sorted((where[s, r, d], s) for s in range(sources) if where[s, r, d] > 0)
            for n, (step, s) in enumerate(got):
                order[step, r, d] = n
                folded[s, r, d] = n + 1
    return order, folded


class Meta:
    def __init__(self, child_blocks, pivot_count, sources):
        self.child_blocks, self.pivot_count, self.sources = child_blocks, pivot_count, sources

    def pack(self, child_map, pivots, row_index, col_index, where, turns):
        place = jnp.stack([row_index, col_index]).astype(jnp.int32)
        held = jnp.asarray(np.concatenate([where, turns]))[:, row_index, col_index]
        return jnp.concatenate([child_map.reshape(-1), pivots, place, held])

    def has(self, meta, child, block, front_block):
        return meta[child * self.child_blocks + block] == front_block

    def pivot(self, meta, p):
        return meta[2 * self.child_blocks + p]

    def row(self, meta):
        return meta[2 * self.child_blocks + self.pivot_count]

    def col(self, meta):
        return meta[2 * self.child_blocks + self.pivot_count + 1]

    def held(self, meta, s):
        return meta[2 * self.child_blocks + self.pivot_count + 2 + s]

    def source(self, meta, turn):
        return self.held(meta, self.sources + turn)

    def is_pivot(self, meta, front_block):
        hit = front_block == self.pivot(meta, 0)
        for p in range(1, self.pivot_count):
            hit = jnp.logical_or(hit, front_block == self.pivot(meta, p))
        return hit


def as_float(flag):
    return jnp.where(flag, 1.0, 0.0).astype(jnp.float32)


def eye_mask():
    return lax.broadcasted_iota(jnp.int32, (BLK, BLK), 0) == lax.broadcasted_iota(jnp.int32, (BLK, BLK), 1)


def split(value):
    high = value.astype(jnp.bfloat16)
    return high, (value - high.astype(jnp.float32)).astype(jnp.bfloat16)


def dot_t(a, b):
    return lax.dot_general(
        a, b, (((1,), (1,)), ((), ())), precision=highest, preferred_element_type=jnp.float32
    )


def dot(a, b):
    return jnp.dot(a, b, precision=highest, preferred_element_type=jnp.float32)


def pick_kernel(info, rows, cols, meta, child, diag, panel, pivot_part):
    half = rows // 2
    r, q = info.row(meta), info.col(meta)
    mine, within = r // half, r % half
    p = pl.program_id(0)
    front_block = info.pivot(meta, p)
    block = front_block % info.child_blocks
    present = jnp.logical_and(info.has(meta, mine, block, front_block), block % half == within)
    panel[0] = child[0] * as_float(present)
    first = p * (p + 1) // 2
    for t in range(info.pivot_count):
        other = info.pivot(meta, t)
        other_block = other % info.child_blocks
        here = jnp.logical_and(info.has(meta, mine, other_block, other), other_block % cols == q)

        @pl.when(t <= p)
        def _():
            at = pl.multiple_of(other_block // cols * BLK, BLK)
            pivot_part[first + t] = panel[0, :, pl.ds(at, BLK)] * as_float(here)

    on_diagonal = jnp.logical_and(front_block % rows == r, front_block % cols == q)

    @pl.when(on_diagonal)
    def _():
        pivot_part[first + p] += jnp.where(eye_mask(), diag[0], 0.0)


def cholesky_kernel(count, blocks, lower, inverse, inverse_t, work, rest):
    at = lambda i, j: i * (i + 1) // 2 + j
    span = lambda i: slice(i * BLK, (i + 1) * BLK)
    lower[...] = jnp.zeros_like(lower)
    inverse[...] = jnp.zeros_like(inverse)
    rest[...] = blocks[...]
    row_ids = lax.broadcasted_iota(jnp.int32, (BLK, BLK), 0)
    col_ids = lax.broadcasted_iota(jnp.int32, (BLK, BLK), 1)
    wide_ids = lax.broadcasted_iota(jnp.int32, (1, 2 * BLK), 1)
    column_ids = lax.broadcasted_iota(jnp.int32, (BLK, 1), 0)
    for p in range(count):
        work[:, :BLK] = rest[at(p, p)]
        work[:, BLK:] = jnp.where(row_ids == col_ids, 1.0, 0.0)

        def eliminate(j, carry):
            row = work[pl.ds(j, 1), :]
            lead = jnp.sum(jnp.where(wide_ids == j, row, 0.0), axis=1, keepdims=True)
            left = work[:, :BLK]
            column = jnp.sum(jnp.where(col_ids == j, left, 0.0), axis=1, keepdims=True)
            column = jnp.where(column_ids > j, column, 0.0)
            scaled = row / lead
            work[...] = work[...] - column * scaled
            return carry

        lax.fori_loop(0, BLK, eliminate, 0)
        left = work[:, :BLK]
        lead = jnp.sum(jnp.where(row_ids == col_ids, left, 0.0), axis=1, keepdims=True)
        scale = 1.0 / jnp.sqrt(lead)
        lower[span(p), span(p)] = jnp.where(row_ids <= col_ids, left * scale, 0.0).T
        inverse[span(p), span(p)] = work[:, BLK:] * scale
        own_inverse = inverse[span(p), span(p)]
        for i in range(p + 1, count):
            lower[span(i), span(p)] = dot_t(rest[at(i, p)], own_inverse)
        for i in range(p + 1, count):
            for k in range(p + 1, i + 1):
                rest[at(i, k)] -= dot_t(lower[span(i), span(p)], lower[span(k), span(p)])
    for i in range(1, count):
        for j in range(i):
            known = slice(j * BLK, i * BLK)
            partial = dot(lower[span(i), known], inverse[known, span(j)])
            inverse[span(i), span(j)] = -dot(inverse[span(i), span(i)], partial)
    inverse_t[...] = inverse[...].T


def columns_kernel(info, rows, cols, child_slots, width, meta, own, other, inverse, *refs):
    stacked = refs[-1]
    r, q = info.row(meta), info.col(meta)
    mine = r // (rows // 2)
    v, step = pl.program_id(0), pl.program_id(1)
    parts = []
    for i in range(width):
        block = (step * width + i) * cols + q
        front_block = block + v * info.child_blocks
        keep = jnp.logical_not(info.is_pivot(meta, front_block))
        lanes = slice(i * BLK, (i + 1) * BLK)
        take = as_float(jnp.logical_and(keep, info.has(meta, mine, block, front_block)))
        take_other = as_float(jnp.logical_and(keep, info.has(meta, 1 - mine, block, front_block)))
        parts.append(own[:, lanes] * take + other[:, lanes] * take_other)
    high, low = split(dot(inverse[...], jnp.concatenate(parts, axis=1)))
    depth = high.shape[0]
    stacked[:depth], stacked[depth : 2 * depth], stacked[2 * depth :] = high, high, low


def chosen(holder, used, pieces):
    value = pieces[0][...]
    for n, piece in zip(used[1:], pieces[1:]):
        value = jnp.where(holder == n, piece[...], value)
    return value


def rows_kernel(info, rows, cols, width, share, turn, first, used, meta, *refs):
    r, q = info.row(meta), info.col(meta)
    mine = r // (rows // 2)
    s, step = info.source(meta, turn), pl.program_id(0) + first
    lower, inverse_t = refs[len(used) :][:2]
    factor, parts, work = refs[-3:]
    piece = chosen(info.held(meta, s), used, refs[: len(used)])
    half_depth = piece.shape[0] // 2
    own_value = dot(piece[:half_depth].T, inverse_t[...])
    other_value = dot(piece[half_depth:].T, inverse_t[...])
    at = pl.multiple_of(q * share // BLK * BLK, BLK)
    depth = lower.shape[0]
    for i in range(width):
        block = (step * width + i) * cols + r + s * rows
        span = slice(i * BLK, (i + 1) * BLK)
        for v in range(2):
            front_block = block + v * info.child_blocks
            take = as_float(info.has(meta, mine, block, front_block))
            take_other = as_float(info.has(meta, 1 - mine, block, front_block))
            value = own_value[span, :] * take + other_value[span, :] * take_other
            high, low = split(value)
            parts[v, i, :, :depth], parts[v, i, :, depth : 2 * depth], parts[v, i, :, 2 * depth :] = high, low, high
            work[...] = value
            factor[v, i, 0] = work[:, pl.ds(at, BLK)]
            for p in range(info.pivot_count):

                @pl.when(front_block == info.pivot(meta, p))
                def _():
                    factor[v, i, 0] = lower[p * BLK : (p + 1) * BLK, pl.ds(at, BLK)]
                    parts[v, i] = jnp.zeros_like(parts[v, i])


def update_kernel(info, rows, cols, child_slots, width, turn, first, meta, *refs):
    own, other, left, right, diag = refs[:5]
    tile, token = refs[-2:]
    token[...] = jnp.zeros_like(token)
    r, q = info.row(meta), info.col(meta)
    mine = r // (rows // 2)
    step, v = pl.program_id(0), pl.program_id(1)
    left_rows = left[...].reshape(2 * ROWS_AT_ONCE * BLK, left.shape[-1])

    def takes(block, front_block):
        keep = jnp.logical_not(info.is_pivot(meta, front_block))
        return [as_float(jnp.logical_and(keep, info.has(meta, c, block, front_block))) for c in (mine, 1 - mine)]

    def row_block(j):
        return (first + step * ROWS_AT_ONCE + j) * cols + info.source(meta, turn) * rows + r

    row_takes = {
        (u, j): takes(row_block(j), row_block(j) + u * info.child_blocks)
        for u in range(2)
        for j in range(ROWS_AT_ONCE)
    }
    for start in range(0, child_slots, width):
        at = pl.multiple_of((v * child_slots + start) * BLK, BLK)
        change = jnp.dot(left_rows, right[:, pl.ds(at, width * BLK)], preferred_element_type=jnp.float32)
        for i in range(width):
            block = (start + i) * cols + q
            col_takes = takes(block, block + v * info.child_blocks)
            lanes = slice((start + i) * BLK, (start + i + 1) * BLK)
            for (u, j), row_take in row_takes.items():
                n = u * ROWS_AT_ONCE + j
                tile[u, j, 0, :, lanes] = (
                    own[j, 0, 0, :, lanes] * (row_take[0] * col_takes[0])
                    + other[j, :, lanes] * (row_take[1] * col_takes[1])
                    - change[n * BLK : (n + 1) * BLK, i * BLK : (i + 1) * BLK]
                )
    for u in range(2):
        for j in range(ROWS_AT_ONCE):
            front_block = row_block(j) + u * info.child_blocks
            slot = front_block // cols
            here = jnp.logical_and(front_block % cols == q, slot // child_slots == v)

            @pl.when(jnp.logical_and(here, jnp.logical_not(info.is_pivot(meta, front_block))))
            def _():
                at = pl.multiple_of(slot % child_slots * BLK, BLK)
                tile[u, j, 0, :, pl.ds(at, BLK)] += jnp.where(eye_mask(), diag[u, j, 0], 0.0)


def params(grid_size, mib=32):
    return pltpu.CompilerParams(
        dimension_semantics=("arbitrary",) * grid_size, vmem_limit_bytes=mib * 1024 * 1024
    )


def about(micros):
    micros *= PACE
    return pl.CostEstimate(flops=int(micros * 1.15e9), bytes_accessed=int(micros * 3.69e6), transcendentals=0)


def pause_kernel(*refs):
    refs[-1][...] = jnp.ones_like(refs[-1])


def pause(micros, *after):
    ones = pl.pallas_call(
        pause_kernel,
        in_specs=[pl.BlockSpec(memory_space=pl.ANY)] * len(after),
        out_shape=jax.ShapeDtypeStruct((8, BLK), jnp.float32),
        cost_estimate=about(micros),
        name="pause",
    )(*after)
    return ones[0, 0]


def per_device(contrib, front_diag, child_map, pivots):
    rows, cols = lax.axis_size("row"), lax.axis_size("col")
    r, q = lax.axis_index("row"), lax.axis_index("col")
    half = rows // 2
    half_bit = half.bit_length() - 1
    sources = cols // rows
    local_rows, child_width = front_diag.shape[0], contrib.shape[1]
    row_slots = local_rows // BLK
    tile_cols = NF // cols
    child_slots = child_width // BLK
    child_rows = contrib.shape[0] // BLK
    row_half = child_rows // 2
    child_blocks, pivot_count = child_map.shape[1], pivots.shape[0]
    depth = pivot_count * BLK
    width = min(4, child_slots)
    steps, where = spread_plan(rows, cols)
    turns = np.argsort(where, axis=0, kind="stable").astype(np.int32)
    early = set(np.take_along_axis(where, turns[:1], 0).ravel()) - {0}
    order = None
    if len(steps) > 2 * sources:
        order, where = fold_plan(where)
    held_count = int(where.max()) + 1
    info = Meta(child_blocks, pivot_count, sources)
    meta = info.pack(child_map, pivots, r, q, where, turns)
    f32, bf16 = jnp.float32, jnp.bfloat16
    shape = jax.ShapeDtypeStruct

    lower_count = pivot_count * (pivot_count + 1) // 2
    panel, pivot_part = pl.pallas_call(
        functools.partial(pick_kernel, info, rows, cols),
        grid_spec=pltpu.PrefetchScalarGridSpec(
            num_scalar_prefetch=1,
            grid=(pivot_count,),
            in_specs=[
                pl.BlockSpec(
                    (1, BLK, child_width), lambda p, m: (info.pivot(m, p) % child_blocks // half, 0, 0)
                ),
                pl.BlockSpec((1, 1, BLK), lambda p, m: (info.pivot(m, p) // rows, 0, 0)),
            ],
            out_specs=[
                pl.BlockSpec((1, BLK, child_width), lambda p, m: (p, 0, 0)),
                pl.BlockSpec((lower_count, BLK, BLK), lambda p, m: (0, 0, 0)),
            ],
        ),
        out_shape=[
            shape((pivot_count, BLK, child_width), f32),
            shape((lower_count, BLK, BLK), f32),
        ],
        compiler_params=params(1),
        name="pick",
        cost_estimate=about(5),
    )(meta, contrib.reshape(child_rows, BLK, child_width), front_diag.reshape(row_slots, 1, BLK))
    own = panel.reshape(depth, child_width)
    for bit in range(half_bit):
        own = own + swapped(own, "row", bit)
    other = swapped(own, "row", half_bit)

    def folded(held):
        if order is None:
            return held
        mine_order = jnp.asarray(order)[:, r, q]
        merged = [held[0]]
        for n in range(held_count - 1):
            merged.append(sum(jnp.where(mine_order[k] == n, held[k], 0.0) for k in range(1, len(held))))
        return merged

    pivot_blocks = pivot_part
    for bit in range(cols.bit_length() - 1):
        across = swapped(pivot_blocks, "col", bit)
        across_first = across if bit == 0 else across_first
        pivot_blocks = pivot_blocks + across
    pivot_blocks = gated(pivot_blocks, other)
    for bit in range(half_bit, -1, -1):
        pivot_blocks = pivot_blocks + swapped(pivot_blocks, "row", bit)

    both = jnp.concatenate([own, other]) * one_after([across, other, pivot_blocks][BOTH]).astype(f32)
    halves = HALVES if child_slots // ROWS_AT_ONCE % HALVES == 0 and order is None else 1
    held = [[both]]
    for n, (buffer, pairs) in enumerate(steps):
        sent = held[buffer][0]
        if n + 1 not in early:
            sent = jnp.split(sent, halves, axis=1)
        else:
            sent = [sent]
        held.append([lax.ppermute(part, ("row", "col"), pairs) for part in sent])
    meanwhile = [part for n in early for part in held[n]]
    if order is not None:
        held = [[part] for part in folded([parts[0] for parts in held])]

    lower, inverse, inverse_t = pl.pallas_call(
        functools.partial(cholesky_kernel, pivot_count),
        out_shape=[shape((depth, depth), f32)] * 3,
        scratch_shapes=[pltpu.VMEM((BLK, 2 * BLK), f32), pltpu.VMEM((lower_count, BLK, BLK), f32)],
        compiler_params=params(0),
        name="factor_pivots",
        cost_estimate=about(59),
    )(pivot_blocks)

    own_view = contrib.reshape(child_slots, sources, 2, BLK, child_width)
    mine = r // half
    partner_turns = jnp.asarray(turns)[:, r ^ half, q]
    received = []
    for turn in range(sources):
        chunks = (child_slots,)
        if turn > 0 and sum(CHUNKS) == child_slots:
            chunks = CHUNKS
        first = 0
        for chunk in chunks:
            if not received:
                start = one_after([pivot_blocks, other, across, across_first][B0])
            elif len(received) == 1:
                start = one_after(inverse)
            else:
                if len(received) == 1:
                    start = one_after(inverse)
                elif G5 == 0:
                    start = pause(MAGNET, inverse, part).astype(jnp.int32)
                elif G5 == 1:
                    start = one_after(inverse, received[0][2])
                elif G5 == 2:
                    start = pause(MAGNET, received[0][2], part).astype(jnp.int32)
                else:
                    start = pause(MAGNET, inverse, part, *[held[n][0] for n in early]).astype(jnp.int32)
            part = lax.dynamic_slice(
                own_view,
                (first, partner_turns[turn] * start, 1 - mine, 0, 0),
                (chunk, 1, 1, BLK, child_width),
            ).reshape(chunk, BLK, child_width)
            received.append((turn, first, swapped(part, "row", half_bit)))
            first += chunk
    meanwhile.append(received[0][2])

    lanes = width * BLK
    groups = child_slots // width
    whole = lambda *_: (0, 0)
    untouched = pl.BlockSpec(memory_space=pl.ANY)
    col_parts = pl.pallas_call(
        functools.partial(columns_kernel, info, rows, cols, child_slots, width),
        grid_spec=pltpu.PrefetchScalarGridSpec(
            num_scalar_prefetch=1,
            grid=(2, groups),
            in_specs=[
                pl.BlockSpec((depth, lanes), lambda v, g, m: (0, g)),
                pl.BlockSpec((depth, lanes), lambda v, g, m: (0, g)),
                pl.BlockSpec((depth, depth), whole),
            ]
            + [untouched] * len(meanwhile),
            out_specs=pl.BlockSpec((3 * depth, lanes), lambda v, g, m: (0, v * groups + g)),
        ),
        out_shape=shape((3 * depth, tile_cols), bf16),
        compiler_params=params(2),
        name="factor_at_columns",
        cost_estimate=about(10),
    )(meta, own, other, inverse, *meanwhile)

    share = depth // cols
    factor = None
    tile = token = None
    diag_view = front_diag.reshape(2, child_slots, sources, 1, BLK)
    mine_of = lambda m: info.row(m) // half
    square = pl.BlockSpec((depth, depth), whole)
    few = min(2, width)
    counts = [1] + [halves] * (sources - 1)
    row_parts = [[] for _ in counts]

    order_of_work = [("rows", 0, 0), ("rows", 1, 0), ("tile", 0)]
    chunks_of = [[(first, part) for at_turn, first, part in received if at_turn == turn] for turn in range(sources)]
    order_of_work = [("rows", 0, 0), ("rows", 1, 0), ("tile", 0, 0)] if G6 else [("rows", 0, 0), ("tile", 0, 0), ("rows", 1, 0)]
    for turn in range(1, sources):
        ahead = len(chunks_of[turn]) // 2 if counts[turn] == 2 and ORDER else 0
        order_of_work += [("tile", turn, n) for n in range(ahead)]
        order_of_work += [("rows", turn, n) for n in range(counts[turn]) if (turn, n) != (1, 0)]
        order_of_work += [("tile", turn, n) for n in range(ahead, len(chunks_of[turn]))]
    for work, turn, *rest in order_of_work:
        parts_count = counts[turn]
        if work == "rows":
            (at_half,) = rest
            used = sorted({int(n) for n in np.take_along_axis(where, turns[turn : turn + 1], 0).ravel()})
            steps_here = child_slots // few // parts_count
            first = at_half * steps_here

            def piece(n, turn=turn, first=first, at_half=at_half):
                base = first if len(held[n]) == 1 else 0
                return held[n][-1 if base else min(at_half, len(held[n]) - 1)], pl.BlockSpec(
                    (2 * depth, few * BLK),
                    lambda g, m: (0, jnp.where(info.held(m, info.source(m, turn)) == n, base + g, 0)),
                )

            operands = [piece(n)[0] for n in used] + [lower, inverse_t]
            in_specs = [piece(n)[1] for n in used] + [square, square]
            if factor is None:
                factor, aliases = jnp.zeros((2, 1, sources, BLK, BLK), f32), {}
            else:
                aliases = {len(operands) + 1: 0}
            operands += [factor, [meta, received[0][2]][GATE3] if token is None else token]
            in_specs += [untouched] * 2
            factor, row_part = pl.pallas_call(
                functools.partial(rows_kernel, info, rows, cols, few, share, turn, first, used),
                grid_spec=pltpu.PrefetchScalarGridSpec(
                    num_scalar_prefetch=1,
                    grid=(steps_here,),
                    in_specs=in_specs,
                    out_specs=[
                        pl.BlockSpec(
                            (2, few, 1, BLK, BLK),
                            lambda g, m, turn=turn, first=first: (0, first + g, info.source(m, turn), 0, 0),
                        ),
                        pl.BlockSpec((2, few, BLK, 3 * depth), lambda g, m: (0, g, 0, 0)),
                    ],
                    scratch_shapes=[pltpu.VMEM((BLK, depth), f32)],
                ),
                out_shape=[
                    shape((2, child_slots, sources, BLK, BLK), f32),
                    shape((2, child_slots // parts_count, BLK, 3 * depth), bf16),
                ],
                input_output_aliases=aliases,
                compiler_params=params(1, 40),
                name="factor_rows",
                cost_estimate=about(3.0 * steps_here * (LATE if turn else 1.0)),
            )(meta, *operands)
            row_parts[turn].append(row_part)
            continue

        for first, part in [chunks_of[turn][rest[0]]]:
            at = first // ROWS_AT_ONCE
            row_part = row_parts[turn][first * parts_count // child_slots]
            left_at = at % (child_slots // parts_count // ROWS_AT_ONCE)
            source_of = functools.partial(info.source, turn=turn)
            in_specs = [
                pl.BlockSpec(
                    (ROWS_AT_ONCE, 1, 1, BLK, child_width),
                    lambda t, v, m, at=at, source_of=source_of: (at + t, source_of(m), mine_of(m), 0, 0),
                ),
                pl.BlockSpec((ROWS_AT_ONCE, BLK, child_width), lambda t, v, m: (t, 0, 0)),
                pl.BlockSpec((2, ROWS_AT_ONCE, BLK, 3 * depth), lambda t, v, m, at=left_at: (0, at + t, 0, 0)),
                pl.BlockSpec((3 * depth, tile_cols), whole),
                pl.BlockSpec(
                    (2, ROWS_AT_ONCE, 1, 1, BLK),
                    lambda t, v, m, at=at, source_of=source_of: (0, at + t, source_of(m), 0, 0),
                ),
            ]
            operands = [own_view, part, row_part, col_parts, diag_view]
            aliases = {}
            if tile is None and G6:
                in_specs.append(untouched)
                operands.append(row_parts[1][0])
            elif tile is not None:
                in_specs.append(untouched)
                operands.append(tile)
                aliases = {len(operands): 0}
            tile, token = pl.pallas_call(
                functools.partial(update_kernel, info, rows, cols, child_slots, width, turn, first),
                grid_spec=pltpu.PrefetchScalarGridSpec(
                    num_scalar_prefetch=1,
                    grid=(part.shape[0] // ROWS_AT_ONCE, 2),
                    in_specs=in_specs,
                    out_specs=[
                        pl.BlockSpec(
                            (2, ROWS_AT_ONCE, 1, BLK, child_width),
                            lambda t, v, m, at=at, source_of=source_of: (0, at + t, source_of(m), 0, v),
                        ),
                        pl.BlockSpec((8, BLK), lambda t, v, m: (0, 0)),
                    ],
                ),
                out_shape=[shape((2, child_slots, sources, BLK, tile_cols), f32), shape((8, BLK), f32)],
                input_output_aliases=aliases,
                compiler_params=params(2, 36),
                name="update_tile",
                cost_estimate=about(3.0 * part.shape[0] * (LATE if turn else 1.0)),
            )(meta, *operands)
    factor = factor.reshape(local_rows, BLK)
    if share < BLK:
        factor = lax.dynamic_slice_in_dim(factor, q * share % BLK, share, 1)

    return factor, tile.reshape(local_rows, tile_cols)


def solution(mesh):
    placed = (P(("front", "row"), "col"), P(("front", "row")), P("front", None), P("front"))
    return jax.shard_map(
        per_device,
        mesh=mesh,
        in_specs=placed,
        out_specs=(P(("front", "row"), "col"), P(("front", "row"), "col")),
        check_vma=False,
    )
```

```python
import functools

import jax
import jax.numpy as jnp
import numpy as np
from jax import lax
from jax.experimental import pallas as pl
from jax.experimental.pallas import tpu as pltpu
from jax.sharding import PartitionSpec as P

NF = 8192
BLK = 128
HALVES = 2
ORDER = 1
B0 = 3
GATE3 = 0
MAGNET = 50
G5 = 0
G6 = 0
PIECES = 1
BOTH = 0
CHUNKS = (4, 4)
ROWS_AT_ONCE = 2
PACE = 1.0
LATE = 1.0

highest = lax.Precision.HIGHEST


def swapped(shard, axis, bit):
    return lax.ppermute(shard, axis, [(i, i ^ 1 << bit) for i in range(lax.axis_size(axis))])


def one_after(*arrays):
    first = [array[(0,) * array.ndim] for array in arrays]
    there = functools.reduce(jnp.logical_and, [value == value for value in first])
    return jnp.where(there, 1, 0)


def gated(value, *arrays):
    return value * one_after(*arrays).astype(value.dtype)


def spread_plan(rows, cols):
    sources = cols // rows
    where = -np.ones((sources, rows, cols), np.int32)
    for r in range(rows):
        for s in range(sources):
            where[s, r, r + s * rows] = 0
    steps = []
    while (where < 0).any():
        for buffer in range(len(steps) + 1):
            moves = []
            for r in range(rows):
                sign = 1 if r <= cols - 1 - (r + (sources - 1) * rows) else -1
                taken = set()
                for h in range(cols)[::-sign]:
                    for s in range(sources):
                        if where[s, r, h] != buffer:
                            continue
                        open_to = [
                            d for d in range(cols)
                            if where[s, r, d] < 0 and d not in taken and abs(d - h) <= rows
                        ]
                        if open_to:
                            d = max(open_to, key=lambda d: sign * (d - h))
                            taken.add(d)
                            moves.append((s, r, h, d))
            if moves:
                break
        steps.append((buffer, [(r * cols + h, r * cols + d) for _, r, h, d in moves]))
        for s, r, _, d in moves:
            where[s, r, d] = len(steps)
    return steps, where


def fold_plan(where):
    sources, rows, cols = where.shape
    steps = where.max()
    order = -np.ones((steps + 1, rows, cols), np.int32)
    folded = np.zeros_like(where)
    for r in range(rows):
        for d in range(cols):
            got = sorted((where[s, r, d], s) for s in range(sources) if where[s, r, d] > 0)
            for n, (step, s) in enumerate(got):
                order[step, r, d] = n
                folded[s, r, d] = n + 1
    return order, folded


class Meta:
    def __init__(self, child_blocks, pivot_count, sources):
        self.child_blocks, self.pivot_count, self.sources = child_blocks, pivot_count, sources

    def pack(self, child_map, pivots, row_index, col_index, where, turns):
        place = jnp.stack([row_index, col_index]).astype(jnp.int32)
        held = jnp.asarray(np.concatenate([where, turns]))[:, row_index, col_index]
        return jnp.concatenate([child_map.reshape(-1), pivots, place, held])

    def has(self, meta, child, block, front_block):
        return meta[child * self.child_blocks + block] == front_block

    def pivot(self, meta, p):
        return meta[2 * self.child_blocks + p]

    def row(self, meta):
        return meta[2 * self.child_blocks + self.pivot_count]

    def col(self, meta):
        return meta[2 * self.child_blocks + self.pivot_count + 1]

    def held(self, meta, s):
        return meta[2 * self.child_blocks + self.pivot_count + 2 + s]

    def source(self, meta, turn):
        return self.held(meta, self.sources + turn)

    def is_pivot(self, meta, front_block):
        hit = front_block == self.pivot(meta, 0)
        for p in range(1, self.pivot_count):
            hit = jnp.logical_or(hit, front_block == self.pivot(meta, p))
        return hit


def as_float(flag):
    return jnp.where(flag, 1.0, 0.0).astype(jnp.float32)


def eye_mask():
    return lax.broadcasted_iota(jnp.int32, (BLK, BLK), 0) == lax.broadcasted_iota(jnp.int32, (BLK, BLK), 1)


def split(value):
    high = value.astype(jnp.bfloat16)
    return high, (value - high.astype(jnp.float32)).astype(jnp.bfloat16)


def dot_t(a, b):
    return lax.dot_general(
        a, b, (((1,), (1,)), ((), ())), precision=highest, preferred_element_type=jnp.float32
    )


def dot(a, b):
    return jnp.dot(a, b, precision=highest, preferred_element_type=jnp.float32)


def pick_kernel(info, rows, cols, meta, child, diag, panel, pivot_part):
    half = rows // 2
    r, q = info.row(meta), info.col(meta)
    mine, within = r // half, r % half
    p = pl.program_id(0)
    front_block = info.pivot(meta, p)
    block = front_block % info.child_blocks
    present = jnp.logical_and(info.has(meta, mine, block, front_block), block % half == within)
    panel[0] = child[0] * as_float(present)
    first = p * (p + 1) // 2
    for t in range(info.pivot_count):
        other = info.pivot(meta, t)
        other_block = other % info.child_blocks
        here = jnp.logical_and(info.has(meta, mine, other_block, other), other_block % cols == q)

        @pl.when(t <= p)
        def _():
            at = pl.multiple_of(other_block // cols * BLK, BLK)
            pivot_part[first + t] = panel[0, :, pl.ds(at, BLK)] * as_float(here)

    on_diagonal = jnp.logical_and(front_block % rows == r, front_block % cols == q)

    @pl.when(on_diagonal)
    def _():
        pivot_part[first + p] += jnp.where(eye_mask(), diag[0], 0.0)


def cholesky_kernel(count, blocks, lower, inverse, inverse_t, work, rest):
    at = lambda i, j: i * (i + 1) // 2 + j
    span = lambda i: slice(i * BLK, (i + 1) * BLK)
    lower[...] = jnp.zeros_like(lower)
    inverse[...] = jnp.zeros_like(inverse)
    rest[...] = blocks[...]
    row_ids = lax.broadcasted_iota(jnp.int32, (BLK, BLK), 0)
    col_ids = lax.broadcasted_iota(jnp.int32, (BLK, BLK), 1)
    wide_ids = lax.broadcasted_iota(jnp.int32, (1, 2 * BLK), 1)
    column_ids = lax.broadcasted_iota(jnp.int32, (BLK, 1), 0)
    for p in range(count):
        work[:, :BLK] = rest[at(p, p)]
        work[:, BLK:] = jnp.where(row_ids == col_ids, 1.0, 0.0)

        def eliminate(j, carry):
            row = work[pl.ds(j, 1), :]
            lead = jnp.sum(jnp.where(wide_ids == j, row, 0.0), axis=1, keepdims=True)
            left = work[:, :BLK]
            column = jnp.sum(jnp.where(col_ids == j, left, 0.0), axis=1, keepdims=True)
            column = jnp.where(column_ids > j, column, 0.0)
            scaled = row / lead
            work[...] = work[...] - column * scaled
            return carry

        lax.fori_loop(0, BLK, eliminate, 0)
        left = work[:, :BLK]
        lead = jnp.sum(jnp.where(row_ids == col_ids, left, 0.0), axis=1, keepdims=True)
        scale = 1.0 / jnp.sqrt(lead)
        lower[span(p), span(p)] = jnp.where(row_ids <= col_ids, left * scale, 0.0).T
        inverse[span(p), span(p)] = work[:, BLK:] * scale
        own_inverse = inverse[span(p), span(p)]
        for i in range(p + 1, count):
            lower[span(i), span(p)] = dot_t(rest[at(i, p)], own_inverse)
        for i in range(p + 1, count):
            for k in range(p + 1, i + 1):
                rest[at(i, k)] -= dot_t(lower[span(i), span(p)], lower[span(k), span(p)])
    for i in range(1, count):
        for j in range(i):
            known = slice(j * BLK, i * BLK)
            partial = dot(lower[span(i), known], inverse[known, span(j)])
            inverse[span(i), span(j)] = -dot(inverse[span(i), span(i)], partial)
    inverse_t[...] = inverse[...].T


def columns_kernel(info, rows, cols, child_slots, width, meta, own, other, inverse, *refs):
    stacked = refs[-1]
    r, q = info.row(meta), info.col(meta)
    mine = r // (rows // 2)
    v, step = pl.program_id(0), pl.program_id(1)
    parts = []
    for i in range(width):
        block = (step * width + i) * cols + q
        front_block = block + v * info.child_blocks
        keep = jnp.logical_not(info.is_pivot(meta, front_block))
        lanes = slice(i * BLK, (i + 1) * BLK)
        take = as_float(jnp.logical_and(keep, info.has(meta, mine, block, front_block)))
        take_other = as_float(jnp.logical_and(keep, info.has(meta, 1 - mine, block, front_block)))
        parts.append(own[:, lanes] * take + other[:, lanes] * take_other)
    high, low = split(dot(inverse[...], jnp.concatenate(parts, axis=1)))
    depth = high.shape[0]
    stacked[:depth], stacked[depth : 2 * depth], stacked[2 * depth :] = high, high, low


def chosen(holder, used, pieces):
    value = pieces[0][...]
    for n, piece in zip(used[1:], pieces[1:]):
        value = jnp.where(holder == n, piece[...], value)
    return value


def rows_kernel(info, rows, cols, width, share, turn, first, used, meta, *refs):
    r, q = info.row(meta), info.col(meta)
    mine = r // (rows // 2)
    s, step = info.source(meta, turn), pl.program_id(0) + first
    lower, inverse_t = refs[len(used) :][:2]
    factor, parts, work = refs[-3:]
    piece = chosen(info.held(meta, s), used, refs[: len(used)])
    half_depth = piece.shape[0] // 2
    own_value = dot(piece[:half_depth].T, inverse_t[...])
    other_value = dot(piece[half_depth:].T, inverse_t[...])
    at = pl.multiple_of(q * share // BLK * BLK, BLK)
    depth = lower.shape[0]
    for i in range(width):
        block = (step * width + i) * cols + r + s * rows
        span = slice(i * BLK, (i + 1) * BLK)
        for v in range(2):
            front_block = block + v * info.child_blocks
            take = as_float(info.has(meta, mine, block, front_block))
            take_other = as_float(info.has(meta, 1 - mine, block, front_block))
            value = own_value[span, :] * take + other_value[span, :] * take_other
            high, low = split(value)
            parts[v, i, :, :depth], parts[v, i, :, depth : 2 * depth], parts[v, i, :, 2 * depth :] = high, low, high
            work[...] = value
            factor[v, i, 0] = work[:, pl.ds(at, BLK)]
            for p in range(info.pivot_count):

                @pl.when(front_block == info.pivot(meta, p))
                def _():
                    factor[v, i, 0] = lower[p * BLK : (p + 1) * BLK, pl.ds(at, BLK)]
                    parts[v, i] = jnp.zeros_like(parts[v, i])


def update_kernel(info, rows, cols, child_slots, width, turn, first, meta, *refs):
    own, other, left, right, diag = refs[:5]
    tile, token = refs[-2:]
    token[...] = jnp.zeros_like(token)
    r, q = info.row(meta), info.col(meta)
    mine = r // (rows // 2)
    v, step = pl.program_id(0), pl.program_id(1)
    left_rows = left[...].reshape(2 * ROWS_AT_ONCE * BLK, left.shape[-1])

    def takes(block, front_block):
        keep = jnp.logical_not(info.is_pivot(meta, front_block))
        return [as_float(jnp.logical_and(keep, info.has(meta, c, block, front_block))) for c in (mine, 1 - mine)]

    def row_block(j):
        return (first + step * ROWS_AT_ONCE + j) * cols + info.source(meta, turn) * rows + r

    row_takes = {
        (u, j): takes(row_block(j), row_block(j) + u * info.child_blocks)
        for u in range(2)
        for j in range(ROWS_AT_ONCE)
    }
    for start in range(0, child_slots, width):
        lanes = slice(start * BLK, (start + width) * BLK)
        change = jnp.dot(left_rows, right[:, lanes], preferred_element_type=jnp.float32)
        for i in range(width):
            block = (start + i) * cols + q
            col_takes = takes(block, block + v * info.child_blocks)
            lanes = slice((start + i) * BLK, (start + i + 1) * BLK)
            for (u, j), row_take in row_takes.items():
                n = u * ROWS_AT_ONCE + j
                tile[u, j, 0, :, lanes] = (
                    own[j, 0, 0, :, lanes] * (row_take[0] * col_takes[0])
                    + other[j, :, lanes] * (row_take[1] * col_takes[1])
                    - change[n * BLK : (n + 1) * BLK, i * BLK : (i + 1) * BLK]
                )
    for u in range(2):
        for j in range(ROWS_AT_ONCE):
            front_block = row_block(j) + u * info.child_blocks
            slot = front_block // cols
            here = jnp.logical_and(front_block % cols == q, slot // child_slots == v)

            @pl.when(jnp.logical_and(here, jnp.logical_not(info.is_pivot(meta, front_block))))
            def _():
                at = pl.multiple_of(slot % child_slots * BLK, BLK)
                tile[u, j, 0, :, pl.ds(at, BLK)] += jnp.where(eye_mask(), diag[u, j, 0], 0.0)


def params(grid_size, mib=32):
    return pltpu.CompilerParams(
        dimension_semantics=("arbitrary",) * grid_size, vmem_limit_bytes=mib * 1024 * 1024
    )


def about(micros):
    micros *= PACE
    return pl.CostEstimate(flops=int(micros * 1.15e9), bytes_accessed=int(micros * 3.69e6), transcendentals=0)


def pause_kernel(*refs):
    refs[-1][...] = jnp.ones_like(refs[-1])


def pause(micros, *after):
    ones = pl.pallas_call(
        pause_kernel,
        in_specs=[pl.BlockSpec(memory_space=pl.ANY)] * len(after),
        out_shape=jax.ShapeDtypeStruct((8, BLK), jnp.float32),
        cost_estimate=about(micros),
        name="pause",
    )(*after)
    return ones[0, 0]


def per_device(contrib, front_diag, child_map, pivots):
    rows, cols = lax.axis_size("row"), lax.axis_size("col")
    r, q = lax.axis_index("row"), lax.axis_index("col")
    half = rows // 2
    half_bit = half.bit_length() - 1
    sources = cols // rows
    local_rows, child_width = front_diag.shape[0], contrib.shape[1]
    row_slots = local_rows // BLK
    tile_cols = NF // cols
    child_slots = child_width // BLK
    child_rows = contrib.shape[0] // BLK
    row_half = child_rows // 2
    child_blocks, pivot_count = child_map.shape[1], pivots.shape[0]
    depth = pivot_count * BLK
    width = min(4, child_slots)
    steps, where = spread_plan(rows, cols)
    turns = np.argsort(where, axis=0, kind="stable").astype(np.int32)
    early = set(np.take_along_axis(where, turns[:1], 0).ravel()) - {0}
    order = None
    if len(steps) > 2 * sources:
        order, where = fold_plan(where)
    held_count = int(where.max()) + 1
    info = Meta(child_blocks, pivot_count, sources)
    meta = info.pack(child_map, pivots, r, q, where, turns)
    f32, bf16 = jnp.float32, jnp.bfloat16
    shape = jax.ShapeDtypeStruct

    lower_count = pivot_count * (pivot_count + 1) // 2
    panel, pivot_part = pl.pallas_call(
        functools.partial(pick_kernel, info, rows, cols),
        grid_spec=pltpu.PrefetchScalarGridSpec(
            num_scalar_prefetch=1,
            grid=(pivot_count,),
            in_specs=[
                pl.BlockSpec(
                    (1, BLK, child_width), lambda p, m: (info.pivot(m, p) % child_blocks // half, 0, 0)
                ),
                pl.BlockSpec((1, 1, BLK), lambda p, m: (info.pivot(m, p) // rows, 0, 0)),
            ],
            out_specs=[
                pl.BlockSpec((1, BLK, child_width), lambda p, m: (p, 0, 0)),
                pl.BlockSpec((lower_count, BLK, BLK), lambda p, m: (0, 0, 0)),
            ],
        ),
        out_shape=[
            shape((pivot_count, BLK, child_width), f32),
            shape((lower_count, BLK, BLK), f32),
        ],
        compiler_params=params(1, 60),
        name="pick",
        cost_estimate=about(5),
    )(meta, contrib.reshape(child_rows, BLK, child_width), front_diag.reshape(row_slots, 1, BLK))
    own = panel.reshape(depth, child_width)
    for bit in range(half_bit):
        own = own + swapped(own, "row", bit)
    other = swapped(own, "row", half_bit)

    def folded(held):
        if order is None:
            return held
        mine_order = jnp.asarray(order)[:, r, q]
        merged = [held[0]]
        for n in range(held_count - 1):
            merged.append(sum(jnp.where(mine_order[k] == n, held[k], 0.0) for k in range(1, len(held))))
        return merged

    pivot_blocks = pivot_part
    for bit in range(cols.bit_length() - 1):
        across = swapped(pivot_blocks, "col", bit)
        across_first = across if bit == 0 else across_first
        pivot_blocks = pivot_blocks + across
    pivot_blocks = gated(pivot_blocks, other)
    for bit in range(half_bit, -1, -1):
        pivot_blocks = pivot_blocks + swapped(pivot_blocks, "row", bit)

    both = jnp.concatenate([own, other]) * one_after([across, other, pivot_blocks][BOTH]).astype(f32)
    halves = HALVES if child_slots // ROWS_AT_ONCE % HALVES == 0 and order is None else 1
    held = [[both]]
    for n, (buffer, pairs) in enumerate(steps):
        sent = held[buffer][0]
        if n + 1 not in early:
            sent = jnp.split(sent, halves, axis=1)
        else:
            sent = [sent]
        held.append([lax.ppermute(part, ("row", "col"), pairs) for part in sent])
    meanwhile = [part for n in early for part in held[n]]
    if order is not None:
        held = [[part] for part in folded([parts[0] for parts in held])]

    lower, inverse, inverse_t = pl.pallas_call(
        functools.partial(cholesky_kernel, pivot_count),
        out_shape=[shape((depth, depth), f32)] * 3,
        scratch_shapes=[pltpu.VMEM((BLK, 2 * BLK), f32), pltpu.VMEM((lower_count, BLK, BLK), f32)],
        compiler_params=params(0),
        name="factor_pivots",
        cost_estimate=about(59),
    )(pivot_blocks)

    own_view = contrib.reshape(child_slots, sources, 2, BLK, child_width)
    mine = r // half
    partner_turns = jnp.asarray(turns)[:, r ^ half, q]
    received = []
    for turn in range(sources):
        chunks = (child_slots,)
        if turn > 0 and sum(CHUNKS) == child_slots:
            chunks = CHUNKS
        first = 0
        for chunk in chunks:
            if not received:
                start = one_after([pivot_blocks, other, across, across_first][B0])
            elif len(received) == 1:
                start = one_after(inverse)
            else:
                if len(received) == 1:
                    start = one_after(inverse)
                elif G5 == 0:
                    start = pause(MAGNET, inverse, part).astype(jnp.int32)
                elif G5 == 1:
                    start = one_after(inverse, received[0][2])
                elif G5 == 2:
                    start = pause(MAGNET, received[0][2], part).astype(jnp.int32)
                else:
                    start = pause(MAGNET, inverse, part, *[held[n][0] for n in early]).astype(jnp.int32)
            part = lax.dynamic_slice(
                own_view,
                (first, partner_turns[turn] * start, 1 - mine, 0, 0),
                (chunk, 1, 1, BLK, child_width),
            ).reshape(chunk, BLK, child_width)
            received.append((turn, first, swapped(part, "row", half_bit)))
            first += chunk
    meanwhile.append(received[0][2])

    lanes = width * BLK
    groups = child_slots // width
    whole = lambda *_: (0, 0)
    untouched = pl.BlockSpec(memory_space=pl.ANY)
    col_parts = pl.pallas_call(
        functools.partial(columns_kernel, info, rows, cols, child_slots, width),
        grid_spec=pltpu.PrefetchScalarGridSpec(
            num_scalar_prefetch=1,
            grid=(2, groups),
            in_specs=[
                pl.BlockSpec((depth, lanes), lambda v, g, m: (0, g)),
                pl.BlockSpec((depth, lanes), lambda v, g, m: (0, g)),
                pl.BlockSpec((depth, depth), whole),
            ]
            + [untouched] * len(meanwhile),
            out_specs=pl.BlockSpec((3 * depth, lanes), lambda v, g, m: (0, v * groups + g)),
        ),
        out_shape=shape((3 * depth, tile_cols), bf16),
        compiler_params=params(2),
        name="factor_at_columns",
        cost_estimate=about(10),
    )(meta, own, other, inverse, *meanwhile)

    share = depth // cols
    factor = None
    tile = token = None
    diag_view = front_diag.reshape(2, child_slots, sources, 1, BLK)
    mine_of = lambda m: info.row(m) // half
    square = pl.BlockSpec((depth, depth), whole)
    few = min(2, width)
    counts = [1] + [halves] * (sources - 1)
    row_parts = [[] for _ in counts]

    order_of_work = [("rows", 0, 0), ("rows", 1, 0), ("tile", 0)]
    chunks_of = [[] for _ in range(sources)]
    for turn, first, part in received:
        pieces = PIECES if turn == 0 and part.shape[0] % (PIECES * ROWS_AT_ONCE) == 0 else 1
        count = part.shape[0] // pieces
        chunks_of[turn] += [(first + n * count, part, n * count, count) for n in range(pieces)]
    order_of_work = [("rows", 0, 0)] + [("tile", 0, n) for n in range(len(chunks_of[0]))] + [("rows", 1, 0)]
    for turn in range(1, sources):
        ahead = len(chunks_of[turn]) // 2 if counts[turn] == 2 and ORDER else 0
        order_of_work += [("tile", turn, n) for n in range(ahead)]
        order_of_work += [("rows", turn, n) for n in range(counts[turn]) if (turn, n) != (1, 0)]
        order_of_work += [("tile", turn, n) for n in range(ahead, len(chunks_of[turn]))]
    for work, turn, *rest in order_of_work:
        parts_count = counts[turn]
        if work == "rows":
            (at_half,) = rest
            used = sorted({int(n) for n in np.take_along_axis(where, turns[turn : turn + 1], 0).ravel()})
            steps_here = child_slots // few // parts_count
            first = at_half * steps_here

            def piece(n, turn=turn, first=first, at_half=at_half):
                base = first if len(held[n]) == 1 else 0
                return held[n][-1 if base else min(at_half, len(held[n]) - 1)], pl.BlockSpec(
                    (2 * depth, few * BLK),
                    lambda g, m: (0, jnp.where(info.held(m, info.source(m, turn)) == n, base + g, 0)),
                )

            operands = [piece(n)[0] for n in used] + [lower, inverse_t]
            in_specs = [piece(n)[1] for n in used] + [square, square]
            if factor is None:
                factor, aliases = jnp.zeros((2, 1, sources, BLK, BLK), f32), {}
            else:
                aliases = {len(operands) + 1: 0}
            operands += [factor, [meta, received[0][2]][GATE3] if token is None else token]
            in_specs += [untouched] * 2
            factor, row_part = pl.pallas_call(
                functools.partial(rows_kernel, info, rows, cols, few, share, turn, first, used),
                grid_spec=pltpu.PrefetchScalarGridSpec(
                    num_scalar_prefetch=1,
                    grid=(steps_here,),
                    in_specs=in_specs,
                    out_specs=[
                        pl.BlockSpec(
                            (2, few, 1, BLK, BLK),
                            lambda g, m, turn=turn, first=first: (0, first + g, info.source(m, turn), 0, 0),
                        ),
                        pl.BlockSpec((2, few, BLK, 3 * depth), lambda g, m: (0, g, 0, 0)),
                    ],
                    scratch_shapes=[pltpu.VMEM((BLK, depth), f32)],
                ),
                out_shape=[
                    shape((2, child_slots, sources, BLK, BLK), f32),
                    shape((2, child_slots // parts_count, BLK, 3 * depth), bf16),
                ],
                input_output_aliases=aliases,
                compiler_params=params(1, 40),
                name="factor_rows",
                cost_estimate=about(3.0 * steps_here * (LATE if turn else 1.0)),
            )(meta, *operands)
            row_parts[turn].append(row_part)
            continue

        for first, part, offset, count in [chunks_of[turn][rest[0]]]:
            at = first // ROWS_AT_ONCE
            row_part = row_parts[turn][first * parts_count // child_slots]
            left_at = at % (child_slots // parts_count // ROWS_AT_ONCE)
            source_of = functools.partial(info.source, turn=turn)
            in_specs = [
                pl.BlockSpec(
                    (ROWS_AT_ONCE, 1, 1, BLK, child_width),
                    lambda v, t, m, at=at, source_of=source_of: (at + t, source_of(m), mine_of(m), 0, 0),
                ),
                pl.BlockSpec((ROWS_AT_ONCE, BLK, child_width), lambda v, t, m, at=offset // ROWS_AT_ONCE: (at + t, 0, 0)),
                pl.BlockSpec((2, ROWS_AT_ONCE, BLK, 3 * depth), lambda v, t, m, at=left_at: (0, at + t, 0, 0)),
                pl.BlockSpec((3 * depth, child_width), lambda v, t, m: (0, v)),
                pl.BlockSpec(
                    (2, ROWS_AT_ONCE, 1, 1, BLK),
                    lambda v, t, m, at=at, source_of=source_of: (0, at + t, source_of(m), 0, 0),
                ),
            ]
            operands = [own_view, part, row_part, col_parts, diag_view]
            aliases = {}
            if tile is None and G6:
                in_specs.append(untouched)
                operands.append(row_parts[1][0])
            elif tile is not None:
                in_specs.append(untouched)
                operands.append(tile)
                aliases = {len(operands): 0}
            tile, token = pl.pallas_call(
                functools.partial(update_kernel, info, rows, cols, child_slots, width, turn, first),
                grid_spec=pltpu.PrefetchScalarGridSpec(
                    num_scalar_prefetch=1,
                    grid=(2, count // ROWS_AT_ONCE),
                    in_specs=in_specs,
                    out_specs=[
                        pl.BlockSpec(
                            (2, ROWS_AT_ONCE, 1, BLK, child_width),
                            lambda v, t, m, at=at, source_of=source_of: (0, at + t, source_of(m), 0, v),
                        ),
                        pl.BlockSpec((8, BLK), lambda v, t, m: (0, 0)),
                    ],
                ),
                out_shape=[shape((2, child_slots, sources, BLK, tile_cols), f32), shape((8, BLK), f32)],
                input_output_aliases=aliases,
                compiler_params=params(2, 36),
                name="update_tile",
                cost_estimate=about(3.0 * count * (LATE if turn else 1.0)),
            )(meta, *operands)
    factor = factor.reshape(local_rows, BLK)
    if share < BLK:
        factor = lax.dynamic_slice_in_dim(factor, q * share % BLK, share, 1)

    return factor, tile.reshape(local_rows, tile_cols)


def solution(mesh):
    placed = (P(("front", "row"), "col"), P(("front", "row")), P("front", None), P("front"))
    return jax.shard_map(
        per_device,
        mesh=mesh,
        in_specs=placed,
        out_specs=(P(("front", "row"), "col"), P(("front", "row"), "col")),
        check_vma=False,
    )
```

```python
import functools

import jax
import jax.numpy as jnp
import numpy as np
from jax import lax
from jax.experimental import pallas as pl
from jax.experimental.pallas import tpu as pltpu
from jax.sharding import PartitionSpec as P

NF = 8192
BLK = 128
HALVES = 2
ORDER = 1
B0 = 3
GATE3 = 0
MAGNET = 50
G5 = 0
G6 = 0
PIECES = 1
BOTH = 0
CHUNKS = (4, 4)
ROWS_AT_ONCE = 2
PACE = 1.0
LATE = 1.0

highest = lax.Precision.HIGHEST


def swapped(shard, axis, bit):
    return lax.ppermute(shard, axis, [(i, i ^ 1 << bit) for i in range(lax.axis_size(axis))])


def one_after(*arrays):
    first = [array[(0,) * array.ndim] for array in arrays]
    there = functools.reduce(jnp.logical_and, [value == value for value in first])
    return jnp.where(there, 1, 0)


def gated(value, *arrays):
    return value * one_after(*arrays).astype(value.dtype)


def spread_plan(rows, cols):
    sources = cols // rows
    where = -np.ones((sources, rows, cols), np.int32)
    for r in range(rows):
        for s in range(sources):
            where[s, r, r + s * rows] = 0
    steps = []
    while (where < 0).any():
        for buffer in range(len(steps) + 1):
            moves = []
            for r in range(rows):
                sign = 1 if r <= cols - 1 - (r + (sources - 1) * rows) else -1
                taken = set()
                for h in range(cols)[::-sign]:
                    for s in range(sources):
                        if where[s, r, h] != buffer:
                            continue
                        open_to = [
                            d for d in range(cols)
                            if where[s, r, d] < 0 and d not in taken and abs(d - h) <= rows
                        ]
                        if open_to:
                            d = max(open_to, key=lambda d: sign * (d - h))
                            taken.add(d)
                            moves.append((s, r, h, d))
            if moves:
                break
        steps.append((buffer, [(r * cols + h, r * cols + d) for _, r, h, d in moves]))
        for s, r, _, d in moves:
            where[s, r, d] = len(steps)
    return steps, where


def fold_plan(where):
    sources, rows, cols = where.shape
    steps = where.max()
    order = -np.ones((steps + 1, rows, cols), np.int32)
    folded = np.zeros_like(where)
    for r in range(rows):
        for d in range(cols):
            got = sorted((where[s, r, d], s) for s in range(sources) if where[s, r, d] > 0)
            for n, (step, s) in enumerate(got):
                order[step, r, d] = n
                folded[s, r, d] = n + 1
    return order, folded


class Meta:
    def __init__(self, child_blocks, pivot_count, sources):
        self.child_blocks, self.pivot_count, self.sources = child_blocks, pivot_count, sources

    def pack(self, child_map, pivots, row_index, col_index, where, turns):
        place = jnp.stack([row_index, col_index]).astype(jnp.int32)
        held = jnp.asarray(np.concatenate([where, turns]))[:, row_index, col_index]
        return jnp.concatenate([child_map.reshape(-1), pivots, place, held])

    def has(self, meta, child, block, front_block):
        return meta[child * self.child_blocks + block] == front_block

    def pivot(self, meta, p):
        return meta[2 * self.child_blocks + p]

    def row(self, meta):
        return meta[2 * self.child_blocks + self.pivot_count]

    def col(self, meta):
        return meta[2 * self.child_blocks + self.pivot_count + 1]

    def held(self, meta, s):
        return meta[2 * self.child_blocks + self.pivot_count + 2 + s]

    def source(self, meta, turn):
        return self.held(meta, self.sources + turn)

    def is_pivot(self, meta, front_block):
        hit = front_block == self.pivot(meta, 0)
        for p in range(1, self.pivot_count):
            hit = jnp.logical_or(hit, front_block == self.pivot(meta, p))
        return hit


def as_float(flag):
    return jnp.where(flag, 1.0, 0.0).astype(jnp.float32)


def eye_mask():
    return lax.broadcasted_iota(jnp.int32, (BLK, BLK), 0) == lax.broadcasted_iota(jnp.int32, (BLK, BLK), 1)


def split(value):
    high = value.astype(jnp.bfloat16)
    return high, (value - high.astype(jnp.float32)).astype(jnp.bfloat16)


def dot_t(a, b):
    return lax.dot_general(
        a, b, (((1,), (1,)), ((), ())), precision=highest, preferred_element_type=jnp.float32
    )


def dot(a, b):
    return jnp.dot(a, b, precision=highest, preferred_element_type=jnp.float32)


def pick_kernel(info, rows, cols, meta, *refs):
    count = info.pivot_count
    children, diags = refs[:count], refs[count : 2 * count]
    panel, pivot_part = refs[2 * count :]
    half = rows // 2
    r, q = info.row(meta), info.col(meta)
    mine, within = r // half, r % half
    for p in range(count):
        front_block = info.pivot(meta, p)
        block = front_block % info.child_blocks
        present = jnp.logical_and(info.has(meta, mine, block, front_block), block % half == within)
        panel[p] = children[p][0] * as_float(present)
        first = p * (p + 1) // 2
        for t in range(p + 1):
            other = info.pivot(meta, t)
            other_block = other % info.child_blocks
            here = jnp.logical_and(info.has(meta, mine, other_block, other), other_block % cols == q)
            at = pl.multiple_of(other_block // cols * BLK, BLK)
            pivot_part[first + t] = panel[p, :, pl.ds(at, BLK)] * as_float(here)

        @pl.when(jnp.logical_and(front_block % rows == r, front_block % cols == q))
        def _():
            pivot_part[first + p] += jnp.where(eye_mask(), diags[p][0], 0.0)


def cholesky_kernel(count, blocks, lower, inverse, inverse_t, work, rest):
    at = lambda i, j: i * (i + 1) // 2 + j
    span = lambda i: slice(i * BLK, (i + 1) * BLK)
    lower[...] = jnp.zeros_like(lower)
    inverse[...] = jnp.zeros_like(inverse)
    rest[...] = blocks[...]
    row_ids = lax.broadcasted_iota(jnp.int32, (BLK, BLK), 0)
    col_ids = lax.broadcasted_iota(jnp.int32, (BLK, BLK), 1)
    wide_ids = lax.broadcasted_iota(jnp.int32, (1, 2 * BLK), 1)
    column_ids = lax.broadcasted_iota(jnp.int32, (BLK, 1), 0)
    for p in range(count):
        work[:, :BLK] = rest[at(p, p)]
        work[:, BLK:] = jnp.where(row_ids == col_ids, 1.0, 0.0)

        def eliminate(j, carry):
            row = work[pl.ds(j, 1), :]
            lead = jnp.sum(jnp.where(wide_ids == j, row, 0.0), axis=1, keepdims=True)
            left = work[:, :BLK]
            column = jnp.sum(jnp.where(col_ids == j, left, 0.0), axis=1, keepdims=True)
            column = jnp.where(column_ids > j, column, 0.0)
            scaled = row / lead
            work[...] = work[...] - column * scaled
            return carry

        lax.fori_loop(0, BLK, eliminate, 0)
        left = work[:, :BLK]
        lead = jnp.sum(jnp.where(row_ids == col_ids, left, 0.0), axis=1, keepdims=True)
        scale = 1.0 / jnp.sqrt(lead)
        lower[span(p), span(p)] = jnp.where(row_ids <= col_ids, left * scale, 0.0).T
        inverse[span(p), span(p)] = work[:, BLK:] * scale
        own_inverse = inverse[span(p), span(p)]
        for i in range(p + 1, count):
            lower[span(i), span(p)] = dot_t(rest[at(i, p)], own_inverse)
        for i in range(p + 1, count):
            for k in range(p + 1, i + 1):
                rest[at(i, k)] -= dot_t(lower[span(i), span(p)], lower[span(k), span(p)])
    for i in range(1, count):
        for j in range(i):
            known = slice(j * BLK, i * BLK)
            partial = dot(lower[span(i), known], inverse[known, span(j)])
            inverse[span(i), span(j)] = -dot(inverse[span(i), span(i)], partial)
    inverse_t[...] = inverse[...].T


def columns_kernel(info, rows, cols, child_slots, width, meta, own, other, inverse, *refs):
    stacked = refs[-1]
    r, q = info.row(meta), info.col(meta)
    mine = r // (rows // 2)
    v, step = pl.program_id(0), pl.program_id(1)
    parts = []
    for i in range(width):
        block = (step * width + i) * cols + q
        front_block = block + v * info.child_blocks
        keep = jnp.logical_not(info.is_pivot(meta, front_block))
        lanes = slice(i * BLK, (i + 1) * BLK)
        take = as_float(jnp.logical_and(keep, info.has(meta, mine, block, front_block)))
        take_other = as_float(jnp.logical_and(keep, info.has(meta, 1 - mine, block, front_block)))
        parts.append(own[:, lanes] * take + other[:, lanes] * take_other)
    high, low = split(dot(inverse[...], jnp.concatenate(parts, axis=1)))
    depth = high.shape[0]
    stacked[:depth], stacked[depth : 2 * depth], stacked[2 * depth :] = high, high, low


def chosen(holder, used, pieces):
    value = pieces[0][...]
    for n, piece in zip(used[1:], pieces[1:]):
        value = jnp.where(holder == n, piece[...], value)
    return value


def rows_kernel(info, rows, cols, width, share, turn, first, used, meta, *refs):
    r, q = info.row(meta), info.col(meta)
    mine = r // (rows // 2)
    s, step = info.source(meta, turn), pl.program_id(0) + first
    lower, inverse_t = refs[len(used) :][:2]
    factor, parts, work = refs[-3:]
    piece = chosen(info.held(meta, s), used, refs[: len(used)])
    half_depth = piece.shape[0] // 2
    own_value = dot(piece[:half_depth].T, inverse_t[...])
    other_value = dot(piece[half_depth:].T, inverse_t[...])
    at = pl.multiple_of(q * share // BLK * BLK, BLK)
    depth = lower.shape[0]
    for i in range(width):
        block = (step * width + i) * cols + r + s * rows
        span = slice(i * BLK, (i + 1) * BLK)
        for v in range(2):
            front_block = block + v * info.child_blocks
            take = as_float(info.has(meta, mine, block, front_block))
            take_other = as_float(info.has(meta, 1 - mine, block, front_block))
            value = own_value[span, :] * take + other_value[span, :] * take_other
            high, low = split(value)
            parts[v, i, :, :depth], parts[v, i, :, depth : 2 * depth], parts[v, i, :, 2 * depth :] = high, low, high
            work[...] = value
            factor[v, i, 0] = work[:, pl.ds(at, BLK)]
            for p in range(info.pivot_count):

                @pl.when(front_block == info.pivot(meta, p))
                def _():
                    factor[v, i, 0] = lower[p * BLK : (p + 1) * BLK, pl.ds(at, BLK)]
                    parts[v, i] = jnp.zeros_like(parts[v, i])


def update_kernel(info, rows, cols, child_slots, width, turn, first, meta, *refs):
    own, other, left, right, diag = refs[:5]
    tile, token = refs[-2:]
    token[...] = jnp.zeros_like(token)
    r, q = info.row(meta), info.col(meta)
    mine = r // (rows // 2)
    v, step = pl.program_id(0), pl.program_id(1)
    left_rows = left[...].reshape(2 * ROWS_AT_ONCE * BLK, left.shape[-1])

    def takes(block, front_block):
        keep = jnp.logical_not(info.is_pivot(meta, front_block))
        return [as_float(jnp.logical_and(keep, info.has(meta, c, block, front_block))) for c in (mine, 1 - mine)]

    def row_block(j):
        return (first + step * ROWS_AT_ONCE + j) * cols + info.source(meta, turn) * rows + r

    row_takes = {
        (u, j): takes(row_block(j), row_block(j) + u * info.child_blocks)
        for u in range(2)
        for j in range(ROWS_AT_ONCE)
    }
    for start in range(0, child_slots, width):
        lanes = slice(start * BLK, (start + width) * BLK)
        change = jnp.dot(left_rows, right[:, lanes], preferred_element_type=jnp.float32)
        for i in range(width):
            block = (start + i) * cols + q
            col_takes = takes(block, block + v * info.child_blocks)
            lanes = slice((start + i) * BLK, (start + i + 1) * BLK)
            for (u, j), row_take in row_takes.items():
                n = u * ROWS_AT_ONCE + j
                tile[u, j, 0, :, lanes] = (
                    own[j, 0, 0, :, lanes] * (row_take[0] * col_takes[0])
                    + other[j, :, lanes] * (row_take[1] * col_takes[1])
                    - change[n * BLK : (n + 1) * BLK, i * BLK : (i + 1) * BLK]
                )
    for u in range(2):
        for j in range(ROWS_AT_ONCE):
            front_block = row_block(j) + u * info.child_blocks
            slot = front_block // cols
            here = jnp.logical_and(front_block % cols == q, slot // child_slots == v)

            @pl.when(jnp.logical_and(here, jnp.logical_not(info.is_pivot(meta, front_block))))
            def _():
                at = pl.multiple_of(slot % child_slots * BLK, BLK)
                tile[u, j, 0, :, pl.ds(at, BLK)] += jnp.where(eye_mask(), diag[u, j, 0], 0.0)


def params(grid_size, mib=32):
    return pltpu.CompilerParams(
        dimension_semantics=("arbitrary",) * grid_size, vmem_limit_bytes=mib * 1024 * 1024
    )


def about(micros):
    micros *= PACE
    return pl.CostEstimate(flops=int(micros * 1.15e9), bytes_accessed=int(micros * 3.69e6), transcendentals=0)


def pause_kernel(*refs):
    refs[-1][...] = jnp.ones_like(refs[-1])


def pause(micros, *after):
    ones = pl.pallas_call(
        pause_kernel,
        in_specs=[pl.BlockSpec(memory_space=pl.ANY)] * len(after),
        out_shape=jax.ShapeDtypeStruct((8, BLK), jnp.float32),
        cost_estimate=about(micros),
        name="pause",
    )(*after)
    return ones[0, 0]


def per_device(contrib, front_diag, child_map, pivots):
    rows, cols = lax.axis_size("row"), lax.axis_size("col")
    r, q = lax.axis_index("row"), lax.axis_index("col")
    half = rows // 2
    half_bit = half.bit_length() - 1
    sources = cols // rows
    local_rows, child_width = front_diag.shape[0], contrib.shape[1]
    row_slots = local_rows // BLK
    tile_cols = NF // cols
    child_slots = child_width // BLK
    child_rows = contrib.shape[0] // BLK
    row_half = child_rows // 2
    child_blocks, pivot_count = child_map.shape[1], pivots.shape[0]
    depth = pivot_count * BLK
    width = min(4, child_slots)
    steps, where = spread_plan(rows, cols)
    turns = np.argsort(where, axis=0, kind="stable").astype(np.int32)
    early = set(np.take_along_axis(where, turns[:1], 0).ravel()) - {0}
    order = None
    if len(steps) > 2 * sources:
        order, where = fold_plan(where)
    held_count = int(where.max()) + 1
    info = Meta(child_blocks, pivot_count, sources)
    meta = info.pack(child_map, pivots, r, q, where, turns)
    f32, bf16 = jnp.float32, jnp.bfloat16
    shape = jax.ShapeDtypeStruct

    lower_count = pivot_count * (pivot_count + 1) // 2
    child_spec = lambda p: pl.BlockSpec(
        (1, BLK, child_width), lambda g, m: (info.pivot(m, p) % child_blocks // half, 0, 0)
    )
    diag_spec = lambda p: pl.BlockSpec((1, 1, BLK), lambda g, m: (info.pivot(m, p) // rows, 0, 0))
    child_view = contrib.reshape(child_rows, BLK, child_width)
    panel, pivot_part = pl.pallas_call(
        functools.partial(pick_kernel, info, rows, cols),
        grid_spec=pltpu.PrefetchScalarGridSpec(
            num_scalar_prefetch=1,
            grid=(1,),
            in_specs=[child_spec(p) for p in range(pivot_count)] + [diag_spec(p) for p in range(pivot_count)],
            out_specs=[
                pl.BlockSpec((pivot_count, BLK, child_width), lambda g, m: (0, 0, 0)),
                pl.BlockSpec((lower_count, BLK, BLK), lambda g, m: (0, 0, 0)),
            ],
        ),
        out_shape=[
            shape((pivot_count, BLK, child_width), f32),
            shape((lower_count, BLK, BLK), f32),
        ],
        compiler_params=params(1, 60),
        name="pick",
        cost_estimate=about(5),
    )(meta, *[child_view] * pivot_count, *[front_diag.reshape(row_slots, 1, BLK)] * pivot_count)
    own = panel.reshape(depth, child_width)
    for bit in range(half_bit):
        own = own + swapped(own, "row", bit)
    other = swapped(own, "row", half_bit)

    def folded(held):
        if order is None:
            return held
        mine_order = jnp.asarray(order)[:, r, q]
        merged = [held[0]]
        for n in range(held_count - 1):
            merged.append(sum(jnp.where(mine_order[k] == n, held[k], 0.0) for k in range(1, len(held))))
        return merged

    pivot_blocks = pivot_part
    for bit in range(cols.bit_length() - 1):
        across = swapped(pivot_blocks, "col", bit)
        across_first = across if bit == 0 else across_first
        pivot_blocks = pivot_blocks + across
    pivot_blocks = gated(pivot_blocks, other)
    for bit in range(half_bit, -1, -1):
        pivot_blocks = pivot_blocks + swapped(pivot_blocks, "row", bit)

    both = jnp.concatenate([own, other]) * one_after([across, other, pivot_blocks][BOTH]).astype(f32)
    halves = HALVES if child_slots // ROWS_AT_ONCE % HALVES == 0 and order is None else 1
    held = [[both]]
    for n, (buffer, pairs) in enumerate(steps):
        sent = held[buffer][0]
        if n + 1 not in early:
            sent = jnp.split(sent, halves, axis=1)
        else:
            sent = [sent]
        held.append([lax.ppermute(part, ("row", "col"), pairs) for part in sent])
    meanwhile = [part for n in early for part in held[n]]
    if order is not None:
        held = [[part] for part in folded([parts[0] for parts in held])]

    lower, inverse, inverse_t = pl.pallas_call(
        functools.partial(cholesky_kernel, pivot_count),
        out_shape=[shape((depth, depth), f32)] * 3,
        scratch_shapes=[pltpu.VMEM((BLK, 2 * BLK), f32), pltpu.VMEM((lower_count, BLK, BLK), f32)],
        compiler_params=params(0),
        name="factor_pivots",
        cost_estimate=about(59),
    )(pivot_blocks)

    own_view = contrib.reshape(child_slots, sources, 2, BLK, child_width)
    mine = r // half
    partner_turns = jnp.asarray(turns)[:, r ^ half, q]
    received = []
    for turn in range(sources):
        chunks = (child_slots,)
        if turn > 0 and sum(CHUNKS) == child_slots:
            chunks = CHUNKS
        first = 0
        for chunk in chunks:
            if not received:
                start = one_after([pivot_blocks, other, across, across_first][B0])
            elif len(received) == 1:
                start = one_after(inverse)
            else:
                if len(received) == 1:
                    start = one_after(inverse)
                elif G5 == 0:
                    start = pause(MAGNET, inverse, part).astype(jnp.int32)
                elif G5 == 1:
                    start = one_after(inverse, received[0][2])
                elif G5 == 2:
                    start = pause(MAGNET, received[0][2], part).astype(jnp.int32)
                else:
                    start = pause(MAGNET, inverse, part, *[held[n][0] for n in early]).astype(jnp.int32)
            part = lax.dynamic_slice(
                own_view,
                (first, partner_turns[turn] * start, 1 - mine, 0, 0),
                (chunk, 1, 1, BLK, child_width),
            ).reshape(chunk, BLK, child_width)
            received.append((turn, first, swapped(part, "row", half_bit)))
            first += chunk
    meanwhile.append(received[0][2])

    lanes = width * BLK
    groups = child_slots // width
    whole = lambda *_: (0, 0)
    untouched = pl.BlockSpec(memory_space=pl.ANY)
    col_parts = pl.pallas_call(
        functools.partial(columns_kernel, info, rows, cols, child_slots, width),
        grid_spec=pltpu.PrefetchScalarGridSpec(
            num_scalar_prefetch=1,
            grid=(2, groups),
            in_specs=[
                pl.BlockSpec((depth, lanes), lambda v, g, m: (0, g)),
                pl.BlockSpec((depth, lanes), lambda v, g, m: (0, g)),
                pl.BlockSpec((depth, depth), whole),
            ]
            + [untouched] * len(meanwhile),
            out_specs=pl.BlockSpec((3 * depth, lanes), lambda v, g, m: (0, v * groups + g)),
        ),
        out_shape=shape((3 * depth, tile_cols), bf16),
        compiler_params=params(2),
        name="factor_at_columns",
        cost_estimate=about(10),
    )(meta, own, other, inverse, *meanwhile)

    share = depth // cols
    factor = None
    tile = token = None
    diag_view = front_diag.reshape(2, child_slots, sources, 1, BLK)
    mine_of = lambda m: info.row(m) // half
    square = pl.BlockSpec((depth, depth), whole)
    few = min(2, width)
    counts = [1] + [halves] * (sources - 1)
    row_parts = [[] for _ in counts]

    order_of_work = [("rows", 0, 0), ("rows", 1, 0), ("tile", 0)]
    chunks_of = [[] for _ in range(sources)]
    for turn, first, part in received:
        pieces = PIECES if turn == 0 and part.shape[0] % (PIECES * ROWS_AT_ONCE) == 0 else 1
        count = part.shape[0] // pieces
        chunks_of[turn] += [(first + n * count, part, n * count, count) for n in range(pieces)]
    order_of_work = [("rows", 0, 0)] + [("tile", 0, n) for n in range(len(chunks_of[0]))] + [("rows", 1, 0)]
    for turn in range(1, sources):
        ahead = len(chunks_of[turn]) // 2 if counts[turn] == 2 and ORDER else 0
        order_of_work += [("tile", turn, n) for n in range(ahead)]
        order_of_work += [("rows", turn, n) for n in range(counts[turn]) if (turn, n) != (1, 0)]
        order_of_work += [("tile", turn, n) for n in range(ahead, len(chunks_of[turn]))]
    for work, turn, *rest in order_of_work:
        parts_count = counts[turn]
        if work == "rows":
            (at_half,) = rest
            used = sorted({int(n) for n in np.take_along_axis(where, turns[turn : turn + 1], 0).ravel()})
            steps_here = child_slots // few // parts_count
            first = at_half * steps_here

            def piece(n, turn=turn, first=first, at_half=at_half):
                base = first if len(held[n]) == 1 else 0
                return held[n][-1 if base else min(at_half, len(held[n]) - 1)], pl.BlockSpec(
                    (2 * depth, few * BLK),
                    lambda g, m: (0, jnp.where(info.held(m, info.source(m, turn)) == n, base + g, 0)),
                )

            operands = [piece(n)[0] for n in used] + [lower, inverse_t]
            in_specs = [piece(n)[1] for n in used] + [square, square]
            if factor is None:
                factor, aliases = jnp.zeros((2, 1, sources, BLK, BLK), f32), {}
            else:
                aliases = {len(operands) + 1: 0}
            operands += [factor, [meta, received[0][2]][GATE3] if token is None else token]
            in_specs += [untouched] * 2
            factor, row_part = pl.pallas_call(
                functools.partial(rows_kernel, info, rows, cols, few, share, turn, first, used),
                grid_spec=pltpu.PrefetchScalarGridSpec(
                    num_scalar_prefetch=1,
                    grid=(steps_here,),
                    in_specs=in_specs,
                    out_specs=[
                        pl.BlockSpec(
                            (2, few, 1, BLK, BLK),
                            lambda g, m, turn=turn, first=first: (0, first + g, info.source(m, turn), 0, 0),
                        ),
                        pl.BlockSpec((2, few, BLK, 3 * depth), lambda g, m: (0, g, 0, 0)),
                    ],
                    scratch_shapes=[pltpu.VMEM((BLK, depth), f32)],
                ),
                out_shape=[
                    shape((2, child_slots, sources, BLK, BLK), f32),
                    shape((2, child_slots // parts_count, BLK, 3 * depth), bf16),
                ],
                input_output_aliases=aliases,
                compiler_params=params(1, 40),
                name="factor_rows",
                cost_estimate=about(3.0 * steps_here * (LATE if turn else 1.0)),
            )(meta, *operands)
            row_parts[turn].append(row_part)
            continue

        for first, part, offset, count in [chunks_of[turn][rest[0]]]:
            at = first // ROWS_AT_ONCE
            row_part = row_parts[turn][first * parts_count // child_slots]
            left_at = at % (child_slots // parts_count // ROWS_AT_ONCE)
            source_of = functools.partial(info.source, turn=turn)
            in_specs = [
                pl.BlockSpec(
                    (ROWS_AT_ONCE, 1, 1, BLK, child_width),
                    lambda v, t, m, at=at, source_of=source_of: (at + t, source_of(m), mine_of(m), 0, 0),
                ),
                pl.BlockSpec((ROWS_AT_ONCE, BLK, child_width), lambda v, t, m, at=offset // ROWS_AT_ONCE: (at + t, 0, 0)),
                pl.BlockSpec((2, ROWS_AT_ONCE, BLK, 3 * depth), lambda v, t, m, at=left_at: (0, at + t, 0, 0)),
                pl.BlockSpec((3 * depth, child_width), lambda v, t, m: (0, v)),
                pl.BlockSpec(
                    (2, ROWS_AT_ONCE, 1, 1, BLK),
                    lambda v, t, m, at=at, source_of=source_of: (0, at + t, source_of(m), 0, 0),
                ),
            ]
            operands = [own_view, part, row_part, col_parts, diag_view]
            aliases = {}
            if tile is None and G6:
                in_specs.append(untouched)
                operands.append(row_parts[1][0])
            elif tile is not None:
                in_specs.append(untouched)
                operands.append(tile)
                aliases = {len(operands): 0}
            tile, token = pl.pallas_call(
                functools.partial(update_kernel, info, rows, cols, child_slots, width, turn, first),
                grid_spec=pltpu.PrefetchScalarGridSpec(
                    num_scalar_prefetch=1,
                    grid=(2, count // ROWS_AT_ONCE),
                    in_specs=in_specs,
                    out_specs=[
                        pl.BlockSpec(
                            (2, ROWS_AT_ONCE, 1, BLK, child_width),
                            lambda v, t, m, at=at, source_of=source_of: (0, at + t, source_of(m), 0, v),
                        ),
                        pl.BlockSpec((8, BLK), lambda v, t, m: (0, 0)),
                    ],
                ),
                out_shape=[shape((2, child_slots, sources, BLK, tile_cols), f32), shape((8, BLK), f32)],
                input_output_aliases=aliases,
                compiler_params=params(2, 36),
                name="update_tile",
                cost_estimate=about(3.0 * count * (LATE if turn else 1.0)),
            )(meta, *operands)
    factor = factor.reshape(local_rows, BLK)
    if share < BLK:
        factor = lax.dynamic_slice_in_dim(factor, q * share % BLK, share, 1)

    return factor, tile.reshape(local_rows, tile_cols)


def solution(mesh):
    placed = (P(("front", "row"), "col"), P(("front", "row")), P("front", None), P("front"))
    return jax.shard_map(
        per_device,
        mesh=mesh,
        in_specs=placed,
        out_specs=(P(("front", "row"), "col"), P(("front", "row"), "col")),
        check_vma=False,
    )
```

```python
import functools

import jax
import jax.numpy as jnp
import numpy as np
from jax import lax
from jax.experimental import pallas as pl
from jax.experimental.pallas import tpu as pltpu
from jax.sharding import PartitionSpec as P

NF = 8192
BLK = 128
HALVES = 2
ORDER = 1
B0 = 3
GATE3 = 0
MAGNET = 50
G5 = 0
G6 = 0
PIECES = 1
BOTH = 0
CHUNKS = (4, 4)
ROWS_AT_ONCE = 2
PACE = 1.0
LATE = 1.0

highest = lax.Precision.HIGHEST


def swapped(shard, axis, bit):
    return lax.ppermute(shard, axis, [(i, i ^ 1 << bit) for i in range(lax.axis_size(axis))])


def one_after(*arrays):
    first = [array[(0,) * array.ndim] for array in arrays]
    there = functools.reduce(jnp.logical_and, [value == value for value in first])
    return jnp.where(there, 1, 0)


def gated(value, *arrays):
    return value * one_after(*arrays).astype(value.dtype)


def spread_plan(rows, cols):
    sources = cols // rows
    where = -np.ones((sources, rows, cols), np.int32)
    for r in range(rows):
        for s in range(sources):
            where[s, r, r + s * rows] = 0
    steps = []
    while (where < 0).any():
        for buffer in range(len(steps) + 1):
            moves = []
            for r in range(rows):
                sign = 1 if r <= cols - 1 - (r + (sources - 1) * rows) else -1
                taken = set()
                for h in range(cols)[::-sign]:
                    for s in range(sources):
                        if where[s, r, h] != buffer:
                            continue
                        open_to = [
                            d for d in range(cols)
                            if where[s, r, d] < 0 and d not in taken and abs(d - h) <= rows
                        ]
                        if open_to:
                            d = max(open_to, key=lambda d: sign * (d - h))
                            taken.add(d)
                            moves.append((s, r, h, d))
            if moves:
                break
        steps.append((buffer, [(r * cols + h, r * cols + d) for _, r, h, d in moves]))
        for s, r, _, d in moves:
            where[s, r, d] = len(steps)
    return steps, where


def fold_plan(where):
    sources, rows, cols = where.shape
    steps = where.max()
    order = -np.ones((steps + 1, rows, cols), np.int32)
    folded = np.zeros_like(where)
    for r in range(rows):
        for d in range(cols):
            got = sorted((where[s, r, d], s) for s in range(sources) if where[s, r, d] > 0)
            for n, (step, s) in enumerate(got):
                order[step, r, d] = n
                folded[s, r, d] = n + 1
    return order, folded


class Meta:
    def __init__(self, child_blocks, pivot_count, sources):
        self.child_blocks, self.pivot_count, self.sources = child_blocks, pivot_count, sources

    def pack(self, child_map, pivots, row_index, col_index, where, turns):
        place = jnp.stack([row_index, col_index]).astype(jnp.int32)
        held = jnp.asarray(np.concatenate([where, turns]))[:, row_index, col_index]
        return jnp.concatenate([child_map.reshape(-1), pivots, place, held])

    def has(self, meta, child, block, front_block):
        return meta[child * self.child_blocks + block] == front_block

    def pivot(self, meta, p):
        return meta[2 * self.child_blocks + p]

    def row(self, meta):
        return meta[2 * self.child_blocks + self.pivot_count]

    def col(self, meta):
        return meta[2 * self.child_blocks + self.pivot_count + 1]

    def held(self, meta, s):
        return meta[2 * self.child_blocks + self.pivot_count + 2 + s]

    def source(self, meta, turn):
        return self.held(meta, self.sources + turn)

    def is_pivot(self, meta, front_block):
        hit = front_block == self.pivot(meta, 0)
        for p in range(1, self.pivot_count):
            hit = jnp.logical_or(hit, front_block == self.pivot(meta, p))
        return hit


def as_float(flag):
    return jnp.where(flag, 1.0, 0.0).astype(jnp.float32)


def eye_mask():
    return lax.broadcasted_iota(jnp.int32, (BLK, BLK), 0) == lax.broadcasted_iota(jnp.int32, (BLK, BLK), 1)


def split(value):
    high = value.astype(jnp.bfloat16)
    return high, (value - high.astype(jnp.float32)).astype(jnp.bfloat16)


def dot_t(a, b):
    return lax.dot_general(
        a, b, (((1,), (1,)), ((), ())), precision=highest, preferred_element_type=jnp.float32
    )


def dot(a, b):
    return jnp.dot(a, b, precision=highest, preferred_element_type=jnp.float32)


def pick_kernel(info, rows, cols, meta, *refs):
    count = info.pivot_count
    children, diags = refs[:count], refs[count : 2 * count]
    panel, pivot_part = refs[2 * count :]
    half = rows // 2
    r, q = info.row(meta), info.col(meta)
    mine, within = r // half, r % half
    for p in range(count):
        front_block = info.pivot(meta, p)
        block = front_block % info.child_blocks
        present = jnp.logical_and(info.has(meta, mine, block, front_block), block % half == within)
        panel[p] = children[p][0] * as_float(present)
        first = p * (p + 1) // 2
        for t in range(p + 1):
            other = info.pivot(meta, t)
            other_block = other % info.child_blocks
            here = jnp.logical_and(info.has(meta, mine, other_block, other), other_block % cols == q)
            at = pl.multiple_of(other_block // cols * BLK, BLK)
            pivot_part[first + t] = panel[p, :, pl.ds(at, BLK)] * as_float(here)

        @pl.when(jnp.logical_and(front_block % rows == r, front_block % cols == q))
        def _():
            pivot_part[first + p] += jnp.where(eye_mask(), diags[p][0], 0.0)


def cholesky_kernel(count, blocks, lower, inverse, inverse_t, work, rest):
    at = lambda i, j: i * (i + 1) // 2 + j
    span = lambda i: slice(i * BLK, (i + 1) * BLK)
    lower[...] = jnp.zeros_like(lower)
    inverse[...] = jnp.zeros_like(inverse)
    rest[...] = blocks[...]
    row_ids = lax.broadcasted_iota(jnp.int32, (BLK, BLK), 0)
    col_ids = lax.broadcasted_iota(jnp.int32, (BLK, BLK), 1)
    wide_ids = lax.broadcasted_iota(jnp.int32, (1, 2 * BLK), 1)
    column_ids = lax.broadcasted_iota(jnp.int32, (BLK, 1), 0)
    for p in range(count):
        work[:, :BLK] = rest[at(p, p)]
        work[:, BLK:] = jnp.where(row_ids == col_ids, 1.0, 0.0)

        def eliminate(j, carry):
            row = work[pl.ds(j, 1), :]
            lead = jnp.sum(jnp.where(wide_ids == j, row, 0.0), axis=1, keepdims=True)
            left = work[:, :BLK]
            column = jnp.sum(jnp.where(col_ids == j, left, 0.0), axis=1, keepdims=True)
            column = jnp.where(column_ids > j, column, 0.0)
            scaled = row / lead
            work[...] = work[...] - column * scaled
            return carry

        lax.fori_loop(0, BLK, eliminate, 0)
        left = work[:, :BLK]
        lead = jnp.sum(jnp.where(row_ids == col_ids, left, 0.0), axis=1, keepdims=True)
        scale = 1.0 / jnp.sqrt(lead)
        lower[span(p), span(p)] = jnp.where(row_ids <= col_ids, left * scale, 0.0).T
        inverse[span(p), span(p)] = work[:, BLK:] * scale
        own_inverse = inverse[span(p), span(p)]
        for i in range(p + 1, count):
            lower[span(i), span(p)] = dot_t(rest[at(i, p)], own_inverse)
        for i in range(p + 1, count):
            for k in range(p + 1, i + 1):
                rest[at(i, k)] -= dot_t(lower[span(i), span(p)], lower[span(k), span(p)])
    for i in range(1, count):
        for j in range(i):
            known = slice(j * BLK, i * BLK)
            partial = dot(lower[span(i), known], inverse[known, span(j)])
            inverse[span(i), span(j)] = -dot(inverse[span(i), span(i)], partial)
    inverse_t[...] = inverse[...].T


def columns_kernel(info, rows, cols, child_slots, width, meta, own, other, inverse, *refs):
    stacked = refs[-1]
    r, q = info.row(meta), info.col(meta)
    mine = r // (rows // 2)
    v, step = pl.program_id(0), pl.program_id(1)
    parts = []
    for i in range(width):
        block = (step * width + i) * cols + q
        front_block = block + v * info.child_blocks
        keep = jnp.logical_not(info.is_pivot(meta, front_block))
        lanes = slice(i * BLK, (i + 1) * BLK)
        take = as_float(jnp.logical_and(keep, info.has(meta, mine, block, front_block)))
        take_other = as_float(jnp.logical_and(keep, info.has(meta, 1 - mine, block, front_block)))
        parts.append(own[:, lanes] * take + other[:, lanes] * take_other)
    high, low = split(dot(inverse[...], jnp.concatenate(parts, axis=1)))
    depth = high.shape[0]
    stacked[:depth], stacked[depth : 2 * depth], stacked[2 * depth :] = high, high, low


def chosen(holder, used, pieces):
    value = pieces[0][...]
    for n, piece in zip(used[1:], pieces[1:]):
        value = jnp.where(holder == n, piece[...], value)
    return value


def rows_kernel(info, rows, cols, width, share, turn, first, used, meta, *refs):
    r, q = info.row(meta), info.col(meta)
    mine = r // (rows // 2)
    s, step = info.source(meta, turn), pl.program_id(0) + first
    lower, inverse_t = refs[len(used) :][:2]
    factor, parts, work = refs[-3:]
    piece = chosen(info.held(meta, s), used, refs[: len(used)])
    half_depth = piece.shape[0] // 2
    own_value = dot(piece[:half_depth].T, inverse_t[...])
    other_value = dot(piece[half_depth:].T, inverse_t[...])
    at = pl.multiple_of(q * share // BLK * BLK, BLK)
    depth = lower.shape[0]
    for i in range(width):
        block = (step * width + i) * cols + r + s * rows
        span = slice(i * BLK, (i + 1) * BLK)
        for v in range(2):
            front_block = block + v * info.child_blocks
            take = as_float(info.has(meta, mine, block, front_block))
            take_other = as_float(info.has(meta, 1 - mine, block, front_block))
            value = own_value[span, :] * take + other_value[span, :] * take_other
            high, low = split(value)
            parts[v, i, :, :depth], parts[v, i, :, depth : 2 * depth], parts[v, i, :, 2 * depth :] = high, low, high
            work[...] = value
            factor[v, i, 0] = work[:, pl.ds(at, BLK)]
            for p in range(info.pivot_count):

                @pl.when(front_block == info.pivot(meta, p))
                def _():
                    factor[v, i, 0] = lower[p * BLK : (p + 1) * BLK, pl.ds(at, BLK)]
                    parts[v, i] = jnp.zeros_like(parts[v, i])


def update_kernel(info, rows, cols, child_slots, width, turn, first, meta, *refs):
    own, other, left, right, diag = refs[:5]
    tile, token = refs[-2:]
    token[...] = jnp.zeros_like(token)
    r, q = info.row(meta), info.col(meta)
    mine = r // (rows // 2)
    v, step = pl.program_id(0), pl.program_id(1)
    left_rows = left[...].reshape(2 * ROWS_AT_ONCE * BLK, left.shape[-1])

    def takes(block, front_block):
        keep = jnp.logical_not(info.is_pivot(meta, front_block))
        return [as_float(jnp.logical_and(keep, info.has(meta, c, block, front_block))) for c in (mine, 1 - mine)]

    def row_block(j):
        return (first + step * ROWS_AT_ONCE + j) * cols + info.source(meta, turn) * rows + r

    row_takes = {
        (u, j): takes(row_block(j), row_block(j) + u * info.child_blocks)
        for u in range(2)
        for j in range(ROWS_AT_ONCE)
    }
    for start in range(0, child_slots, width):
        lanes = slice(start * BLK, (start + width) * BLK)
        change = jnp.dot(left_rows, right[:, lanes], preferred_element_type=jnp.float32)
        for i in range(width):
            block = (start + i) * cols + q
            col_takes = takes(block, block + v * info.child_blocks)
            lanes = slice((start + i) * BLK, (start + i + 1) * BLK)
            for (u, j), row_take in row_takes.items():
                n = u * ROWS_AT_ONCE + j
                tile[u, j, 0, :, lanes] = (
                    own[j, 0, 0, :, lanes] * (row_take[0] * col_takes[0])
                    + other[j, :, lanes] * (row_take[1] * col_takes[1])
                    - change[n * BLK : (n + 1) * BLK, i * BLK : (i + 1) * BLK]
                )
    for u in range(2):
        for j in range(ROWS_AT_ONCE):
            front_block = row_block(j) + u * info.child_blocks
            slot = front_block // cols
            here = jnp.logical_and(front_block % cols == q, slot // child_slots == v)

            @pl.when(jnp.logical_and(here, jnp.logical_not(info.is_pivot(meta, front_block))))
            def _():
                at = pl.multiple_of(slot % child_slots * BLK, BLK)
                tile[u, j, 0, :, pl.ds(at, BLK)] += jnp.where(eye_mask(), diag[u, j, 0], 0.0)


def params(grid_size, mib=32):
    return pltpu.CompilerParams(
        dimension_semantics=("arbitrary",) * grid_size, vmem_limit_bytes=mib * 1024 * 1024
    )


def about(micros):
    micros *= PACE
    return pl.CostEstimate(flops=int(micros * 1.15e9), bytes_accessed=int(micros * 3.69e6), transcendentals=0)


def pause_kernel(*refs):
    refs[-1][...] = jnp.ones_like(refs[-1])


def pause(micros, *after):
    ones = pl.pallas_call(
        pause_kernel,
        in_specs=[pl.BlockSpec(memory_space=pl.ANY)] * len(after),
        out_shape=jax.ShapeDtypeStruct((8, BLK), jnp.float32),
        cost_estimate=about(micros),
        name="pause",
    )(*after)
    return ones[0, 0]


def per_device(contrib, front_diag, child_map, pivots):
    rows, cols = lax.axis_size("row"), lax.axis_size("col")
    r, q = lax.axis_index("row"), lax.axis_index("col")
    half = rows // 2
    half_bit = half.bit_length() - 1
    sources = cols // rows
    local_rows, child_width = front_diag.shape[0], contrib.shape[1]
    row_slots = local_rows // BLK
    tile_cols = NF // cols
    child_slots = child_width // BLK
    child_rows = contrib.shape[0] // BLK
    row_half = child_rows // 2
    child_blocks, pivot_count = child_map.shape[1], pivots.shape[0]
    depth = pivot_count * BLK
    width = min(4, child_slots)
    steps, where = spread_plan(rows, cols)
    turns = np.argsort(where, axis=0, kind="stable").astype(np.int32)
    early = set(np.take_along_axis(where, turns[:1], 0).ravel()) - {0}
    order = None
    if len(steps) > 2 * sources:
        order, where = fold_plan(where)
    held_count = int(where.max()) + 1
    info = Meta(child_blocks, pivot_count, sources)
    meta = info.pack(child_map, pivots, r, q, where, turns)
    f32, bf16 = jnp.float32, jnp.bfloat16
    shape = jax.ShapeDtypeStruct

    lower_count = pivot_count * (pivot_count + 1) // 2
    child_spec = lambda p: pl.BlockSpec(
        (1, BLK, child_width), lambda g, m: (info.pivot(m, p) % child_blocks // half, 0, 0)
    )
    diag_spec = lambda p: pl.BlockSpec((1, 1, BLK), lambda g, m: (info.pivot(m, p) // rows, 0, 0))
    child_view = contrib.reshape(child_rows, BLK, child_width)
    panel, pivot_part = pl.pallas_call(
        functools.partial(pick_kernel, info, rows, cols),
        grid_spec=pltpu.PrefetchScalarGridSpec(
            num_scalar_prefetch=1,
            grid=(1,),
            in_specs=[child_spec(p) for p in range(pivot_count)] + [diag_spec(p) for p in range(pivot_count)],
            out_specs=[
                pl.BlockSpec((pivot_count, BLK, child_width), lambda g, m: (0, 0, 0)),
                pl.BlockSpec((lower_count, BLK, BLK), lambda g, m: (0, 0, 0)),
            ],
        ),
        out_shape=[
            shape((pivot_count, BLK, child_width), f32),
            shape((lower_count, BLK, BLK), f32),
        ],
        compiler_params=params(1, 60),
        name="pick",
        cost_estimate=about(5),
    )(meta, *[child_view] * pivot_count, *[front_diag.reshape(row_slots, 1, BLK)] * pivot_count)
    own = panel.reshape(depth, child_width)
    for bit in range(half_bit):
        own = own + swapped(own, "row", bit)
    other = swapped(own, "row", half_bit)

    def folded(held):
        if order is None:
            return held
        mine_order = jnp.asarray(order)[:, r, q]
        merged = [held[0]]
        for n in range(held_count - 1):
            merged.append(sum(jnp.where(mine_order[k] == n, held[k], 0.0) for k in range(1, len(held))))
        return merged

    pivot_blocks = pivot_part
    for bit in range(cols.bit_length() - 1):
        across = swapped(pivot_blocks, "col", bit)
        across_first = across if bit == 0 else across_first
        pivot_blocks = pivot_blocks + across
    pivot_blocks = gated(pivot_blocks, other)
    for bit in range(half_bit, -1, -1):
        pivot_blocks = pivot_blocks + swapped(pivot_blocks, "row", bit)

    both = jnp.concatenate([own, other]) * one_after([across, other, pivot_blocks][BOTH]).astype(f32)
    halves = HALVES if child_slots // ROWS_AT_ONCE % HALVES == 0 and order is None else 1
    held = [[both]]
    for n, (buffer, pairs) in enumerate(steps):
        sent = held[buffer][0]
        if n + 1 not in early:
            sent = jnp.split(sent, halves, axis=1)
        else:
            sent = [sent]
        held.append([lax.ppermute(part, ("row", "col"), pairs) for part in sent])
    meanwhile = [part for n in early for part in held[n]]
    if order is not None:
        held = [[part] for part in folded([parts[0] for parts in held])]

    lower, inverse, inverse_t = pl.pallas_call(
        functools.partial(cholesky_kernel, pivot_count),
        out_shape=[shape((depth, depth), f32)] * 3,
        scratch_shapes=[pltpu.VMEM((BLK, 2 * BLK), f32), pltpu.VMEM((lower_count, BLK, BLK), f32)],
        compiler_params=params(0),
        name="factor_pivots",
        cost_estimate=about(59),
    )(pivot_blocks)

    own_view = contrib.reshape(child_slots, sources, 2, BLK, child_width)
    mine = r // half
    partner_turns = jnp.asarray(turns)[:, r ^ half, q]
    received = []
    for turn in range(sources):
        chunks = (child_slots,)
        if turn > 0 and sum(CHUNKS) == child_slots:
            chunks = CHUNKS
        first = 0
        for chunk in chunks:
            if not received:
                start = one_after([pivot_blocks, other, across, across_first][B0])
            elif len(received) == 1:
                start = one_after(inverse)
            else:
                if len(received) == 1:
                    start = one_after(inverse)
                elif G5 == 0:
                    start = pause(MAGNET, inverse, part).astype(jnp.int32)
                elif G5 == 1:
                    start = one_after(inverse, received[0][2])
                elif G5 == 2:
                    start = pause(MAGNET, received[0][2], part).astype(jnp.int32)
                else:
                    start = pause(MAGNET, inverse, part, *[held[n][0] for n in early]).astype(jnp.int32)
            part = lax.dynamic_slice(
                own_view,
                (first, partner_turns[turn] * start, 1 - mine, 0, 0),
                (chunk, 1, 1, BLK, child_width),
            ).reshape(chunk, BLK, child_width)
            received.append((turn, first, swapped(part, "row", half_bit)))
            first += chunk
    meanwhile.append(received[0][2])

    lanes = width * BLK
    groups = child_slots // width
    whole = lambda *_: (0, 0)
    untouched = pl.BlockSpec(memory_space=pl.ANY)
    col_parts = pl.pallas_call(
        functools.partial(columns_kernel, info, rows, cols, child_slots, width),
        grid_spec=pltpu.PrefetchScalarGridSpec(
            num_scalar_prefetch=1,
            grid=(2, groups),
            in_specs=[
                pl.BlockSpec((depth, lanes), lambda v, g, m: (0, g)),
                pl.BlockSpec((depth, lanes), lambda v, g, m: (0, g)),
                pl.BlockSpec((depth, depth), whole),
            ]
            + [untouched] * len(meanwhile),
            out_specs=pl.BlockSpec((3 * depth, lanes), lambda v, g, m: (0, v * groups + g)),
        ),
        out_shape=shape((3 * depth, tile_cols), bf16),
        compiler_params=params(2),
        name="factor_at_columns",
        cost_estimate=about(10),
    )(meta, own, other, inverse, *meanwhile)

    share = depth // cols
    factor = None
    tile = token = None
    diag_view = front_diag.reshape(2, child_slots, sources, 1, BLK)
    mine_of = lambda m: info.row(m) // half
    square = pl.BlockSpec((depth, depth), whole)
    few = width
    counts = [1] + [halves] * (sources - 1)
    row_parts = [[] for _ in counts]

    order_of_work = [("rows", 0, 0), ("rows", 1, 0), ("tile", 0)]
    chunks_of = [[] for _ in range(sources)]
    for turn, first, part in received:
        pieces = PIECES if turn == 0 and part.shape[0] % (PIECES * ROWS_AT_ONCE) == 0 else 1
        count = part.shape[0] // pieces
        chunks_of[turn] += [(first + n * count, part, n * count, count) for n in range(pieces)]
    order_of_work = [("rows", 0, 0)] + [("tile", 0, n) for n in range(len(chunks_of[0]))] + [("rows", 1, 0)]
    for turn in range(1, sources):
        ahead = len(chunks_of[turn]) // 2 if counts[turn] == 2 and ORDER else 0
        order_of_work += [("tile", turn, n) for n in range(ahead)]
        order_of_work += [("rows", turn, n) for n in range(counts[turn]) if (turn, n) != (1, 0)]
        order_of_work += [("tile", turn, n) for n in range(ahead, len(chunks_of[turn]))]
    for work, turn, *rest in order_of_work:
        parts_count = counts[turn]
        if work == "rows":
            (at_half,) = rest
            used = sorted({int(n) for n in np.take_along_axis(where, turns[turn : turn + 1], 0).ravel()})
            steps_here = child_slots // few // parts_count
            first = at_half * steps_here

            def piece(n, turn=turn, first=first, at_half=at_half):
                base = first if len(held[n]) == 1 else 0
                return held[n][-1 if base else min(at_half, len(held[n]) - 1)], pl.BlockSpec(
                    (2 * depth, few * BLK),
                    lambda g, m: (0, jnp.where(info.held(m, info.source(m, turn)) == n, base + g, 0)),
                )

            operands = [piece(n)[0] for n in used] + [lower, inverse_t]
            in_specs = [piece(n)[1] for n in used] + [square, square]
            if factor is None:
                factor, aliases = jnp.zeros((2, 1, sources, BLK, BLK), f32), {}
            else:
                aliases = {len(operands) + 1: 0}
            operands += [factor, [meta, received[0][2]][GATE3] if token is None else token]
            in_specs += [untouched] * 2
            factor, row_part = pl.pallas_call(
                functools.partial(rows_kernel, info, rows, cols, few, share, turn, first, used),
                grid_spec=pltpu.PrefetchScalarGridSpec(
                    num_scalar_prefetch=1,
                    grid=(steps_here,),
                    in_specs=in_specs,
                    out_specs=[
                        pl.BlockSpec(
                            (2, few, 1, BLK, BLK),
                            lambda g, m, turn=turn, first=first: (0, first + g, info.source(m, turn), 0, 0),
                        ),
                        pl.BlockSpec((2, few, BLK, 3 * depth), lambda g, m: (0, g, 0, 0)),
                    ],
                    scratch_shapes=[pltpu.VMEM((BLK, depth), f32)],
                ),
                out_shape=[
                    shape((2, child_slots, sources, BLK, BLK), f32),
                    shape((2, child_slots // parts_count, BLK, 3 * depth), bf16),
                ],
                input_output_aliases=aliases,
                compiler_params=params(1, 40),
                name="factor_rows",
                cost_estimate=about(1.5 * few * steps_here * (LATE if turn else 1.0)),
            )(meta, *operands)
            row_parts[turn].append(row_part)
            continue

        for first, part, offset, count in [chunks_of[turn][rest[0]]]:
            at = first // ROWS_AT_ONCE
            row_part = row_parts[turn][first * parts_count // child_slots]
            left_at = at % (child_slots // parts_count // ROWS_AT_ONCE)
            source_of = functools.partial(info.source, turn=turn)
            in_specs = [
                pl.BlockSpec(
                    (ROWS_AT_ONCE, 1, 1, BLK, child_width),
                    lambda v, t, m, at=at, source_of=source_of: (at + t, source_of(m), mine_of(m), 0, 0),
                ),
                pl.BlockSpec((ROWS_AT_ONCE, BLK, child_width), lambda v, t, m, at=offset // ROWS_AT_ONCE: (at + t, 0, 0)),
                pl.BlockSpec((2, ROWS_AT_ONCE, BLK, 3 * depth), lambda v, t, m, at=left_at: (0, at + t, 0, 0)),
                pl.BlockSpec((3 * depth, child_width), lambda v, t, m: (0, v)),
                pl.BlockSpec(
                    (2, ROWS_AT_ONCE, 1, 1, BLK),
                    lambda v, t, m, at=at, source_of=source_of: (0, at + t, source_of(m), 0, 0),
                ),
            ]
            operands = [own_view, part, row_part, col_parts, diag_view]
            aliases = {}
            if tile is None and G6:
                in_specs.append(untouched)
                operands.append(row_parts[1][0])
            elif tile is not None:
                in_specs.append(untouched)
                operands.append(tile)
                aliases = {len(operands): 0}
            tile, token = pl.pallas_call(
                functools.partial(update_kernel, info, rows, cols, child_slots, width, turn, first),
                grid_spec=pltpu.PrefetchScalarGridSpec(
                    num_scalar_prefetch=1,
                    grid=(2, count // ROWS_AT_ONCE),
                    in_specs=in_specs,
                    out_specs=[
                        pl.BlockSpec(
                            (2, ROWS_AT_ONCE, 1, BLK, child_width),
                            lambda v, t, m, at=at, source_of=source_of: (0, at + t, source_of(m), 0, v),
                        ),
                        pl.BlockSpec((8, BLK), lambda v, t, m: (0, 0)),
                    ],
                ),
                out_shape=[shape((2, child_slots, sources, BLK, tile_cols), f32), shape((8, BLK), f32)],
                input_output_aliases=aliases,
                compiler_params=params(2, 36),
                name="update_tile",
                cost_estimate=about(3.0 * count * (LATE if turn else 1.0)),
            )(meta, *operands)
    factor = factor.reshape(local_rows, BLK)
    if share < BLK:
        factor = lax.dynamic_slice_in_dim(factor, q * share % BLK, share, 1)

    return factor, tile.reshape(local_rows, tile_cols)


def solution(mesh):
    placed = (P(("front", "row"), "col"), P(("front", "row")), P("front", None), P("front"))
    return jax.shard_map(
        per_device,
        mesh=mesh,
        in_specs=placed,
        out_specs=(P(("front", "row"), "col"), P(("front", "row"), "col")),
        check_vma=False,
    )
```
